256 devices in a mesh: table: 32 (over y, z), dp: 8 (over x, core).
Axes of the slice: x: 4, y: 4, z: 8, core: 2. Of those that a mesh axis runs over, the one named last changes fastest.
Arguments:
- dense_input: bfloat16 [32768, 512], P(('table', 'dp')), may hold values from -6 to 6
- bottom_weight: bfloat16 [512, 512], replicated, may hold values from -0.059814453 to 0.059814453
- cold_table: bfloat16 [1048576, 64], P('table'), may hold values from -0.8984375 to 0.8984375
- projection: bfloat16 [256, 512], replicated, may hold values from -0.375 to 0.375
- hot_table: bfloat16 [1024, 512], replicated, may hold values from -0.41992188 to 0.41992188
- cold_owner: int32 [32768, 7, 4, 1], P(('table', 'dp')), may hold values from 0 to 31; in each aligned block of 3584 rows (0 to 3583, 3584 to 7167, ..., all dimensions but the last counted through in order) at most 224 rows name the same one
- cold_local: int32 [32768, 7, 4], P(('table', 'dp')), may hold values from 0 to 32767
- cold_band: int32 [32768, 7, 4], P(('table', 'dp')), may hold values from 0 to 3
- hot_unique: int32 [65536], P(('table', 'dp')), may hold values from 0 to 1023, as said below
- hot_map: int32 [32768, 8, 4], P(('table', 'dp')), may hold values from 0 to 255
- grad_inter: float32 [32768, 256], P(('table', 'dp')), may hold values from -0.3 to 0.3
Outputs:
- interactions: float32 [32768, 256], P(('table', 'dp'))
- cold_grad: float32 [1048576, 64], P(('table', 'dp'))
- hot_grad: float32 [1024, 512], P('table')
- projection_grad: float32 [256, 512], P('table')
- bottom_grad: float32 [512, 512], P('table')
The draws below stay inside these ranges and needn't reach their ends.
Inputs may be any that keep to these rules, and one draw needn't show every extreme that they name: `cold_owner`: among the 3584 cold lookups of one device (aligned blocks of samples in order), no shard is named more than 224 times, a bound that some block reaches. `hot_unique`: the 256 ids in each device's block are distinct. `hot_map`: positions refer to the list of the device that holds the sample.
All inputs are finite; a program needn't handle non-finite values.
Results may differ from the reference program's by a relative error of at most 0.0052.
Values may be sent and summed in bfloat16 or wider, within the bound.
No kernel may reach another device: no remote copies, remote signals or barrier semaphores. Data moves between devices by JAX's collectives and lax.ppermute only.
A program may use at most 128 MiB of HBM per device.

```python
import math
import jax
import jax.numpy as jnp
import numpy as np
from jax import lax

HW = 512
CW = 64
NB = 4
DIN = 512
FC = 7
FH = 8
LOOKS = 4
HOT = 1024
UNIQ = 256
B_DEV = 128
ROWS_DEV = 32768
FEATS = 16
DEV_BLOCKS = 256
SAMPLES = 32768
LOOK_DEV = 3584
CAP = 224
ROWS = 1048576
N_TABLE = 32


def draw_hot_unique(key, part):
    key = jax.random.fold_in(key, 11)
    subkeys = jax.random.split(key, DEV_BLOCKS)
    picks = jax.vmap(lambda single: jax.random.permutation(single, HOT)[:UNIQ])(subkeys)
    return picks.reshape(-1).astype(jnp.int32)


def place_ends(values, key, least, largest):
    longest = values.shape.index(max(values.shape))
    spots = []
    for shift in (0, 1):
        where = [jax.random.randint(jax.random.fold_in(key, axis), (), 0, length) for axis, length in enumerate(values.shape)]
        where[longest] = (where[longest] + shift) % values.shape[longest]
        spots.append(tuple(where))
    return values.at[spots[0]].set(least).at[spots[1]].set(largest)


def steps_of(own_key, shape, cuts, least, top_value):
    def one(dim, shards_of):
        draws = jax.random.uniform(jax.random.fold_in(jax.random.fold_in(own_key, 6), dim), (shards_of,), jnp.float32, least / len(cuts), top_value / len(cuts))
        return jnp.repeat(jnp.exp(draws), shape[dim] // shards_of).reshape((-1,) + (1,) * (len(shape) - dim - 1))

    gain = one(*cuts[0])
    for cut in cuts[1:]:
        gain = gain * one(*cut)
    return gain


def shared_out(rng, own, number, rows, count, top, bound, lean):
    sequence = jax.random.permutation(rng, count)
    crowded, usual = shares(count, rows * top, bound, lean, True), shares(count, rows * top, bound, lean, False)
    places = jnp.arange(count)

    def named(sizes, rotation):
        used = int((sizes > 0).sum())
        fixed = max(1, used // 4)
        moved = fixed + (places - fixed + rotation * (used - fixed)) % max(1, count - fixed)
        return jnp.zeros((count,), jnp.int32).at[sequence[jnp.where(places < fixed, places, moved)]].set(jnp.asarray(sizes, jnp.int32))

    sizes = jnp.where(number % 4 == 0, named(crowded, number // 4), named(usual, number - number // 4 - 1))
    mixed = jax.random.permutation(jax.random.fold_in(own, 3), count)
    donor, sink = mixed[0:count // 2 * 2:2], mixed[1:count // 2 * 2:2]
    room = jnp.minimum(sizes[donor] - 1, bound - sizes[sink]) // 2
    room = jnp.where((donor == sequence[0]) | (sink == sequence[0]) | (sizes[sink] == 0), 0, jnp.maximum(room, 0))
    moved = jax.random.randint(jax.random.fold_in(own, 4), (count // 2,), 0, 1 << 20) % (room + 1)
    sizes = sizes.at[donor].add(-moved).at[sink].add(moved)
    labels = jnp.searchsorted(jnp.cumsum(sizes), jnp.arange(rows * top), side="right").astype(jnp.int32)
    listing = labels.reshape(top, rows).T
    listing = listing[jax.random.permutation(jax.random.fold_in(own, 1), rows)]
    rotation = jax.random.randint(jax.random.fold_in(own, 2), (rows, 1), 0, top)
    return jnp.take_along_axis(listing, (jnp.arange(top)[None, :] + rotation) % top, axis=1)


def shares(amount, total, most, slope, full):
    portions = [(1 << 20) // math.isqrt(standing ** slope) + 1 for standing in range(1, amount + 1)]
    largest = most if full else min(most, max(-(-total // amount), total * portions[0] // sum(portions)))
    least = 1 if total - largest >= amount - 1 else 0
    holding, surplus = [largest] + [least] * (amount - 1), total - largest - least * (amount - 1)
    while surplus > 0:
        movable = [i for i in range(1, amount) if holding[i] < largest] or [i for i in range(1, amount) if holding[i] < most]
        whole, budget = sum([portions[i] for i in movable]), surplus
        for i in movable:
            more = min(most - holding[i], max(1, budget * portions[i] // whole), surplus)
            holding[i] = holding[i] + more
            surplus = surplus - more
    return np.array(holding)


def noise(rng, shape, width, most, cuts=(), kind=jnp.bfloat16):
    level = steps_of(rng, shape, cuts, -0.22, 0.18) if cuts else 1.0
    values = jax.random.normal(rng, shape, jnp.float32) * width * level
    return jnp.minimum(jnp.maximum(values, -most), most).astype(kind)


def setup_inputs(seed: int = 0) -> dict:
    streams_of = jax.random.split(jax.random.key(seed), 12)
    dense_input = noise(streams_of[0], (SAMPLES, DIN), 1.0, 6.0, ((0, 256),))
    bottom_weight = noise(streams_of[1], (DIN, HW), 0.01, 0.059814453)
    cold_table = noise(streams_of[2], (ROWS, CW), 0.15, 0.8984375, ((0, 32),))
    projection = noise(streams_of[3], (NB * CW, HW), (NB * CW) ** -0.5, 0.375)
    hot_table = noise(streams_of[4], (HOT, HW), 0.07, 0.41992188)
    cold_owner_keys = jax.random.split(jax.random.fold_in(streams_of[5], 1), SAMPLES * FC * LOOKS // LOOK_DEV)
    cold_owner_turns = jax.random.permutation(jax.random.fold_in(streams_of[5], 3), SAMPLES * FC * LOOKS // LOOK_DEV)
    cold_owner = jax.vmap(lambda own, number: shared_out(jax.random.fold_in(streams_of[5], 2), own, number, LOOK_DEV, N_TABLE, 1, CAP, 2))(cold_owner_keys, cold_owner_turns).reshape((SAMPLES, FC, LOOKS, 1))
    cold_local = place_ends(jax.random.randint(streams_of[6], (SAMPLES, FC, LOOKS), 0, ROWS_DEV), jax.random.fold_in(streams_of[6], 1), 0, ROWS_DEV - 1).astype(jnp.int32)
    cold_band = place_ends(jax.random.randint(streams_of[7], (SAMPLES, FC, LOOKS), 0, NB), jax.random.fold_in(streams_of[7], 1), 0, NB - 1).astype(jnp.int32)
    hot_unique = draw_hot_unique(jax.random.fold_in(streams_of[11], 71), 0)
    hot_map = place_ends(jax.random.randint(streams_of[9], (SAMPLES, FH, LOOKS), 0, UNIQ), jax.random.fold_in(streams_of[9], 1), 0, UNIQ - 1).astype(jnp.int32)
    grad_inter = noise(streams_of[10], (SAMPLES, FEATS * FEATS), 0.05, 0.3, ((0, 256),), jnp.float32)
    return dict(dense_input=dense_input, bottom_weight=bottom_weight, cold_table=cold_table, projection=projection, hot_table=hot_table, cold_owner=cold_owner, cold_local=cold_local, cold_band=cold_band, hot_unique=hot_unique, hot_map=hot_map, grad_inter=grad_inter)


def silu_slope(pre):
    sigma = jax.nn.sigmoid(pre)
    return sigma * (1.0 + pre * (1.0 - sigma))


def reference(dense_input, bottom_weight, cold_table, projection, hot_table, cold_owner, cold_local, cold_band, hot_unique, hot_map, grad_inter):
    feats = 1 + FC + FH
    highest = lax.Precision.HIGHEST

    def one_block(carry, index):
        cold_acc, hot_acc, proj_acc, bottom_acc = carry
        start = index * B_DEV
        dense_block = lax.dynamic_slice_in_dim(dense_input, start, B_DEV, 0)
        owner_block = lax.dynamic_slice_in_dim(cold_owner, start, B_DEV, 0)[..., 0]
        local_block = lax.dynamic_slice_in_dim(cold_local, start, B_DEV, 0)
        band_block = lax.dynamic_slice_in_dim(cold_band, start, B_DEV, 0)
        map_block = lax.dynamic_slice_in_dim(hot_map, start, B_DEV, 0)
        grad_block = lax.dynamic_slice_in_dim(grad_inter, start, B_DEV, 0).reshape(B_DEV, feats, feats)
        unique_block = lax.dynamic_slice_in_dim(hot_unique, (index * UNIQ).astype(jnp.int32), UNIQ, 0)

        pre = jnp.dot(dense_block, bottom_weight, preferred_element_type=jnp.float32)
        bottom = jax.nn.silu(pre).astype(jnp.bfloat16)

        global_ids = (owner_block * ROWS_DEV + local_block).astype(jnp.int32)
        looked = cold_table[global_ids].astype(jnp.float32)
        band_mask = (band_block[..., None] == jnp.arange(NB, dtype=jnp.int32)).astype(jnp.float32)
        pooled = jnp.einsum("bfln,bflc->bfnc", band_mask, looked, precision=highest).astype(jnp.bfloat16)
        pooled = pooled.reshape(B_DEV * FC, NB * CW)
        cold_emb = jnp.dot(pooled, projection, preferred_element_type=jnp.float32).astype(jnp.bfloat16)

        unique_rows = hot_table[unique_block]
        counts = jnp.sum((map_block.reshape(B_DEV * FH, LOOKS)[:, :, None] == jnp.arange(UNIQ, dtype=jnp.int32)).astype(jnp.float32), axis=1).astype(jnp.bfloat16)
        hot_emb = jnp.dot(counts, unique_rows, preferred_element_type=jnp.float32).astype(jnp.bfloat16)

        stack = jnp.concatenate([bottom[:, None, :], cold_emb.reshape(B_DEV, FC, HW), hot_emb.reshape(B_DEV, FH, HW)], axis=1)
        stack_wide = stack.astype(jnp.float32)
        inter = jnp.einsum("bfe,bge->bfg", stack_wide, stack_wide, precision=highest)
        sym = grad_block + jnp.swapaxes(grad_block, 1, 2)
        d_stack = jnp.einsum("bfg,bge->bfe", sym, stack_wide, precision=highest).astype(jnp.bfloat16)

        d_pre = (d_stack[:, 0].astype(jnp.float32) * silu_slope(pre)).astype(jnp.bfloat16)
        bottom_acc = bottom_acc + jnp.dot(dense_block.T, d_pre, preferred_element_type=jnp.float32)

        d_cold = d_stack[:, 1:1 + FC].reshape(B_DEV * FC, HW)
        d_pool = jnp.dot(d_cold, projection.T, preferred_element_type=jnp.float32).astype(jnp.bfloat16)
        proj_acc = proj_acc + jnp.dot(pooled.T, d_cold, preferred_element_type=jnp.float32)
        d_rows = jnp.einsum("bfln,bfnc->bflc", band_mask, d_pool.reshape(B_DEV, FC, NB, CW).astype(jnp.float32), precision=highest)
        cold_acc = cold_acc.at[global_ids.reshape(-1)].add(d_rows.reshape(-1, CW))

        d_hot = d_stack[:, 1 + FC:].reshape(B_DEV * FH, HW)
        d_unique = jnp.dot(counts.T, d_hot, preferred_element_type=jnp.float32)
        hot_acc = hot_acc.at[unique_block].add(d_unique)
        return (cold_acc, hot_acc, proj_acc, bottom_acc), inter.reshape(B_DEV, feats * feats)

    start_carry = (jnp.zeros((ROWS, CW), jnp.float32), jnp.zeros((HOT, HW), jnp.float32),
                   jnp.zeros((NB * CW, HW), jnp.float32), jnp.zeros((DIN, HW), jnp.float32))
    blocks = jnp.arange(DEV_BLOCKS, dtype=jnp.int32)
    final, inters = lax.scan(one_block, start_carry, blocks)
    cold_acc, hot_acc, proj_acc, bottom_acc = final
    return inters.reshape(SAMPLES, feats * feats), cold_acc, hot_acc, proj_acc, bottom_acc
```

```python
import jax
import jax.numpy as jnp
from jax import lax
from jax.sharding import PartitionSpec as P


def silu_slope(pre):
    sigma = jax.nn.sigmoid(pre)
    return sigma * (1.0 + pre * (1.0 - sigma))


def spread_sum(parts):
    core = lax.axis_index("dp") % 2
    pairs = parts.reshape((4, 2) + parts.shape[1:])
    kept = lax.dynamic_index_in_dim(pairs, core, 1, keepdims=False)
    given = lax.dynamic_index_in_dim(pairs, 1 - core, 1, keepdims=False)
    taken = lax.ppermute(given.astype(jnp.bfloat16), "dp", [(i, i ^ 1) for i in range(8)])
    both = kept + taken.astype(jnp.float32)
    moved = lax.all_to_all(
        both.astype(jnp.bfloat16),
        "dp",
        split_axis=0,
        concat_axis=0,
        tiled=True,
        axis_index_groups=[[0, 2, 4, 6], [1, 3, 5, 7]],
    )
    return jnp.sum(moved.astype(jnp.float32), axis=0)


def shards(
    dense_input,
    bottom_weight,
    cold_table,
    projection,
    hot_table,
    cold_owner,
    cold_local,
    cold_band,
    hot_unique,
    hot_map,
    grad_inter,
):
    batch_rows = dense_input.shape[0]
    cold_feats = cold_local.shape[1]
    bag_size = cold_local.shape[2]
    hot_feats = hot_map.shape[1]
    tables = lax.axis_size("table")
    rows_dev = cold_table.shape[0]
    cold_width = cold_table.shape[1]
    hidden = projection.shape[1]
    band_count = projection.shape[0] // cold_width
    unique_count = hot_unique.shape[0]
    feats = 1 + cold_feats + hot_feats
    lookups = batch_rows * cold_feats * bag_size
    capacity = 2 * lookups // tables
    highest = lax.Precision.HIGHEST
    owner_ids = cold_owner.reshape(lookups)
    local_rows = cold_local.reshape(lookups)
    owner_hits = (owner_ids[:, None] == jnp.arange(tables, dtype=jnp.int32)[None, :]).astype(
        jnp.int32
    )
    running = jnp.cumsum(owner_hits, axis=0)
    slot_ids = jnp.sum((running - 1) * owner_hits, axis=1)
    position = owner_ids * capacity + slot_ids
    send_ids = (
        jnp.zeros((tables * capacity,), jnp.int32)
        .at[position]
        .set(local_rows)
        .reshape(tables, capacity)
    )
    asked = lax.all_to_all(send_ids, "table", split_axis=0, concat_axis=0, tiled=True)
    fetched = cold_table[asked]
    received = lax.all_to_all(fetched, "table", split_axis=0, concat_axis=0, tiled=True)
    arrived = received.reshape(tables * capacity, cold_width)[position].reshape(
        batch_rows * cold_feats, bag_size, cold_width
    )
    pre = jnp.dot(dense_input, bottom_weight, preferred_element_type=jnp.float32)
    bottom = jax.nn.silu(pre).astype(jnp.bfloat16)
    unique_rows = hot_table[hot_unique]
    counts = jnp.sum(
        (
            hot_map.reshape(batch_rows * hot_feats, bag_size)[:, :, None]
            == jnp.arange(unique_count, dtype=jnp.int32)
        ).astype(jnp.int32),
        axis=1,
    ).astype(jnp.bfloat16)
    hot_emb = jnp.dot(counts, unique_rows, preferred_element_type=jnp.float32).astype(jnp.bfloat16)
    band_mask = (
        cold_band.reshape(batch_rows * cold_feats, bag_size)[..., None]
        == jnp.arange(band_count, dtype=jnp.int32)
    ).astype(jnp.bfloat16)
    pooled = jnp.einsum(
        "qln,qlc->qnc", band_mask, arrived, preferred_element_type=jnp.float32
    ).astype(jnp.bfloat16)
    pooled = pooled.reshape(batch_rows * cold_feats, band_count * cold_width)
    cold_emb = jnp.dot(pooled, projection, preferred_element_type=jnp.float32).astype(jnp.bfloat16)
    stack = jnp.concatenate(
        [
            bottom[:, None, :],
            cold_emb.reshape(batch_rows, cold_feats, hidden),
            hot_emb.reshape(batch_rows, hot_feats, hidden),
        ],
        axis=1,
    )
    inter = jnp.einsum("bfe,bge->bfg", stack, stack, preferred_element_type=jnp.float32)
    grad_block = grad_inter.reshape(batch_rows, feats, feats)
    sym = grad_block + jnp.swapaxes(grad_block, 1, 2)
    d_stack = jnp.einsum("bfg,bge->bfe", sym, stack.astype(jnp.float32), precision=highest).astype(
        jnp.bfloat16
    )
    d_cold = d_stack[:, 1 : 1 + cold_feats].reshape(batch_rows * cold_feats, hidden)
    d_pool = jnp.einsum("qo,ko->qk", d_cold, projection, preferred_element_type=jnp.float32).astype(
        jnp.bfloat16
    )
    d_rows = jnp.einsum(
        "qln,qnc->qlc",
        band_mask,
        d_pool.reshape(batch_rows * cold_feats, band_count, cold_width),
        preferred_element_type=jnp.float32,
    ).astype(jnp.bfloat16)
    grad_slots = (
        jnp.zeros((tables * capacity, cold_width), jnp.bfloat16)
        .at[position]
        .set(d_rows.reshape(lookups, cold_width))
        .reshape(tables, capacity, cold_width)
    )
    returned = lax.all_to_all(grad_slots, "table", split_axis=0, concat_axis=0, tiled=True)
    cold_sum = (
        jnp.zeros((rows_dev, cold_width), jnp.float32)
        .at[asked.reshape(-1)]
        .add(returned.reshape(-1, cold_width).astype(jnp.float32))
    )
    cold_grad = spread_sum(cold_sum.reshape(8, rows_dev // 8, cold_width)).reshape(
        rows_dev // 8, cold_width
    )
    d_pre = (d_stack[:, 0].astype(jnp.float32) * silu_slope(pre)).astype(jnp.bfloat16)
    bottom_part = jnp.einsum("bi,bo->io", dense_input, d_pre, preferred_element_type=jnp.float32)
    proj_part = jnp.einsum("qk,qo->ko", pooled, d_cold, preferred_element_type=jnp.float32)
    d_hot = d_stack[:, 1 + cold_feats :].reshape(batch_rows * hot_feats, hidden)
    d_unique = jnp.einsum("qu,qo->uo", counts, d_hot, preferred_element_type=jnp.float32)
    hot_part = jnp.zeros((hot_table.shape[0], hidden), jnp.float32).at[hot_unique].add(d_unique)
    parts = [
        part.reshape(tables, part.shape[0] // tables, hidden)
        for part in (hot_part, proj_part, bottom_part)
    ]
    sizes = [part.shape[1] for part in parts]
    joined = jnp.concatenate(parts, axis=1)
    share = joined.shape[1] // 8
    split = jnp.swapaxes(joined.reshape(tables, 8, share, hidden), 0, 1)
    mine = spread_sum(split)
    across = lax.all_to_all(
        mine.astype(jnp.bfloat16), "table", split_axis=0, concat_axis=0, tiled=True
    )
    total = jnp.sum(across.astype(jnp.float32), axis=0)
    whole = lax.all_to_all(
        jnp.broadcast_to(total[None], (8,) + total.shape),
        "dp",
        split_axis=0,
        concat_axis=0,
        tiled=True,
    ).reshape(8 * share, hidden)
    hot_grad = whole[: sizes[0]]
    projection_grad = whole[sizes[0] : sizes[0] + sizes[1]]
    bottom_grad = whole[sizes[0] + sizes[1] :]
    return (
        inter.reshape(batch_rows, feats * feats),
        cold_grad,
        hot_grad,
        projection_grad,
        bottom_grad,
    )


def solution(mesh):
    placed = (
        P(("table", "dp"), None),
        P(),
        P("table", None),
        P(),
        P(),
        P(("table", "dp"), None, None, None),
        P(("table", "dp"), None, None),
        P(("table", "dp"), None, None),
        P(("table", "dp")),
        P(("table", "dp"), None, None),
        P(("table", "dp"), None),
    )
    return jax.shard_map(
        shards,
        mesh=mesh,
        in_specs=placed,
        out_specs=(
            P(("table", "dp"), None),
            P(("table", "dp"), None),
            P("table", None),
            P("table", None),
            P("table", None),
        ),
        check_vma=False,
    )
```

```python
import functools

import jax
import jax.numpy as jnp
from jax import lax
from jax.experimental import pallas as pl
from jax.experimental.pallas import tpu as pltpu
from jax.sharding import PartitionSpec as P

F32 = jnp.float32
BF16 = jnp.bfloat16
LANES = 128
NT = (((1,), (1,)), ((), ()))
TN = (((0,), (0,)), ((), ()))
MIB = 1 << 20


def dot(a, b, dims=(((1,), (0,)), ((), ()))):
    return lax.dot_general(a, b, dims, preferred_element_type=F32)


def split_two(v):
    high = v.astype(BF16)
    return high, (v - high.astype(F32)).astype(BF16)


def iota(shape, dim):
    return lax.broadcasted_iota(jnp.int32, shape, dim)


def call(kernel, outs, scratch=(), specs=None, vmem=16, us=1, grid=None, out_specs=None):
    args = {} if specs is None else {"in_specs": specs}
    if grid is not None:
        args["grid"] = grid
    if out_specs is not None:
        args["out_specs"] = out_specs
    return pl.pallas_call(
        kernel,
        out_shape=outs,
        scratch_shapes=list(scratch),
        compiler_params=pltpu.CompilerParams(vmem_limit_bytes=vmem * MIB),
        cost_estimate=pl.CostEstimate(
            flops=us * 1_100_000_000, bytes_accessed=MIB, transcendentals=0
        ),
        **args,
    )


SMEM = pl.BlockSpec(memory_space=pltpu.SMEM)
VMEM = pl.BlockSpec(memory_space=pltpu.VMEM)


def prep_kernel(tables, pairs, owner_ref, local_ref, ids_ref, pos_ref):
    steps = owner_ref.shape[0]
    row, col = iota((LANES, 2 * LANES), 0), iota((LANES, 2 * LANES), 1)
    tri = jnp.where((row < col) | (col >= LANES), 1.0, 0.0).astype(BF16)
    table_row = iota((tables, LANES), 0)
    slot_row = iota((2 * LANES, LANES), 0)
    hits = [
        jnp.where(owner_ref[j : j + 1, :] == table_row, 1.0, 0.0) for j in range(steps)
    ]
    sums = dot(jnp.concatenate(hits, axis=0).astype(BF16), tri)
    carry = jnp.zeros((tables, LANES), F32)
    left, right = [], []
    for j in range(steps):
        part = sums[j * tables : (j + 1) * tables]
        slot = jnp.sum(hits[j] * (part[:, :LANES] + carry), axis=0, keepdims=True)
        slot = slot.astype(jnp.int32)
        carry = carry + part[:, LANES:]
        upper = jnp.where(slot >= pairs, 1, 0)
        pos_ref[j : j + 1, :] = (
            upper * (tables * pairs - pairs) + owner_ref[j : j + 1, :] * pairs + slot
        )
        local = local_ref[j : j + 1, :]
        code = (((local >> 11) & 1) << 14) | ((local >> 12) << 11) | (local & 2047)
        high, low = (code >> 8).astype(F32), (code & 255).astype(F32)
        left.append(jnp.concatenate([hits[j] * high, hits[j] * low], axis=0).astype(BF16))
        right.append(jnp.where(slot + upper * (LANES - pairs) == slot_row, 1.0, 0.0).astype(BF16))
    placed = dot(jnp.concatenate(left, axis=1), jnp.concatenate(right, axis=1), NT)
    ids_ref[...] = (placed[:tables] * 256.0 + placed[tables:]).astype(jnp.int32)


def pack_kernel(table_ref, packed_ref):
    half = table_ref.shape[1] // 2
    both = jnp.concatenate([table_ref[:, :half], table_ref[:, half:]], axis=0)
    packed_ref[...] = both.astype(F32).T


def lane_is_low(shape):
    return iota(shape, len(shape) - 1) < 64


def gather_kernel(ids_ref, vec_ref, packed_ref, out_ref, got_a, got_b):
    tables, pairs, _ = out_ref.shape
    step = pairs // 2

    def one(part, source):
        first = source * (2 * LANES) + part * step
        base = pl.multiple_of(source * pairs + part * step, 8)
        read_a = [packed_ref[pl.ds(ids_ref[first + u], 1), :] for u in range(step)]
        read_b = [packed_ref[pl.ds(ids_ref[first + LANES + u], 1), :] for u in range(step)]
        for u in range(step):
            got_a[pl.ds(base + u, 1), :] = read_a[u]
            got_b[pl.ds(base + u, 1), :] = read_b[u]
        return source

    def per_source(source, carry):
        lax.fori_loop(0, 2, one, source)
        return carry

    lax.fori_loop(0, tables, per_source, 0)
    upper = (vec_ref[...] >> 14).astype(F32).T
    low = lane_is_low((pairs, LANES))
    for k in range(tables):
        a = got_a[k * pairs : (k + 1) * pairs, :]
        b = got_b[k * pairs : (k + 1) * pairs, :]
        up_a = upper[:pairs, k : k + 1] > 0.5
        up_b = upper[LANES : LANES + pairs, k : k + 1] > 0.5
        a = jnp.where(up_a, pltpu.roll(a, 64, 1), a)
        b = jnp.where(up_b, b, pltpu.roll(b, 64, 1))
        out_ref[k] = jnp.where(low, a, b).astype(BF16)


def front_kernel(
    dense_ref,
    weight_ref,
    hot_ref,
    unique_ref,
    map_ref,
    grad_ref,
    pre_ref,
    bottom_ref,
    emb_ref,
    counts_ref,
    high_ref,
    low_ref,
):
    batch = dense_ref.shape[0]
    hot_feats, bag = map_ref.shape[0], map_ref.shape[1]
    unique = unique_ref.shape[0]
    feats = high_ref.shape[0]
    pre = dot(dense_ref[...], weight_ref[...])
    pre_ref[...] = pre
    bottom_ref[...] = jax.nn.silu(pre).astype(BF16)
    picks = jnp.where(unique_ref[...] == iota((unique, hot_ref.shape[0]), 1), 1.0, 0.0)
    rows = dot(picks.astype(BF16), hot_ref[...]).astype(BF16)
    place = iota((unique, batch), 0)
    for h in range(hot_feats):
        count = jnp.zeros((unique, batch), F32)
        for l in range(bag):
            count += jnp.where(map_ref[h, l : l + 1, :] == place, 1.0, 0.0)
        counts_ref[:, h * batch : (h + 1) * batch] = count.astype(BF16)
        emb_ref[h] = dot(count.T.astype(BF16), rows).astype(BF16)
    grad = grad_ref[...]
    grad_high, grad_low = split_two(grad)
    square = feats * feats
    at = iota((square, square), 0)
    other = iota((square, square), 1) // feats
    same = iota((batch, square), 0) % feats == iota((batch, square), 1) % feats
    for f in range(feats):
        pick = jnp.where(at == f * feats + other, 1.0, 0.0) + jnp.where(
            at == other * feats + f, 1.0, 0.0
        )
        pick = pick.astype(BF16)
        spread = jnp.where(same, dot(grad_high, pick) + dot(grad_low, pick), 0.0)
        high_ref[f], low_ref[f] = split_two(spread)


def main_kernel(
    pos_ref,
    rows_ref,
    band_ref,
    proj_ref,
    bottom_ref,
    hot_ref,
    high_ref,
    low_ref,
    slots_ref,
    d_ref,
    cold_ref,
    pooled_ref,
    wide,
    lookups,
    stack,
):
    tables, pairs, _ = rows_ref.shape
    feats, batch, hidden = stack.shape
    cold_feats = cold_ref.shape[0]
    bag = band_ref.shape[0] // cold_feats
    half = tables * pairs
    low = lane_is_low((pairs, LANES))
    for k in range(tables):
        x = rows_ref[k].astype(F32)
        r = pltpu.roll(x, 64, 1)
        wide[k * pairs : (k + 1) * pairs, :] = jnp.where(low, x, r)
        wide[half + k * pairs : half + (k + 1) * pairs, :] = jnp.where(low, r, x)

    def fetch(i, carry):
        base = pl.multiple_of(i * 16, 16)
        got = [wide[pl.ds(pos_ref[base + u], 1), :] for u in range(16)]
        for u in range(16):
            lookups[pl.ds(base + u, 1), :] = got[u]
        return carry

    lax.fori_loop(0, lookups.shape[0] // 16, fetch, 0)
    band = band_ref[...].astype(F32).T
    side = jnp.where(lane_is_low((batch, LANES)), 0.0, 1.0)
    stack[0] = bottom_ref[...]
    for h in range(feats - 1 - cold_feats):
        stack[1 + cold_feats + h] = hot_ref[h]
    for f in range(cold_feats):
        first = jnp.zeros((batch, LANES), F32)
        second = jnp.zeros((batch, LANES), F32)
        for l in range(bag):
            j = f * bag + l
            x = lookups[j * batch : (j + 1) * batch, :]
            b = band[:, j : j + 1] - side
            first += jnp.where(b == 0.0, x, 0.0)
            second += jnp.where(b == 2.0, x, 0.0)
        pooled = jnp.concatenate([first, second], axis=1).astype(BF16)
        pooled_ref[f] = pooled
        emb = dot(pooled, proj_ref[...]).astype(BF16)
        cold_ref[f] = emb
        stack[1 + f] = emb
    for g in range(batch // 16):
        at = slice(g * 16, (g + 1) * 16)
        x = stack[:, at, :].reshape(feats * 16, hidden)
        high = high_ref[:, at, :].reshape(feats * 16, feats * 16)
        rest = low_ref[:, at, :].reshape(feats * 16, feats * 16)
        d = (dot(high, x) + dot(rest, x)).astype(BF16)
        d_ref[:, at, :] = d.reshape(feats, 16, hidden)
    low = lane_is_low((batch, LANES))
    for f in range(cold_feats):
        d_pool = dot(d_ref[1 + f], proj_ref[...], NT).astype(BF16).astype(F32)
        first, second = d_pool[:, :LANES], d_pool[:, LANES:]
        first_r, second_r = pltpu.roll(first, 64, 1), pltpu.roll(second, 64, 1)
        each = [
            jnp.where(low, first, first_r),
            jnp.where(low, first_r, first),
            jnp.where(low, second, second_r),
            jnp.where(low, second_r, second),
        ]
        for l in range(bag):
            j = f * bag + l
            b = jnp.broadcast_to(band[:, j : j + 1], (batch, LANES))
            x = jnp.where(b < 0.5, each[0], each[1])
            y = jnp.where(b < 2.5, each[2], each[3])
            lookups[j * batch : (j + 1) * batch, :] = jnp.where(b < 1.5, x, y)
    wide[...] = jnp.zeros(wide.shape, F32)

    def place(i, carry):
        base = pl.multiple_of(i * 16, 16)
        got = [lookups[pl.ds(base + u, 1), :] for u in range(16)]
        for u in range(16):
            wide[pl.ds(pos_ref[base + u], 1), :] = got[u]
        return carry

    lax.fori_loop(0, lookups.shape[0] // 16, place, 0)
    low = lane_is_low((pairs, LANES))
    for k in range(tables):
        a = wide[k * pairs : (k + 1) * pairs, :]
        b = wide[half + k * pairs : half + (k + 1) * pairs, :]
        slots_ref[k] = jnp.where(low, a, b).astype(BF16)


def silu_slope(pre):
    sigma = jax.nn.sigmoid(pre)
    return sigma * (1.0 + pre * (1.0 - sigma))


def back_kernel(
    place_ref,
    d_ref,
    pre_ref,
    dense_ref,
    pooled_ref,
    counts_ref,
    unique_ref,
    kept_ref,
    given_ref,
    parts,
):
    feats, batch, hidden = d_ref.shape
    cold_feats = pooled_ref.shape[0]
    hot_feats = feats - 1 - cold_feats
    tables = parts.shape[2] // 32
    cuts = hidden // LANES
    slope = silu_slope(pre_ref[...])
    d_pre = (d_ref[0].astype(F32) * slope).astype(BF16)
    bottom = dot(dense_ref[...], d_pre, TN)
    d_cold = d_ref[1 : 1 + cold_feats].reshape(cold_feats * batch, hidden)
    pooled = pooled_ref[...].reshape(cold_feats * batch, pooled_ref.shape[2])
    proj = dot(pooled, d_cold, TN)
    d_hot = d_ref[1 + cold_feats :].reshape(hot_feats * batch, hidden)
    high, rest = split_two(dot(counts_ref[...], d_hot))
    hot_rows = tables * 32
    picks = jnp.where(
        iota((hot_rows, unique_ref.shape[1]), 0) == unique_ref[...], 1.0, 0.0
    ).astype(BF16)
    hot = dot(picks, high) + dot(picks, rest)
    for c in range(cuts):
        at = slice(c * LANES, (c + 1) * LANES)
        parts[0, c] = hot[:, at]
        parts[1, c] = jnp.concatenate(
            [
                bottom[:, at].reshape(tables, 16, LANES),
                proj[:, at].reshape(tables, 8, LANES),
                jnp.zeros((tables, 8, LANES), F32),
            ],
            axis=1,
        ).reshape(hot_rows, LANES)
    core = place_ref[1]
    for k in range(cuts):
        chunk = (place_ref[0] + k) % cuts
        kept_ref[k] = parts[core, chunk]
        given_ref[k] = parts[1 - core, chunk].astype(BF16)


def inter_kernel(bottom_ref, cold_ref, hot_ref, inter_ref, stack, grams):
    feats, batch, hidden = stack.shape
    cold_feats = cold_ref.shape[0]
    stack[0] = bottom_ref[...]
    for f in range(cold_feats):
        stack[1 + f] = cold_ref[f]
    for h in range(hot_ref.shape[0]):
        stack[1 + cold_feats + h] = hot_ref[h]
    square = feats * feats
    same = iota((square, square), 0) % feats == iota((square, square), 1) % feats
    for g in range(batch // 16):
        at = slice(g * 16, (g + 1) * 16)
        x = stack[:, at, :].reshape(feats * 16, hidden)
        grams[:, at, :] = jnp.where(same, dot(x, x, NT), 0.0).reshape(feats, 16, square)
    total = jnp.zeros((batch, square), F32)
    other = iota((square, square), 0) // feats
    to = iota((square, square), 1)
    for f in range(feats):
        pick = jnp.where(to == f * feats + other, 1.0, 0.0).astype(BF16)
        high, rest = split_two(grams[f])
        total += dot(high, pick) + dot(rest, pick)
    inter_ref[...] = total


def add_kernel(
    place_ref,
    ids_ref,
    vec_ref,
    rows_ref,
    kept_ref,
    given_ref,
    kept_own_ref,
    given_own_ref,
    val_a,
    val_b,
    *sums,
):
    tables, pairs, _ = rows_ref.shape
    for part in sums:
        part[...] = jnp.zeros(part.shape, F32)
    upper = (vec_ref[...] >> 14).astype(F32).T
    low = lane_is_low((pairs, LANES))
    side = jnp.where(low, 0.0, 1.0)
    for k in range(tables):
        x = rows_ref[k].astype(F32)
        r = pltpu.roll(x, 64, 1)
        at = slice(k * pairs, (k + 1) * pairs)
        up_a, up_b = upper[:pairs, k : k + 1], upper[LANES : LANES + pairs, k : k + 1]
        val_a[at, :] = jnp.where(up_a == side, jnp.where(low, x, r), 0.0)
        val_b[at, :] = jnp.where(up_b == side, jnp.where(low, r, x), 0.0)
    half = tables // 2

    def one(group, source):
        first = source * (2 * LANES) + group * 8
        base = pl.multiple_of(source * pairs + group * 8, 8)
        for u in range(8):
            spots = [
                ids_ref[first + half * which * 2 * LANES + side * LANES + u]
                for which in range(2)
                for side in range(2)
            ]
            new = [
                sums[2 * which + side][pl.ds(spots[2 * which + side], 1), :]
                + val[pl.ds(base + half * which * pairs + u, 1), :]
                for which in range(2)
                for side, val in enumerate((val_a, val_b))
            ]
            for part, spot, value in zip(sums, spots, new):
                part[pl.ds(spot, 1), :] = value
        return source

    def per_source(source, carry):
        lax.fori_loop(0, pairs // 8, one, source)
        return carry

    lax.fori_loop(0, half, per_source, 0)
    core = place_ref[1]
    size = kept_own_ref.shape[0]
    half = size // 2
    for k in range(4):
        chunk = 2 * ((place_ref[0] + k) % 4)
        for h in range(2):
            mine = pl.ds(pl.multiple_of((chunk + core) * size + h * half, half), half)
            other = pl.ds(pl.multiple_of((chunk + 1 - core) * size + h * half, half), half)
            keep = functools.reduce(jnp.add, [part[mine, :] for part in sums])
            give = functools.reduce(jnp.add, [part[other, :] for part in sums]).astype(BF16)
            if k == 0:
                kept_own_ref[h * half : (h + 1) * half, :] = keep
                given_own_ref[h * half : (h + 1) * half, :] = give
            else:
                kept_ref[k - 1, h] = keep.astype(BF16)
                given_ref[k - 1, h] = give


def pair_kernel(kept_ref, taken_ref, up_ref, down_ref, next_up_ref, next_down_ref):
    def total(k, h):
        return (kept_ref[k, h].astype(F32) + taken_ref[k, h].astype(F32)).astype(BF16)

    up_ref[0] = total(1, 0)
    up_ref[1] = total(0, 1)
    down_ref[0] = total(1, 1)
    down_ref[1] = total(2, 0)
    next_up_ref[...] = total(0, 0)
    next_down_ref[...] = total(2, 1)


def last_kernel(kept_ref, taken_ref, low_ref, high_ref, far_low_ref, far_high_ref, out_ref):
    half = low_ref.shape[0]
    total = kept_ref[...] + taken_ref[...].astype(F32)
    low = total[:half] + low_ref[...].astype(F32) + far_low_ref[...].astype(F32)
    high = total[half:] + high_ref[...].astype(F32) + far_high_ref[...].astype(F32)
    wide = jnp.concatenate([low, high], axis=0).T
    out_ref[...] = jnp.concatenate([wide[:64], wide[64:]], axis=1)


def to_other_core(x):
    return lax.ppermute(x, "dp", [(i, i ^ 1) for i in range(8)])


def along_x(x, steps):
    return lax.ppermute(x, "dp", [(i, (i + 2 * steps) % 8) for i in range(8)])


def exchange(x, axis):
    return lax.all_to_all(x, axis, split_axis=0, concat_axis=0, tiled=True)


def shards(
    dense_input,
    bottom_weight,
    cold_table,
    projection,
    hot_table,
    cold_owner,
    cold_local,
    cold_band,
    hot_unique,
    hot_map,
    grad_inter,
):
    batch, hidden = dense_input.shape
    cold_feats, bag = cold_local.shape[1], cold_local.shape[2]
    hot_feats = hot_map.shape[1]
    feats = 1 + cold_feats + hot_feats
    tables = lax.axis_size("table")
    rows_dev, width = cold_table.shape
    unique = hot_unique.shape[0]
    lookups = batch * cold_feats * bag
    slots = 2 * lookups // tables
    pairs = slots // 2
    bands = projection.shape[0]
    at_dp = lax.axis_index("dp").astype(jnp.int32)
    place = jnp.stack([at_dp // 2, at_dp % 2])

    def by_sample(v):
        return jnp.transpose(v.reshape(batch, cold_feats, bag), (1, 2, 0)).reshape(
            cold_feats * bag, batch
        )

    shape = jax.ShapeDtypeStruct
    ids, pos = call(
        functools.partial(prep_kernel, tables, pairs),
        (shape((tables, 2 * LANES), jnp.int32), shape((cold_feats * bag, batch), jnp.int32)),
    )(by_sample(cold_owner), by_sample(cold_local))
    pos = pos.reshape(lookups)
    asked = exchange(ids, "table")
    row_ids = (asked & (rows_dev // 2 - 1)).reshape(tables * 2 * LANES)
    packed = call(
        pack_kernel,
        shape((rows_dev // 2, LANES), F32),
        grid=(8,),
        specs=[pl.BlockSpec((width, rows_dev // 8), lambda i: (0, i))],
        out_specs=pl.BlockSpec((rows_dev // 16, LANES), lambda i: (i, 0)),
        us=6,
    )(cold_table.T)
    fetched = call(
        gather_kernel,
        shape((tables, pairs, LANES), BF16),
        scratch=[pltpu.VMEM((tables * pairs, LANES), F32)] * 2,
        specs=[SMEM, VMEM, VMEM],
        us=16,
    )(row_ids, asked, packed)
    received = exchange(fetched, "table")
    pre, bottom, hot_emb, counts, high, low = call(
        front_kernel,
        (
            shape((batch, hidden), F32),
            shape((batch, hidden), BF16),
            shape((hot_feats, batch, hidden), BF16),
            shape((unique, hot_feats * batch), BF16),
            shape((feats, batch, feats * feats), BF16),
            shape((feats, batch, feats * feats), BF16),
        ),
        us=3,
    )(
        dense_input,
        bottom_weight,
        hot_table,
        hot_unique.reshape(unique, 1),
        jnp.transpose(hot_map, (1, 2, 0)),
        grad_inter,
    )
    slot_grads, d_stack, cold_emb, pooled = call(
        main_kernel,
        (
            shape((tables, pairs, LANES), BF16),
            shape((feats, batch, hidden), BF16),
            shape((cold_feats, batch, hidden), BF16),
            shape((cold_feats, batch, bands), BF16),
        ),
        scratch=[
            pltpu.VMEM((2 * tables * pairs, LANES), F32),
            pltpu.VMEM((lookups, LANES), F32),
            pltpu.VMEM((feats, batch, hidden), BF16),
        ],
        specs=[SMEM] + [VMEM] * 7,
        us=14,
        vmem=20,
    )(pos, received, by_sample(cold_band), projection, bottom, hot_emb, high, low)
    returned = exchange(slot_grads, "table")
    cuts = hidden // LANES
    dense_kept, dense_given = call(
        back_kernel,
        (
            shape((cuts, tables * 32, LANES), F32),
            shape((cuts, tables * 32, LANES), BF16),
        ),
        scratch=[pltpu.VMEM((2, cuts, tables * 32, LANES), F32)],
        specs=[SMEM] + [VMEM] * 6,
        us=4,
        vmem=20,
    )(
        place,
        d_stack,
        pre,
        dense_input,
        pooled,
        counts,
        hot_unique.reshape(1, unique),
    )
    dense_pair = dense_kept + to_other_core(dense_given).astype(F32)
    dense_out = dense_pair[1:].astype(BF16)
    dense_row = dense_pair[0]
    for k, steps in enumerate((1, 2, -1)):
        dense_row += along_x(dense_out[k], steps).astype(F32)
    dense_row = dense_row.astype(BF16).reshape(tables, 32, LANES)
    returned, dense_row = lax.optimization_barrier((returned, dense_row))
    dense_all = exchange(dense_row, "table")

    size = rows_dev // 16
    half = size // 2
    kept, given, kept_own, given_own = call(
        add_kernel,
        (
            shape((3, 2, half, LANES), BF16),
            shape((3, 2, half, LANES), BF16),
            shape((size, LANES), F32),
            shape((size, LANES), BF16),
        ),
        scratch=[pltpu.VMEM((tables * pairs, LANES), F32)] * 2
        + [pltpu.VMEM((rows_dev // 2, LANES), F32)] * 4,
        specs=[SMEM, SMEM, VMEM, VMEM],
        us=20,
        vmem=46,
    )(place, row_ids, asked, returned)
    given, given_own, dense_all = lax.optimization_barrier((given, given_own, dense_all))
    taken = to_other_core(given)
    taken_own = to_other_core(given_own)
    up, down, next_up, next_down = call(
        pair_kernel,
        (
            shape((2, half, LANES), BF16),
            shape((2, half, LANES), BF16),
            shape((half, LANES), BF16),
            shape((half, LANES), BF16),
        ),
        us=2,
    )(kept, taken)
    mine = jnp.sum(dense_all.astype(F32), axis=0)
    (up, down, stack_cold) = lax.optimization_barrier((up, down, cold_emb))
    inter = call(
        inter_kernel,
        shape((batch, feats * feats), F32),
        scratch=[
            pltpu.VMEM((feats, batch, hidden), BF16),
            pltpu.VMEM((feats, batch, feats * feats), F32),
        ],
        us=4,
    )(bottom, stack_cold, hot_emb)
    from_below = along_x(up, 1)
    from_above = along_x(down, -1)
    next_up = (next_up.astype(F32) + from_below[0].astype(F32)).astype(BF16)
    next_down = (next_down.astype(F32) + from_above[0].astype(F32)).astype(BF16)
    far_low = along_x(next_up, 1)
    far_high = along_x(next_down, -1)
    cold_grad = call(last_kernel, shape((width, rows_dev // 8), F32), us=2)(
        kept_own, taken_own, from_above[1], from_below[1], far_low, far_high
    ).T
    theirs = to_other_core(mine)
    both = jnp.where(place[1] == 0, jnp.stack([mine, theirs]), jnp.stack([theirs, mine]))
    ring = jnp.stack([both, along_x(both, -1), along_x(both, 2), along_x(both, 1)])
    whole = jnp.concatenate(
        [lax.dynamic_index_in_dim(ring, (c - place[0]) % cuts, 0, False) for c in range(cuts)],
        axis=2,
    )
    return inter, cold_grad, whole[0], whole[1, 16:24], whole[1, :16]


def solution(mesh):
    placed = (
        P(("table", "dp"), None),
        P(),
        P("table", None),
        P(),
        P(),
        P(("table", "dp"), None, None, None),
        P(("table", "dp"), None, None),
        P(("table", "dp"), None, None),
        P(("table", "dp")),
        P(("table", "dp"), None, None),
        P(("table", "dp"), None),
    )
    return jax.shard_map(
        shards,
        mesh=mesh,
        in_specs=placed,
        out_specs=(
            P(("table", "dp"), None),
            P(("table", "dp"), None),
            P("table", None),
            P("table", None),
            P("table", None),
        ),
        check_vma=False,
    )
```

```python
import functools

import jax
import jax.numpy as jnp
from jax import lax
from jax.experimental import pallas as pl
from jax.experimental.pallas import tpu as pltpu
from jax.sharding import PartitionSpec as P

F32 = jnp.float32
BF16 = jnp.bfloat16
LANES = 128
NT = (((1,), (1,)), ((), ()))
TN = (((0,), (0,)), ((), ()))
MIB = 1 << 20


def dot(a, b, dims=(((1,), (0,)), ((), ()))):
    return lax.dot_general(a, b, dims, preferred_element_type=F32)


def split_two(v):
    high = v.astype(BF16)
    return high, (v - high.astype(F32)).astype(BF16)


def iota(shape, dim):
    return lax.broadcasted_iota(jnp.int32, shape, dim)


def call(kernel, outs, scratch=(), specs=None, vmem=16, us=1, grid=None, out_specs=None):
    args = {} if specs is None else {"in_specs": specs}
    if grid is not None:
        args["grid"] = grid
    if out_specs is not None:
        args["out_specs"] = out_specs
    return pl.pallas_call(
        kernel,
        out_shape=outs,
        scratch_shapes=list(scratch),
        compiler_params=pltpu.CompilerParams(vmem_limit_bytes=vmem * MIB),
        cost_estimate=pl.CostEstimate(
            flops=us * 1_100_000_000, bytes_accessed=MIB, transcendentals=0
        ),
        **args,
    )


SMEM = pl.BlockSpec(memory_space=pltpu.SMEM)
VMEM = pl.BlockSpec(memory_space=pltpu.VMEM)
HBM = pl.BlockSpec(memory_space=pltpu.HBM)


def prep_kernel(tables, pairs, owner_ref, local_ref, ids_ref, pos_ref):
    bag = owner_ref.shape[1]
    steps = owner_ref.shape[0] * bag
    owners = [owner_ref[j // bag, j % bag : j % bag + 1, :] for j in range(steps)]
    row, col = iota((LANES, 2 * LANES), 0), iota((LANES, 2 * LANES), 1)
    tri = jnp.where((row < col) | (col >= LANES), 1.0, 0.0).astype(BF16)
    table_row = iota((tables, LANES), 0)
    slot_row = iota((2 * LANES, LANES), 0)
    hits = [
        jnp.where(owner == table_row, 1.0, 0.0) for owner in owners
    ]
    sums = dot(jnp.concatenate(hits, axis=0).astype(BF16), tri)
    carry = jnp.zeros((tables, LANES), F32)
    left, right = [], []
    for j in range(steps):
        part = sums[j * tables : (j + 1) * tables]
        slot = jnp.sum(hits[j] * (part[:, :LANES] + carry), axis=0, keepdims=True)
        slot = slot.astype(jnp.int32)
        carry = carry + part[:, LANES:]
        upper = jnp.where(slot >= pairs, 1, 0)
        pos_ref[j : j + 1, :] = (
            upper * (tables * pairs - pairs) + owners[j] * pairs + slot
        )
        local = local_ref[j // bag, j % bag : j % bag + 1, :]
        code = (((local >> 11) & 1) << 14) | ((local >> 12) << 11) | (local & 2047)
        high, low = (code >> 8).astype(F32), (code & 255).astype(F32)
        left.append(jnp.concatenate([hits[j] * high, hits[j] * low], axis=0).astype(BF16))
        right.append(jnp.where(slot + upper * (LANES - pairs) == slot_row, 1.0, 0.0).astype(BF16))
    placed = dot(jnp.concatenate(left, axis=1), jnp.concatenate(right, axis=1), NT)
    ids = (placed[:tables] * 256.0 + placed[tables:]).astype(jnp.int32)
    for k in range(tables):
        ids_ref[k] = ids[k : k + 1]


def lane_is_low(shape):
    return iota(shape, len(shape) - 1) < 64


def gather_kernel(ids_ref, vec_ref, table_ref, out_ref, packed, got_a, got_b):
    tables, pairs, _ = out_ref.shape
    size = 2048
    for c in range(packed.shape[0] // size):
        first = table_ref[:, 2 * c * size : (2 * c + 1) * size]
        second = table_ref[:, (2 * c + 1) * size : (2 * c + 2) * size]
        both = jnp.concatenate([first, second], axis=0)
        packed[c * size : (c + 1) * size, :] = both.astype(F32).T
    step = pairs // 2

    def one(part, source):
        first = source * (2 * LANES) + part * step
        base = pl.multiple_of(source * pairs + part * step, 8)
        read_a = [packed[pl.ds(ids_ref[first + u], 1), :] for u in range(step)]
        read_b = [packed[pl.ds(ids_ref[first + LANES + u], 1), :] for u in range(step)]
        for u in range(step):
            got_a[pl.ds(base + u, 1), :] = read_a[u]
            got_b[pl.ds(base + u, 1), :] = read_b[u]
        return source

    def per_source(source, carry):
        lax.fori_loop(0, 2, one, source)
        return carry

    lax.fori_loop(0, tables, per_source, 0)
    upper = (vec_ref[...] >> 14).astype(F32).T
    low = lane_is_low((pairs, LANES))
    for k in range(tables):
        a = got_a[k * pairs : (k + 1) * pairs, :]
        b = got_b[k * pairs : (k + 1) * pairs, :]
        up_a = upper[:pairs, k : k + 1] > 0.5
        up_b = upper[LANES : LANES + pairs, k : k + 1] > 0.5
        a = jnp.where(up_a, pltpu.roll(a, 64, 1), a)
        b = jnp.where(up_b, b, pltpu.roll(b, 64, 1))
        out_ref[k] = jnp.where(low, a, b).astype(BF16)


def front_kernel(
    dense_ref,
    weight_ref,
    hot_ref,
    unique_ref,
    map_ref,
    grad_ref,
    pre_ref,
    bottom_ref,
    emb_ref,
    counts_ref,
    high_ref,
    low_ref,
):
    batch = dense_ref.shape[0]
    hot_feats, bag = map_ref.shape[0], map_ref.shape[1]
    unique = unique_ref.shape[0]
    feats = high_ref.shape[0]
    pre = dot(dense_ref[...], weight_ref[...])
    pre_ref[...] = pre
    bottom_ref[...] = jax.nn.silu(pre).astype(BF16)
    picks = jnp.where(unique_ref[...] == iota((unique, hot_ref.shape[0]), 1), 1.0, 0.0)
    rows = dot(picks.astype(BF16), hot_ref[...]).astype(BF16)
    place = iota((unique, batch), 0)
    for h in range(hot_feats):
        count = jnp.zeros((unique, batch), F32)
        for l in range(bag):
            count += jnp.where(map_ref[h, l : l + 1, :] == place, 1.0, 0.0)
        counts_ref[:, h * batch : (h + 1) * batch] = count.astype(BF16)
        emb_ref[h] = dot(count.T.astype(BF16), rows).astype(BF16)
    grad = grad_ref[...]
    grad_high, grad_low = split_two(grad)
    square = feats * feats
    at = iota((square, square), 0)
    other = iota((square, square), 1) // feats
    same = iota((batch, square), 0) % feats == iota((batch, square), 1) % feats
    for f in range(feats):
        pick = jnp.where(at == f * feats + other, 1.0, 0.0) + jnp.where(
            at == other * feats + f, 1.0, 0.0
        )
        pick = pick.astype(BF16)
        spread = jnp.where(same, dot(grad_high, pick) + dot(grad_low, pick), 0.0)
        high_ref[f], low_ref[f] = split_two(spread)


def silu_slope(pre):
    sigma = jax.nn.sigmoid(pre)
    return sigma * (1.0 + pre * (1.0 - sigma))


def main_kernel(
    place_ref,
    pos_ref,
    rows_ref,
    band_ref,
    proj_ref,
    pre_ref,
    dense_ref,
    counts_ref,
    unique_ref,
    bottom_ref,
    hot_ref,
    high_ref,
    low_ref,
    slots_ref,
    cold_ref,
    kept_ref,
    given_ref,
    wide,
    lookups,
    stack,
    high,
    low_part,
    d_stack,
    bags,
    parts,
    kept,
    given,
    sems,
):
    tables, pairs, _ = rows_ref.shape
    feats, batch, hidden = stack.shape
    cold_feats = cold_ref.shape[0]
    bag = band_ref.shape[0] // cold_feats
    half = tables * pairs
    fixed = pl.ds(1 + cold_feats, feats - 1 - cold_feats)
    incoming = [
        pltpu.make_async_copy(bottom_ref, stack.at[0], sems.at[0]),
        pltpu.make_async_copy(hot_ref, stack.at[fixed], sems.at[1]),
        pltpu.make_async_copy(high_ref, high, sems.at[2]),
        pltpu.make_async_copy(low_ref, low_part, sems.at[3]),
    ]
    for copy in incoming:
        copy.start()
    low = lane_is_low((pairs, LANES))
    for k in range(tables):
        x = rows_ref[k].astype(F32)
        r = pltpu.roll(x, 64, 1)
        wide[k * pairs : (k + 1) * pairs, :] = jnp.where(low, x, r)
        wide[half + k * pairs : half + (k + 1) * pairs, :] = jnp.where(low, r, x)

    def fetch(i, carry):
        base = pl.multiple_of(i * 56, 8)
        got = [wide[pl.ds(pos_ref[base + u], 1), :] for u in range(56)]
        for u in range(56):
            lookups[pl.ds(base + u, 1), :] = got[u]
        return carry

    lax.fori_loop(0, lookups.shape[0] // 56, fetch, 0)
    band = band_ref[...].astype(F32).T
    side = jnp.where(lane_is_low((batch, LANES)), 0.0, 1.0)
    for f in range(cold_feats):
        first = jnp.zeros((batch, LANES), F32)
        second = jnp.zeros((batch, LANES), F32)
        for l in range(bag):
            j = f * bag + l
            x = lookups[j * batch : (j + 1) * batch, :]
            b = band[:, j : j + 1] - side
            first += jnp.where(b == 0.0, x, 0.0)
            second += jnp.where(b == 2.0, x, 0.0)
        pooled = jnp.concatenate([first, second], axis=1).astype(BF16)
        bags[f] = pooled
        stack[1 + f] = dot(pooled, proj_ref[...]).astype(BF16)
    outgoing = pltpu.make_async_copy(stack.at[pl.ds(1, cold_feats)], cold_ref, sems.at[4])
    outgoing.start()
    for copy in incoming:
        copy.wait()
    for g in range(batch // 16):
        at = slice(g * 16, (g + 1) * 16)
        x = stack[:, at, :].reshape(feats * 16, hidden)
        first = high[:, at, :].reshape(feats * 16, feats * 16)
        rest = low_part[:, at, :].reshape(feats * 16, feats * 16)
        d = (dot(first, x) + dot(rest, x)).astype(BF16)
        d_stack[:, at, :] = d.reshape(feats, 16, hidden)
    hot_feats = feats - 1 - cold_feats
    cuts = hidden // LANES
    d_pre = (d_stack[0].astype(F32) * silu_slope(pre_ref[...])).astype(BF16)
    bottom = dot(dense_ref[...], d_pre, TN)
    d_cold = d_stack[1 : 1 + cold_feats].reshape(cold_feats * batch, hidden)
    pooled = bags[...].reshape(cold_feats * batch, bags.shape[2])
    proj = dot(pooled, d_cold, TN)
    d_hot = d_stack[1 + cold_feats :].reshape(hot_feats * batch, hidden)
    first, rest = split_two(dot(counts_ref[...], d_hot))
    hot_rows = tables * 32
    picks = jnp.where(
        iota((hot_rows, unique_ref.shape[1]), 0) == unique_ref[...], 1.0, 0.0
    ).astype(BF16)
    hot = dot(picks, first) + dot(picks, rest)
    for c in range(cuts):
        at = slice(c * LANES, (c + 1) * LANES)
        parts[0, c] = hot[:, at]
        parts[1, c] = jnp.concatenate(
            [
                bottom[:, at].reshape(tables, 16, LANES),
                proj[:, at].reshape(tables, 8, LANES),
                jnp.zeros((tables, 8, LANES), F32),
            ],
            axis=1,
        ).reshape(hot_rows, LANES)
    core = place_ref[1]
    for k in range(cuts):
        chunk = (place_ref[0] + k) % cuts
        kept[k] = parts[core, chunk]
        given[k] = parts[1 - core, chunk].astype(BF16)
    dense_copies = [
        pltpu.make_async_copy(given, given_ref, sems.at[5]),
        pltpu.make_async_copy(kept, kept_ref, sems.at[6]),
    ]
    for copy in dense_copies:
        copy.start()
    low = lane_is_low((batch, LANES))
    for f in range(cold_feats):
        d_pool = dot(d_stack[1 + f], proj_ref[...], NT).astype(BF16).astype(F32)
        first, second = d_pool[:, :LANES], d_pool[:, LANES:]
        first_r, second_r = pltpu.roll(first, 64, 1), pltpu.roll(second, 64, 1)
        each = [
            jnp.where(low, first, first_r),
            jnp.where(low, first_r, first),
            jnp.where(low, second, second_r),
            jnp.where(low, second_r, second),
        ]
        for l in range(bag):
            j = f * bag + l
            b = jnp.broadcast_to(band[:, j : j + 1], (batch, LANES))
            x = jnp.where(b < 0.5, each[0], each[1])
            y = jnp.where(b < 2.5, each[2], each[3])
            lookups[j * batch : (j + 1) * batch, :] = jnp.where(b < 1.5, x, y)
            share = wide.shape[0] // (cold_feats * bag)
            wide[j * share : (j + 1) * share, :] = jnp.zeros((share, LANES), F32)

    def place(i, carry):
        base = pl.multiple_of(i * 56, 8)
        got = [lookups[pl.ds(base + u, 1), :] for u in range(56)]
        for u in range(56):
            wide[pl.ds(pos_ref[base + u], 1), :] = got[u]
        return carry

    lax.fori_loop(0, lookups.shape[0] // 56, place, 0)
    low = lane_is_low((pairs, LANES))
    for k in range(tables):
        a = wide[k * pairs : (k + 1) * pairs, :]
        b = wide[half + k * pairs : half + (k + 1) * pairs, :]
        slots_ref[k] = jnp.where(low, a, b).astype(BF16)
    outgoing.wait()
    for copy in dense_copies:
        copy.wait()


def inter_kernel(bottom_ref, cold_ref, hot_ref, inter_ref, stack, grams):
    feats, batch, hidden = stack.shape
    cold_feats = cold_ref.shape[0]
    stack[0] = bottom_ref[...]
    for f in range(cold_feats):
        stack[1 + f] = cold_ref[f]
    for h in range(hot_ref.shape[0]):
        stack[1 + cold_feats + h] = hot_ref[h]
    square = feats * feats
    same = iota((square, square), 0) % feats == iota((square, square), 1) % feats
    for g in range(batch // 16):
        at = slice(g * 16, (g + 1) * 16)
        x = stack[:, at, :].reshape(feats * 16, hidden)
        grams[:, at, :] = jnp.where(same, dot(x, x, NT), 0.0).reshape(feats, 16, square)
    total = jnp.zeros((batch, square), F32)
    other = iota((square, square), 0) // feats
    to = iota((square, square), 1)
    for f in range(feats):
        pick = jnp.where(to == f * feats + other, 1.0, 0.0).astype(BF16)
        high, rest = split_two(grams[f])
        total += dot(high, pick) + dot(rest, pick)
    inter_ref[...] = total


def add_kernel(
    place_ref,
    ids_ref,
    vec_ref,
    rows_ref,
    given_far_ref,
    given_near_ref,
    given_own_ref,
    kept_far_ref,
    kept_near_ref,
    kept_own_ref,
    val_a,
    val_b,
    given,
    kept,
    kept_own,
    sems,
    *sums,
):
    tables, pairs, _ = rows_ref.shape
    upper = (vec_ref[...] >> 14).astype(F32).T
    low = lane_is_low((pairs, LANES))
    side = jnp.where(low, 0.0, 1.0)
    for k in range(tables):
        x = rows_ref[k].astype(F32)
        r = pltpu.roll(x, 64, 1)
        share = sums[0].shape[0] // tables
        for part in sums:
            part[k * share : (k + 1) * share, :] = jnp.zeros((share, LANES), F32)
        at = slice(k * pairs, (k + 1) * pairs)
        up_a, up_b = upper[:pairs, k : k + 1], upper[LANES : LANES + pairs, k : k + 1]
        val_a[at, :] = jnp.where(up_a == side, jnp.where(low, x, r), 0.0)
        val_b[at, :] = jnp.where(up_b == side, jnp.where(low, r, x), 0.0)
    half = tables // 2
    step = pairs // 2

    def one(group, source):
        first = source * (2 * LANES) + group * step
        base = pl.multiple_of(source * pairs + group * step, 8)
        for u in range(step):
            spots = [
                ids_ref[first + half * which * 2 * LANES + side * LANES + u]
                for which in range(2)
                for side in range(2)
            ]
            new = [
                sums[2 * which + side][pl.ds(spots[2 * which + side], 1), :]
                + val[pl.ds(base + half * which * pairs + u, 1), :]
                for which in range(2)
                for side, val in enumerate((val_a, val_b))
            ]
            for part, spot, value in zip(sums, spots, new):
                part[pl.ds(spot, 1), :] = value
        return source

    def per_source(source, carry):
        lax.fori_loop(0, 2, one, source)
        return carry

    lax.fori_loop(0, half, per_source, 0)
    core = place_ref[1]
    half = kept_own.shape[1]
    size = 2 * half

    def total(k, h, of):
        chunk = 2 * ((place_ref[0] + k) % 4) + of
        at = pl.ds(pl.multiple_of(chunk * size + h * half, half), half)
        return functools.reduce(jnp.add, [part[at, :] for part in sums])

    copies = []

    def send(source, target):
        copies.append(pltpu.make_async_copy(source, target, sems.at[len(copies)]))
        copies[-1].start()

    for k, target in enumerate((given_far_ref, given_near_ref, given_near_ref, given_own_ref)):
        for h in range(2):
            given[k, h] = total((2, 1, 3, 0)[k], h, 1 - core).astype(BF16)
        send(given.at[k], target.at[k - 1] if k in (1, 2) else target)
    for k, target in enumerate((kept_far_ref, kept_near_ref, kept_near_ref)):
        for h in range(2):
            kept[k, h] = total((2, 1, 3)[k], h, core).astype(BF16)
        send(kept.at[k], target.at[k - 1] if k else target)
    for h in range(2):
        kept_own[h] = total(0, h, core)
    send(kept_own, kept_own_ref)
    for copy in copies:
        copy.wait()


def sum_rows(rows_ref):
    total = rows_ref[0].astype(F32)
    for k in range(1, rows_ref.shape[0]):
        total += rows_ref[k].astype(F32)
    return total


def dense_kernel(rows_ref, out_ref):
    rows = rows_ref.shape[1]
    out_ref[:rows], out_ref[rows:] = split_two(sum_rows(rows_ref))


def add_pair(kept, taken):
    return (kept.astype(F32) + taken.astype(F32)).astype(BF16)


def far_kernel(place_ref, kept_ref, taken_ref, mine_ref, theirs_ref, up_ref, down_ref):
    half = kept_ref.shape[1]
    rows = mine_ref.shape[0]
    first = place_ref[1] == 0
    mine, theirs = mine_ref[...].astype(F32), theirs_ref[...].astype(F32)
    low = jnp.where(first, mine, theirs).astype(BF16)
    high = jnp.where(first, theirs, mine).astype(BF16)
    for h, out_ref in enumerate((up_ref, down_ref)):
        out_ref[:half] = add_pair(kept_ref[h], taken_ref[h])
        out_ref[half : half + rows] = low
        out_ref[half + rows :] = high


def second_kernel(kept_ref, taken_ref, below_ref, above_ref, up_ref, down_ref):
    half = kept_ref.shape[2]

    def total(k, h, far):
        return (
            kept_ref[k, h].astype(F32) + taken_ref[k, h].astype(F32) + far.astype(F32)
        ).astype(BF16)

    up_ref[:half] = total(0, 0, below_ref[:half])
    up_ref[half : 2 * half] = add_pair(kept_ref[0, 1], taken_ref[0, 1])
    up_ref[2 * half :] = below_ref[half:]
    down_ref[:half] = add_pair(kept_ref[1, 0], taken_ref[1, 0])
    down_ref[half:] = total(1, 1, above_ref[:half])


def own_kernel(kept_ref, taken_ref, out_ref):
    out_ref[...] = kept_ref[...] + taken_ref[...].astype(F32)


def last_kernel(
    place_ref,
    pair_ref,
    below_ref,
    above_ref,
    own_ref,
    next_ref,
    before_ref,
    out_ref,
    hot_ref,
    proj_ref,
    bottom_ref,
):
    half = pair_ref.shape[1]

    def total(h):
        at = slice(h * half, (h + 1) * half)
        return pair_ref[h] + below_ref[at].astype(F32) + above_ref[at].astype(F32)

    wide = jnp.concatenate([total(0), total(1)], axis=0).T
    out_ref[...] = jnp.concatenate([wide[:64], wide[64:]], axis=1)
    tails = (own_ref[half:], next_ref[half:], below_ref[2 * half :], before_ref[half:])
    for k, tail in enumerate(tails):
        chunk = (place_ref[0] + k) % len(tails)
        at = pl.ds(pl.multiple_of(chunk * LANES, LANES), LANES)
        rows = tail.astype(F32)
        hot_ref[:, at] = rows[:32] + rows[32:64]
        rest = rows[64:96] + rows[96:]
        bottom_ref[:, at] = rest[:16]
        proj_ref[:, at] = rest[16:24]


def to_other_core(x):
    return lax.ppermute(x, "dp", [(i, i ^ 1) for i in range(8)])


def along_x(x, steps):
    return lax.ppermute(x, "dp", [(i, (i + 2 * steps) % 8) for i in range(8)])


def exchange(x, axis):
    return lax.all_to_all(x, axis, split_axis=0, concat_axis=0, tiled=True)


def shards(
    dense_input,
    bottom_weight,
    cold_table,
    projection,
    hot_table,
    cold_owner,
    cold_local,
    cold_band,
    hot_unique,
    hot_map,
    grad_inter,
):
    batch, hidden = dense_input.shape
    cold_feats, bag = cold_local.shape[1], cold_local.shape[2]
    hot_feats = hot_map.shape[1]
    feats = 1 + cold_feats + hot_feats
    tables = lax.axis_size("table")
    rows_dev, width = cold_table.shape
    unique = hot_unique.shape[0]
    lookups = batch * cold_feats * bag
    slots = 2 * lookups // tables
    pairs = slots // 2
    bands = projection.shape[0]
    at_dp = lax.axis_index("dp").astype(jnp.int32)
    place = jnp.stack([at_dp // 2, at_dp % 2])

    def by_sample(v):
        return jnp.transpose(v.reshape(batch, cold_feats, bag), (1, 2, 0))

    shape = jax.ShapeDtypeStruct
    ids, pos = call(
        functools.partial(prep_kernel, tables, pairs),
        (shape((tables, 1, 2 * LANES), jnp.int32), shape((cold_feats * bag, batch), jnp.int32)),
    )(by_sample(cold_owner), by_sample(cold_local))
    pos = pos.reshape(lookups)
    asked = exchange(ids, "table").reshape(tables, 2 * LANES)
    row_ids = (asked & (rows_dev // 2 - 1)).reshape(tables * 2 * LANES)
    fetched = call(
        gather_kernel,
        shape((tables, pairs, LANES), BF16),
        scratch=[pltpu.VMEM((rows_dev // 2, LANES), F32)]
        + [pltpu.VMEM((tables * pairs, LANES), F32)] * 2,
        specs=[SMEM, VMEM, VMEM],
        us=12,
        vmem=24,
    )(row_ids, asked, cold_table.T)
    received = exchange(fetched, "table")
    pre, bottom, hot_emb, counts, high, low = call(
        front_kernel,
        (
            shape((batch, hidden), F32),
            shape((batch, hidden), BF16),
            shape((hot_feats, batch, hidden), BF16),
            shape((unique, hot_feats * batch), BF16),
            shape((feats, batch, feats * feats), BF16),
            shape((feats, batch, feats * feats), BF16),
        ),
        us=3,
    )(
        dense_input,
        bottom_weight,
        hot_table,
        hot_unique.reshape(unique, 1),
        jnp.transpose(hot_map, (1, 2, 0)),
        grad_inter,
    )
    cuts = hidden // LANES
    slot_grads, cold_emb, dense_kept, dense_given = call(
        main_kernel,
        (
            shape((tables, pairs, LANES), BF16),
            shape((cold_feats, batch, hidden), BF16),
            shape((cuts, tables * 32, LANES), F32),
            shape((cuts, tables * 32, LANES), BF16),
        ),
        scratch=[
            pltpu.VMEM((2 * tables * pairs, LANES), F32),
            pltpu.VMEM((lookups, LANES), F32),
            pltpu.VMEM((feats, batch, hidden), BF16),
            pltpu.VMEM((feats, batch, feats * feats), BF16),
            pltpu.VMEM((feats, batch, feats * feats), BF16),
            pltpu.VMEM((feats, batch, hidden), BF16),
            pltpu.VMEM((cold_feats, batch, bands), BF16),
            pltpu.VMEM((2, cuts, tables * 32, LANES), F32),
            pltpu.VMEM((cuts, tables * 32, LANES), F32),
            pltpu.VMEM((cuts, tables * 32, LANES), BF16),
            pltpu.SemaphoreType.DMA((7,)),
        ],
        specs=[SMEM] * 2 + [VMEM] * 7 + [HBM] * 4,
        out_specs=[VMEM, HBM, HBM, HBM],
        us=14,
        vmem=62,
    )(
        place,
        pos,
        received,
        by_sample(cold_band).reshape(cold_feats * bag, batch),
        projection,
        pre,
        dense_input,
        counts,
        hot_unique.reshape(1, unique),
        bottom,
        hot_emb,
        high,
        low,
    )
    returned = exchange(slot_grads, "table")
    dense_pair = dense_kept + to_other_core(dense_given).astype(F32)
    dense_out = dense_pair[1:].astype(BF16)
    dense_row = dense_pair[0]
    for k, steps in enumerate((1, 2, -1)):
        dense_row += along_x(dense_out[k], steps).astype(F32)
    dense_row = dense_row.astype(BF16).reshape(tables, 32, LANES)
    returned, dense_row = lax.optimization_barrier((returned, dense_row))
    dense_all = exchange(dense_row, "table")

    half = rows_dev // 32
    given_far, given_near, given_own, kept_far, kept_near, kept_own = call(
        add_kernel,
        (
            shape((2, half, LANES), BF16),
            shape((2, 2, half, LANES), BF16),
            shape((2, half, LANES), BF16),
            shape((2, half, LANES), BF16),
            shape((2, 2, half, LANES), BF16),
            shape((2, half, LANES), F32),
        ),
        scratch=[pltpu.VMEM((tables * pairs, LANES), F32)] * 2
        + [
            pltpu.VMEM((4, 2, half, LANES), BF16),
            pltpu.VMEM((3, 2, half, LANES), BF16),
            pltpu.VMEM((2, half, LANES), F32),
            pltpu.SemaphoreType.DMA((8,)),
        ]
        + [pltpu.VMEM((rows_dev // 2, LANES), F32)] * 4,
        specs=[SMEM, SMEM, VMEM, VMEM],
        out_specs=[HBM] * 6,
        us=20,
        vmem=62,
    )(place, row_ids, asked, returned)
    given_far, given_near, given_own, dense_all = lax.optimization_barrier(
        (given_far, given_near, given_own, dense_all)
    )
    mine = call(dense_kernel, shape((64, LANES), BF16))(dense_all)
    taken_far = to_other_core(given_far)
    theirs = to_other_core(mine)
    taken_near = to_other_core(given_near)
    taken_own = to_other_core(given_own)
    up, down = call(far_kernel, (shape((half + 128, LANES), BF16),) * 2, specs=[SMEM] + [VMEM] * 4)(
        place, kept_far, taken_far, mine, theirs
    )
    from_below = along_x(up, 1)
    from_above = along_x(down, -1)
    up, down, cold_emb = lax.optimization_barrier((up, down, cold_emb))
    inter = call(
        inter_kernel,
        shape((batch, feats * feats), F32),
        scratch=[
            pltpu.VMEM((feats, batch, hidden), BF16),
            pltpu.VMEM((feats, batch, feats * feats), F32),
        ],
        us=4,
    )(bottom, cold_emb, hot_emb)
    from_below, from_above, taken_near, taken_own, inter = lax.optimization_barrier(
        (from_below, from_above, taken_near, taken_own, inter)
    )
    next_up, next_down = call(
        second_kernel,
        (shape((2 * half + 128, LANES), BF16), shape((2 * half, LANES), BF16)),
    )(kept_near, taken_near, from_below, from_above)
    next_up, next_down, kept_own, taken_own = lax.optimization_barrier(
        (next_up, next_down, kept_own, taken_own)
    )
    pair_own = call(own_kernel, shape((2, half, LANES), F32), us=2)(kept_own, taken_own)
    next_below = along_x(next_up, 1)
    next_above = along_x(next_down, -1)
    cold_grad, hot_grad, projection_grad, bottom_grad = call(
        last_kernel,
        (
            shape((width, rows_dev // 8), F32),
            shape((32, hidden), F32),
            shape((8, hidden), F32),
            shape((16, hidden), F32),
        ),
        specs=[SMEM] + [VMEM] * 6,
        us=2,
    )(place, pair_own, next_below, next_above, up, from_above, from_below)
    return inter, cold_grad.T, hot_grad, projection_grad, bottom_grad


def solution(mesh):
    placed = (
        P(("table", "dp"), None),
        P(),
        P("table", None),
        P(),
        P(),
        P(("table", "dp"), None, None, None),
        P(("table", "dp"), None, None),
        P(("table", "dp"), None, None),
        P(("table", "dp")),
        P(("table", "dp"), None, None),
        P(("table", "dp"), None),
    )
    return jax.shard_map(
        shards,
        mesh=mesh,
        in_specs=placed,
        out_specs=(
            P(("table", "dp"), None),
            P(("table", "dp"), None),
            P("table", None),
            P("table", None),
            P("table", None),
        ),
        check_vma=False,
    )
```

```python
import functools

import jax
import jax.numpy as jnp
from jax import lax
from jax.experimental import pallas as pl
from jax.experimental.pallas import tpu as pltpu
from jax.sharding import PartitionSpec as P

F32 = jnp.float32
BF16 = jnp.bfloat16
LANES = 128
NT = (((1,), (1,)), ((), ()))
TN = (((0,), (0,)), ((), ()))
MIB = 1 << 20


def dot(a, b, dims=(((1,), (0,)), ((), ()))):
    return lax.dot_general(a, b, dims, preferred_element_type=F32)


def split_two(v):
    high = v.astype(BF16)
    return high, (v - high.astype(F32)).astype(BF16)


def iota(shape, dim):
    return lax.broadcasted_iota(jnp.int32, shape, dim)


def call(kernel, outs, scratch=(), specs=None, vmem=16, us=1, grid=None, out_specs=None):
    args = {} if specs is None else {"in_specs": specs}
    if grid is not None:
        args["grid"] = grid
    if out_specs is not None:
        args["out_specs"] = out_specs
    return pl.pallas_call(
        kernel,
        out_shape=outs,
        scratch_shapes=list(scratch),
        compiler_params=pltpu.CompilerParams(vmem_limit_bytes=vmem * MIB),
        cost_estimate=pl.CostEstimate(
            flops=us * 1_100_000_000, bytes_accessed=MIB, transcendentals=0
        ),
        **args,
    )


SMEM = pl.BlockSpec(memory_space=pltpu.SMEM)
VMEM = pl.BlockSpec(memory_space=pltpu.VMEM)
HBM = pl.BlockSpec(memory_space=pltpu.HBM)


def prep_kernel(tables, pairs, owner_ref, local_ref, ids_ref, pos_ref):
    bag = owner_ref.shape[1]
    steps = owner_ref.shape[0] * bag
    owners = [owner_ref[j // bag, j % bag : j % bag + 1, :] for j in range(steps)]
    row, col = iota((LANES, 2 * LANES), 0), iota((LANES, 2 * LANES), 1)
    tri = jnp.where((row < col) | (col >= LANES), 1.0, 0.0).astype(BF16)
    table_row = iota((tables, LANES), 0)
    slot_row = iota((2 * LANES, LANES), 0)
    hits = [
        jnp.where(owner == table_row, 1.0, 0.0) for owner in owners
    ]
    sums = dot(jnp.concatenate(hits, axis=0).astype(BF16), tri)
    carry = jnp.zeros((tables, LANES), F32)
    left, right = [], []
    for j in range(steps):
        part = sums[j * tables : (j + 1) * tables]
        slot = jnp.sum(hits[j] * (part[:, :LANES] + carry), axis=0, keepdims=True)
        slot = slot.astype(jnp.int32)
        carry = carry + part[:, LANES:]
        upper = jnp.where(slot >= pairs, 1, 0)
        pos_ref[j : j + 1, :] = (
            upper * (tables * pairs - pairs) + owners[j] * pairs + slot
        )
        local = local_ref[j // bag, j % bag : j % bag + 1, :]
        code = (((local >> 11) & 1) << 14) | ((local >> 12) << 11) | (local & 2047)
        high, low = (code >> 8).astype(F32), (code & 255).astype(F32)
        left.append(
            jnp.concatenate([hits[j] * high, hits[j] * low, hits[j]], axis=0).astype(BF16)
        )
        right.append(jnp.where(slot + upper * (LANES - pairs) == slot_row, 1.0, 0.0).astype(BF16))
    placed = dot(jnp.concatenate(left, axis=1), jnp.concatenate(right, axis=1), NT)
    ids = (placed[:tables] * 256.0 + placed[tables : 2 * tables]).astype(jnp.int32)
    ids = jnp.where(placed[2 * tables :] > 0.5, ids, iota(ids.shape, 0) * 256 + iota(ids.shape, 1))
    lane = iota(ids.shape, 1)
    rows = ids & 16383
    twice = jnp.zeros(ids.shape, F32)
    for d in range(1, 4):
        met = (rows == pltpu.roll(rows, d, 1)) & (lane % 4 >= d) & (lane % LANES < pairs)
        twice = jnp.where(met, 1.0, twice)
    twice = jnp.max(twice, axis=1, keepdims=True).astype(jnp.int32)
    ids = jnp.where(lane == pairs, twice, ids)
    for k in range(tables):
        ids_ref[k] = ids[k : k + 1]


def lane_is_low(shape):
    return iota(shape, len(shape) - 1) < 64


def gather_kernel(ids_ref, vec_ref, table_ref, out_ref, packed, got_a, got_b):
    tables, pairs, _ = out_ref.shape
    size = 2048
    for c in range(packed.shape[0] // size):
        first = table_ref[:, 2 * c * size : (2 * c + 1) * size]
        second = table_ref[:, (2 * c + 1) * size : (2 * c + 2) * size]
        both = jnp.concatenate([first, second], axis=0)
        packed[c * size : (c + 1) * size, :] = both.astype(F32).T
    step = pairs // 2

    def one(part, source):
        first = source * (2 * LANES) + part * step
        base = pl.multiple_of(source * pairs + part * step, 8)
        read_a = [packed[pl.ds(ids_ref[first + u], 1), :] for u in range(step)]
        read_b = [packed[pl.ds(ids_ref[first + LANES + u], 1), :] for u in range(step)]
        for u in range(step):
            got_a[pl.ds(base + u, 1), :] = read_a[u]
            got_b[pl.ds(base + u, 1), :] = read_b[u]
        return source

    def per_source(source, carry):
        lax.fori_loop(0, 2, one, source)
        return carry

    lax.fori_loop(0, tables, per_source, 0)
    upper = (vec_ref[...] >> 14).astype(F32).T
    low = lane_is_low((pairs, LANES))
    for k in range(tables):
        a = got_a[k * pairs : (k + 1) * pairs, :]
        b = got_b[k * pairs : (k + 1) * pairs, :]
        up_a = upper[:pairs, k : k + 1] > 0.5
        up_b = upper[LANES : LANES + pairs, k : k + 1] > 0.5
        a = jnp.where(up_a, pltpu.roll(a, 64, 1), a)
        b = jnp.where(up_b, b, pltpu.roll(b, 64, 1))
        out_ref[k] = jnp.where(low, a, b).astype(BF16)


def front_kernel(
    dense_ref,
    weight_ref,
    hot_ref,
    unique_ref,
    map_ref,
    grad_ref,
    pre_ref,
    bottom_ref,
    emb_ref,
    counts_ref,
    high_ref,
    low_ref,
):
    batch = dense_ref.shape[0]
    hot_feats, bag = map_ref.shape[0], map_ref.shape[1]
    unique = unique_ref.shape[0]
    feats = high_ref.shape[0]
    pre = dot(dense_ref[...], weight_ref[...])
    pre_ref[...] = pre
    bottom_ref[...] = jax.nn.silu(pre).astype(BF16)
    picks = jnp.where(unique_ref[...] == iota((unique, hot_ref.shape[0]), 1), 1.0, 0.0)
    rows = dot(picks.astype(BF16), hot_ref[...]).astype(BF16)
    place = iota((unique, batch), 0)
    for h in range(hot_feats):
        count = jnp.zeros((unique, batch), F32)
        for l in range(bag):
            count += jnp.where(map_ref[h, l : l + 1, :] == place, 1.0, 0.0)
        counts_ref[:, h * batch : (h + 1) * batch] = count.astype(BF16)
        emb_ref[h] = dot(count.T.astype(BF16), rows).astype(BF16)
    grad = grad_ref[...]
    grad_high, grad_low = split_two(grad)
    square = feats * feats
    at = iota((square, square), 0)
    other = iota((square, square), 1) // feats
    same = iota((batch, square), 0) % feats == iota((batch, square), 1) % feats
    for f in range(feats):
        pick = jnp.where(at == f * feats + other, 1.0, 0.0) + jnp.where(
            at == other * feats + f, 1.0, 0.0
        )
        pick = pick.astype(BF16)
        spread = jnp.where(same, dot(grad_high, pick) + dot(grad_low, pick), 0.0)
        high_ref[f], low_ref[f] = split_two(spread)


def silu_slope(pre):
    sigma = jax.nn.sigmoid(pre)
    return sigma * (1.0 + pre * (1.0 - sigma))


def main_kernel(
    place_ref,
    pos_ref,
    rows_ref,
    band_ref,
    proj_ref,
    pre_ref,
    dense_ref,
    counts_ref,
    unique_ref,
    bottom_ref,
    hot_ref,
    high_ref,
    low_ref,
    slots_ref,
    cold_ref,
    kept_ref,
    given_ref,
    wide,
    lookups,
    stack,
    high,
    low_part,
    d_stack,
    bags,
    parts,
    kept,
    given,
    sems,
):
    tables, pairs, _ = rows_ref.shape
    feats, batch, hidden = stack.shape
    cold_feats = cold_ref.shape[0]
    bag = band_ref.shape[0] // cold_feats
    half = tables * pairs
    fixed = pl.ds(1 + cold_feats, feats - 1 - cold_feats)
    incoming = [
        pltpu.make_async_copy(bottom_ref, stack.at[0], sems.at[0]),
        pltpu.make_async_copy(hot_ref, stack.at[fixed], sems.at[1]),
        pltpu.make_async_copy(high_ref, high, sems.at[2]),
        pltpu.make_async_copy(low_ref, low_part, sems.at[3]),
    ]
    for copy in incoming:
        copy.start()
    low = lane_is_low((pairs, LANES))
    for k in range(tables):
        x = rows_ref[k].astype(F32)
        r = pltpu.roll(x, 64, 1)
        wide[k * pairs : (k + 1) * pairs, :] = jnp.where(low, x, r)
        wide[half + k * pairs : half + (k + 1) * pairs, :] = jnp.where(low, r, x)

    def fetch(i, carry):
        base = pl.multiple_of(i * 128, 8)
        got = [wide[pl.ds(pos_ref[base + u], 1), :] for u in range(128)]
        for u in range(128):
            lookups[pl.ds(base + u, 1), :] = got[u]
        return carry

    lax.fori_loop(0, lookups.shape[0] // 128, fetch, 0)
    band = band_ref[...].astype(F32).T
    side = jnp.where(lane_is_low((batch, LANES)), 0.0, 1.0)
    for f in range(cold_feats):
        first = jnp.zeros((batch, LANES), F32)
        second = jnp.zeros((batch, LANES), F32)
        for l in range(bag):
            j = f * bag + l
            x = lookups[j * batch : (j + 1) * batch, :]
            b = band[:, j : j + 1] - side
            first += jnp.where(b == 0.0, x, 0.0)
            second += jnp.where(b == 2.0, x, 0.0)
        pooled = jnp.concatenate([first, second], axis=1).astype(BF16)
        bags[f] = pooled
        stack[1 + f] = dot(pooled, proj_ref[...]).astype(BF16)
    outgoing = pltpu.make_async_copy(stack.at[pl.ds(1, cold_feats)], cold_ref, sems.at[4])
    outgoing.start()
    for copy in incoming:
        copy.wait()
    for g in range(batch // 16):
        at = slice(g * 16, (g + 1) * 16)
        x = stack[:, at, :].reshape(feats * 16, hidden)
        first = high[:, at, :].reshape(feats * 16, feats * 16)
        rest = low_part[:, at, :].reshape(feats * 16, feats * 16)
        d = (dot(first, x) + dot(rest, x)).astype(BF16)
        d_stack[:, at, :] = d.reshape(feats, 16, hidden)
    hot_feats = feats - 1 - cold_feats
    cuts = hidden // LANES
    d_pre = (d_stack[0].astype(F32) * silu_slope(pre_ref[...])).astype(BF16)
    bottom = dot(dense_ref[...], d_pre, TN)
    d_cold = d_stack[1 : 1 + cold_feats].reshape(cold_feats * batch, hidden)
    pooled = bags[...].reshape(cold_feats * batch, bags.shape[2])
    proj = dot(pooled, d_cold, TN)
    d_hot = d_stack[1 + cold_feats :].reshape(hot_feats * batch, hidden)
    first, rest = split_two(dot(counts_ref[...], d_hot))
    hot_rows = tables * 32
    picks = jnp.where(
        iota((hot_rows, unique_ref.shape[1]), 0) == unique_ref[...], 1.0, 0.0
    ).astype(BF16)
    hot = dot(picks, first) + dot(picks, rest)
    for c in range(cuts):
        at = slice(c * LANES, (c + 1) * LANES)
        parts[0, c] = hot[:, at]
        parts[1, c] = jnp.concatenate(
            [
                bottom[:, at].reshape(tables, 16, LANES),
                proj[:, at].reshape(tables, 8, LANES),
                jnp.zeros((tables, 8, LANES), F32),
            ],
            axis=1,
        ).reshape(hot_rows, LANES)
    core = place_ref[1]
    for k in range(cuts):
        chunk = (place_ref[0] + k) % cuts
        kept[k] = parts[core, chunk]
        given[k] = parts[1 - core, chunk].astype(BF16)
    dense_copies = [
        pltpu.make_async_copy(given, given_ref, sems.at[5]),
        pltpu.make_async_copy(kept, kept_ref, sems.at[6]),
    ]
    for copy in dense_copies:
        copy.start()
    low = lane_is_low((batch, LANES))
    for f in range(cold_feats):
        d_pool = dot(d_stack[1 + f], proj_ref[...], NT).astype(BF16).astype(F32)
        first, second = d_pool[:, :LANES], d_pool[:, LANES:]
        first_r, second_r = pltpu.roll(first, 64, 1), pltpu.roll(second, 64, 1)
        each = [
            jnp.where(low, first, first_r),
            jnp.where(low, first_r, first),
            jnp.where(low, second, second_r),
            jnp.where(low, second_r, second),
        ]
        for l in range(bag):
            j = f * bag + l
            b = jnp.broadcast_to(band[:, j : j + 1], (batch, LANES))
            x = jnp.where(b < 0.5, each[0], each[1])
            y = jnp.where(b < 2.5, each[2], each[3])
            lookups[j * batch : (j + 1) * batch, :] = jnp.where(b < 1.5, x, y)
            share = wide.shape[0] // (cold_feats * bag)
            wide[j * share : (j + 1) * share, :] = jnp.zeros((share, LANES), F32)

    def place(i, carry):
        base = pl.multiple_of(i * 128, 8)
        got = [lookups[pl.ds(base + u, 1), :] for u in range(128)]
        for u in range(128):
            wide[pl.ds(pos_ref[base + u], 1), :] = got[u]
        return carry

    lax.fori_loop(0, lookups.shape[0] // 128, place, 0)
    low = lane_is_low((pairs, LANES))
    for k in range(tables):
        a = wide[k * pairs : (k + 1) * pairs, :]
        b = wide[half + k * pairs : half + (k + 1) * pairs, :]
        slots_ref[k] = jnp.where(low, a, b).astype(BF16)
    outgoing.wait()
    for copy in dense_copies:
        copy.wait()


def inter_kernel(bottom_ref, cold_ref, hot_ref, inter_ref, stack, grams):
    feats, batch, hidden = stack.shape
    cold_feats = cold_ref.shape[0]
    stack[0] = bottom_ref[...]
    for f in range(cold_feats):
        stack[1 + f] = cold_ref[f]
    for h in range(hot_ref.shape[0]):
        stack[1 + cold_feats + h] = hot_ref[h]
    square = feats * feats
    same = iota((square, square), 0) % feats == iota((square, square), 1) % feats
    for g in range(batch // 16):
        at = slice(g * 16, (g + 1) * 16)
        x = stack[:, at, :].reshape(feats * 16, hidden)
        grams[:, at, :] = jnp.where(same, dot(x, x, NT), 0.0).reshape(feats, 16, square)
    total = jnp.zeros((batch, square), F32)
    other = iota((square, square), 0) // feats
    to = iota((square, square), 1)
    for f in range(feats):
        pick = jnp.where(to == f * feats + other, 1.0, 0.0).astype(BF16)
        high, rest = split_two(grams[f])
        total += dot(high, pick) + dot(rest, pick)
    inter_ref[...] = total


def add_kernel(
    place_ref,
    ids_ref,
    vec_ref,
    rows_ref,
    given_far_ref,
    given_near_ref,
    given_own_ref,
    kept_far_ref,
    kept_near_ref,
    kept_own_ref,
    val_a,
    val_b,
    given,
    kept,
    kept_own,
    sems,
    *sums,
):
    tables, pairs, _ = rows_ref.shape
    upper = (vec_ref[...] >> 14).astype(F32).T
    low = lane_is_low((pairs, LANES))
    side = jnp.where(low, 0.0, 1.0)
    for k in range(tables):
        x = rows_ref[k].astype(F32)
        r = pltpu.roll(x, 64, 1)
        share = sums[0].shape[0] // tables
        for part in sums:
            part[k * share : (k + 1) * share, :] = jnp.zeros((share, LANES), F32)
        at = slice(k * pairs, (k + 1) * pairs)
        up_a, up_b = upper[:pairs, k : k + 1], upper[LANES : LANES + pairs, k : k + 1]
        val_a[at, :] = jnp.where(up_a == side, jnp.where(low, x, r), 0.0)
        val_b[at, :] = jnp.where(up_b == side, jnp.where(low, r, x), 0.0)
    sides = ((0, val_a, sums[0]), (LANES, val_b, sums[1]))
    step = pairs // 2

    def spread(part, source):
        first = source * (2 * LANES) + part * step
        base = pl.multiple_of(source * pairs + part * step, 8)
        for q in range(0, step, 4):
            work = [
                (to, ids_ref[first + lane + q + t], val[pl.ds(base + q + t, 1), :])
                for lane, val, to in sides
                for t in range(4)
            ]
            new = [to[pl.ds(row, 1), :] + value for to, row, value in work]
            for (to, row, _), value in zip(work, new):
                to[pl.ds(row, 1), :] = value
        return source

    def one_by_one(group, source):
        first = source * (2 * LANES) + group * 8
        base = pl.multiple_of(source * pairs + group * 8, 8)
        for u in range(8):
            for lane, val, to in sides:
                row = ids_ref[first + lane + u]
                to[pl.ds(row, 1), :] = to[pl.ds(row, 1), :] + val[pl.ds(base + u, 1), :]
        return source

    def per_source(source, carry):
        twice = ids_ref[source * (2 * LANES) + pairs]

        @pl.when(twice == 0)
        def _():
            lax.fori_loop(0, 2, spread, source)

        @pl.when(twice != 0)
        def _():
            lax.fori_loop(0, pairs // 8, one_by_one, source)

        return carry

    lax.fori_loop(0, tables, per_source, 0)
    core = place_ref[1]
    half = kept_own.shape[1]
    size = 2 * half

    def total(k, h, of):
        chunk = 2 * ((place_ref[0] + k) % 4) + of
        at = pl.ds(pl.multiple_of(chunk * size + h * half, half), half)
        return functools.reduce(jnp.add, [part[at, :] for part in sums])

    copies = []

    def send(source, target):
        copies.append(pltpu.make_async_copy(source, target, sems.at[len(copies)]))
        copies[-1].start()

    for k, target in enumerate((given_far_ref, given_near_ref, given_near_ref, given_own_ref)):
        for h in range(2):
            given[k, h] = total((2, 1, 3, 0)[k], h, 1 - core).astype(BF16)
        send(given.at[k], target.at[k - 1] if k in (1, 2) else target)
    for k, target in enumerate((kept_far_ref, kept_near_ref, kept_near_ref)):
        for h in range(2):
            kept[k, h] = total((2, 1, 3)[k], h, core).astype(BF16)
        send(kept.at[k], target.at[k - 1] if k else target)
    for h in range(2):
        kept_own[h] = total(0, h, core)
    send(kept_own, kept_own_ref)
    for copy in copies:
        copy.wait()


def sum_rows(rows_ref):
    total = rows_ref[0].astype(F32)
    for k in range(1, rows_ref.shape[0]):
        total += rows_ref[k].astype(F32)
    return total


def dense_kernel(rows_ref, out_ref):
    rows = rows_ref.shape[1]
    out_ref[:rows], out_ref[rows:] = split_two(sum_rows(rows_ref))


def add_pair(kept, taken):
    return (kept.astype(F32) + taken.astype(F32)).astype(BF16)


def far_kernel(place_ref, kept_ref, taken_ref, mine_ref, theirs_ref, up_ref, down_ref):
    half = kept_ref.shape[1]
    rows = mine_ref.shape[0]
    first = place_ref[1] == 0
    mine, theirs = mine_ref[...].astype(F32), theirs_ref[...].astype(F32)
    low = jnp.where(first, mine, theirs).astype(BF16)
    high = jnp.where(first, theirs, mine).astype(BF16)
    for h, out_ref in enumerate((up_ref, down_ref)):
        out_ref[:half] = add_pair(kept_ref[h], taken_ref[h])
        out_ref[half : half + rows] = low
        out_ref[half + rows :] = high


def second_kernel(kept_ref, taken_ref, below_ref, above_ref, up_ref, down_ref):
    half = kept_ref.shape[2]

    def total(k, h, far):
        return (
            kept_ref[k, h].astype(F32) + taken_ref[k, h].astype(F32) + far.astype(F32)
        ).astype(BF16)

    up_ref[:half] = total(0, 0, below_ref[:half])
    up_ref[half : 2 * half] = add_pair(kept_ref[0, 1], taken_ref[0, 1])
    up_ref[2 * half :] = below_ref[half:]
    down_ref[:half] = add_pair(kept_ref[1, 0], taken_ref[1, 0])
    down_ref[half:] = total(1, 1, above_ref[:half])


def own_kernel(kept_ref, taken_ref, out_ref):
    out_ref[...] = kept_ref[...] + taken_ref[...].astype(F32)


def last_kernel(
    place_ref,
    pair_ref,
    below_ref,
    above_ref,
    own_ref,
    next_ref,
    before_ref,
    out_ref,
    hot_ref,
    proj_ref,
    bottom_ref,
):
    half = pair_ref.shape[1]

    def total(h):
        at = slice(h * half, (h + 1) * half)
        return pair_ref[h] + below_ref[at].astype(F32) + above_ref[at].astype(F32)

    wide = jnp.concatenate([total(0), total(1)], axis=0).T
    out_ref[...] = jnp.concatenate([wide[:64], wide[64:]], axis=1)
    tails = (own_ref[half:], next_ref[half:], below_ref[2 * half :], before_ref[half:])
    for k, tail in enumerate(tails):
        chunk = (place_ref[0] + k) % len(tails)
        at = pl.ds(pl.multiple_of(chunk * LANES, LANES), LANES)
        rows = tail.astype(F32)
        hot_ref[:, at] = rows[:32] + rows[32:64]
        rest = rows[64:96] + rows[96:]
        bottom_ref[:, at] = rest[:16]
        proj_ref[:, at] = rest[16:24]


def to_other_core(x):
    return lax.ppermute(x, "dp", [(i, i ^ 1) for i in range(8)])


def along_x(x, steps):
    return lax.ppermute(x, "dp", [(i, (i + 2 * steps) % 8) for i in range(8)])


def exchange(x, axis):
    return lax.all_to_all(x, axis, split_axis=0, concat_axis=0, tiled=True)


def shards(
    dense_input,
    bottom_weight,
    cold_table,
    projection,
    hot_table,
    cold_owner,
    cold_local,
    cold_band,
    hot_unique,
    hot_map,
    grad_inter,
):
    batch, hidden = dense_input.shape
    cold_feats, bag = cold_local.shape[1], cold_local.shape[2]
    hot_feats = hot_map.shape[1]
    feats = 1 + cold_feats + hot_feats
    tables = lax.axis_size("table")
    rows_dev, width = cold_table.shape
    unique = hot_unique.shape[0]
    lookups = batch * cold_feats * bag
    slots = 2 * lookups // tables
    pairs = slots // 2
    bands = projection.shape[0]
    at_dp = lax.axis_index("dp").astype(jnp.int32)
    place = jnp.stack([at_dp // 2, at_dp % 2])

    def by_sample(v):
        return jnp.transpose(v.reshape(batch, cold_feats, bag), (1, 2, 0))

    shape = jax.ShapeDtypeStruct
    ids, pos = call(
        functools.partial(prep_kernel, tables, pairs),
        (shape((tables, 1, 2 * LANES), jnp.int32), shape((cold_feats * bag, batch), jnp.int32)),
    )(by_sample(cold_owner), by_sample(cold_local))
    pos = pos.reshape(lookups)
    asked = exchange(ids, "table").reshape(tables, 2 * LANES)
    row_ids = (asked & (rows_dev // 2 - 1)).reshape(tables * 2 * LANES)
    fetched = call(
        gather_kernel,
        shape((tables, pairs, LANES), BF16),
        scratch=[pltpu.VMEM((rows_dev // 2, LANES), F32)]
        + [pltpu.VMEM((tables * pairs, LANES), F32)] * 2,
        specs=[SMEM, VMEM, VMEM],
        us=12,
        vmem=24,
    )(row_ids, asked, cold_table.T)
    received = exchange(fetched, "table")
    pre, bottom, hot_emb, counts, high, low = call(
        front_kernel,
        (
            shape((batch, hidden), F32),
            shape((batch, hidden), BF16),
            shape((hot_feats, batch, hidden), BF16),
            shape((unique, hot_feats * batch), BF16),
            shape((feats, batch, feats * feats), BF16),
            shape((feats, batch, feats * feats), BF16),
        ),
        us=3,
    )(
        dense_input,
        bottom_weight,
        hot_table,
        hot_unique.reshape(unique, 1),
        jnp.transpose(hot_map, (1, 2, 0)),
        grad_inter,
    )
    cuts = hidden // LANES
    slot_grads, cold_emb, dense_kept, dense_given = call(
        main_kernel,
        (
            shape((tables, pairs, LANES), BF16),
            shape((cold_feats, batch, hidden), BF16),
            shape((cuts, tables * 32, LANES), F32),
            shape((cuts, tables * 32, LANES), BF16),
        ),
        scratch=[
            pltpu.VMEM((2 * tables * pairs, LANES), F32),
            pltpu.VMEM((lookups, LANES), F32),
            pltpu.VMEM((feats, batch, hidden), BF16),
            pltpu.VMEM((feats, batch, feats * feats), BF16),
            pltpu.VMEM((feats, batch, feats * feats), BF16),
            pltpu.VMEM((feats, batch, hidden), BF16),
            pltpu.VMEM((cold_feats, batch, bands), BF16),
            pltpu.VMEM((2, cuts, tables * 32, LANES), F32),
            pltpu.VMEM((cuts, tables * 32, LANES), F32),
            pltpu.VMEM((cuts, tables * 32, LANES), BF16),
            pltpu.SemaphoreType.DMA((7,)),
        ],
        specs=[SMEM] * 2 + [VMEM] * 7 + [HBM] * 4,
        out_specs=[VMEM, HBM, HBM, HBM],
        us=14,
        vmem=62,
    )(
        place,
        pos,
        received,
        by_sample(cold_band).reshape(cold_feats * bag, batch),
        projection,
        pre,
        dense_input,
        counts,
        hot_unique.reshape(1, unique),
        bottom,
        hot_emb,
        high,
        low,
    )
    returned = exchange(slot_grads, "table")
    dense_pair = dense_kept + to_other_core(dense_given).astype(F32)
    dense_out = dense_pair[1:].astype(BF16)
    dense_row = dense_pair[0]
    for k, steps in enumerate((1, 2, -1)):
        dense_row += along_x(dense_out[k], steps).astype(F32)
    dense_row = dense_row.astype(BF16).reshape(tables, 32, LANES)
    returned, dense_row = lax.optimization_barrier((returned, dense_row))
    dense_all = exchange(dense_row, "table")

    half = rows_dev // 32
    given_far, given_near, given_own, kept_far, kept_near, kept_own = call(
        add_kernel,
        (
            shape((2, half, LANES), BF16),
            shape((2, 2, half, LANES), BF16),
            shape((2, half, LANES), BF16),
            shape((2, half, LANES), BF16),
            shape((2, 2, half, LANES), BF16),
            shape((2, half, LANES), F32),
        ),
        scratch=[pltpu.VMEM((tables * pairs, LANES), F32)] * 2
        + [
            pltpu.VMEM((4, 2, half, LANES), BF16),
            pltpu.VMEM((3, 2, half, LANES), BF16),
            pltpu.VMEM((2, half, LANES), F32),
            pltpu.SemaphoreType.DMA((8,)),
        ]
        + [pltpu.VMEM((rows_dev // 2, LANES), F32)] * 2,
        specs=[SMEM, SMEM, VMEM, VMEM],
        out_specs=[HBM] * 6,
        us=20,
        vmem=62,
    )(place, row_ids, asked, returned)
    given_far, dense_all = lax.optimization_barrier((given_far, dense_all))
    mine = call(dense_kernel, shape((64, LANES), BF16))(dense_all)
    taken_far = to_other_core(given_far)
    theirs = to_other_core(mine)
    up, down = call(far_kernel, (shape((half + 128, LANES), BF16),) * 2, specs=[SMEM] + [VMEM] * 4)(
        place, kept_far, taken_far, mine, theirs
    )
    from_below = along_x(up, 1)
    from_above = along_x(down, -1)
    up, down, cold_emb, given_near, given_own = lax.optimization_barrier(
        (up, down, cold_emb, given_near, given_own)
    )
    taken_near = to_other_core(given_near)
    taken_own = to_other_core(given_own)
    inter = call(
        inter_kernel,
        shape((batch, feats * feats), F32),
        scratch=[
            pltpu.VMEM((feats, batch, hidden), BF16),
            pltpu.VMEM((feats, batch, feats * feats), F32),
        ],
        us=4,
    )(bottom, cold_emb, hot_emb)
    from_below, from_above, taken_near, taken_own, inter = lax.optimization_barrier(
        (from_below, from_above, taken_near, taken_own, inter)
    )
    next_up, next_down = call(
        second_kernel,
        (shape((2 * half + 128, LANES), BF16), shape((2 * half, LANES), BF16)),
    )(kept_near, taken_near, from_below, from_above)
    next_up, next_down, kept_own, taken_own = lax.optimization_barrier(
        (next_up, next_down, kept_own, taken_own)
    )
    pair_own = call(own_kernel, shape((2, half, LANES), F32), us=2)(kept_own, taken_own)
    next_below = along_x(next_up, 1)
    next_above = along_x(next_down, -1)
    cold_grad, hot_grad, projection_grad, bottom_grad = call(
        last_kernel,
        (
            shape((width, rows_dev // 8), F32),
            shape((32, hidden), F32),
            shape((8, hidden), F32),
            shape((16, hidden), F32),
        ),
        specs=[SMEM] + [VMEM] * 6,
        us=2,
    )(place, pair_own, next_below, next_above, up, from_above, from_below)
    return inter, cold_grad.T, hot_grad, projection_grad, bottom_grad


def solution(mesh):
    placed = (
        P(("table", "dp"), None),
        P(),
        P("table", None),
        P(),
        P(),
        P(("table", "dp"), None, None, None),
        P(("table", "dp"), None, None),
        P(("table", "dp"), None, None),
        P(("table", "dp")),
        P(("table", "dp"), None, None),
        P(("table", "dp"), None),
    )
    return jax.shard_map(
        shards,
        mesh=mesh,
        in_specs=placed,
        out_specs=(
            P(("table", "dp"), None),
            P(("table", "dp"), None),
            P("table", None),
            P("table", None),
            P("table", None),
        ),
        check_vma=False,
    )
```

```python
import functools

import jax
import jax.numpy as jnp
from jax import lax
from jax.experimental import pallas as pl
from jax.experimental.pallas import tpu as pltpu
from jax.sharding import PartitionSpec as P

F32 = jnp.float32
BF16 = jnp.bfloat16
LANES = 128
NT = (((1,), (1,)), ((), ()))
TN = (((0,), (0,)), ((), ()))
MIB = 1 << 20


def dot(a, b, dims=(((1,), (0,)), ((), ()))):
    return lax.dot_general(a, b, dims, preferred_element_type=F32)


def split_two(v):
    high = v.astype(BF16)
    return high, (v - high.astype(F32)).astype(BF16)


def iota(shape, dim):
    return lax.broadcasted_iota(jnp.int32, shape, dim)


def call(kernel, outs, scratch=(), specs=None, vmem=16, us=1, grid=None, out_specs=None):
    args = {} if specs is None else {"in_specs": specs}
    if grid is not None:
        args["grid"] = grid
    if out_specs is not None:
        args["out_specs"] = out_specs
    return pl.pallas_call(
        kernel,
        out_shape=outs,
        scratch_shapes=list(scratch),
        compiler_params=pltpu.CompilerParams(vmem_limit_bytes=vmem * MIB),
        cost_estimate=pl.CostEstimate(
            flops=us * 1_100_000_000, bytes_accessed=MIB, transcendentals=0
        ),
        **args,
    )


SMEM = pl.BlockSpec(memory_space=pltpu.SMEM)
VMEM = pl.BlockSpec(memory_space=pltpu.VMEM)
HBM = pl.BlockSpec(memory_space=pltpu.HBM)


def prep_kernel(tables, pairs, owner_ref, local_ref, ids_ref, pos_ref):
    bag = owner_ref.shape[1]
    steps = owner_ref.shape[0] * bag
    owners = [owner_ref[j // bag, j % bag : j % bag + 1, :] for j in range(steps)]
    row, col = iota((LANES, 2 * LANES), 0), iota((LANES, 2 * LANES), 1)
    tri = jnp.where((row < col) | (col >= LANES), 1.0, 0.0).astype(BF16)
    table_row = iota((tables, LANES), 0)
    slot_row = iota((2 * LANES, LANES), 0)
    hits = [
        jnp.where(owner == table_row, 1.0, 0.0) for owner in owners
    ]
    sums = dot(jnp.concatenate(hits, axis=0).astype(BF16), tri)
    carry = jnp.zeros((tables, LANES), F32)
    left, right = [], []
    for j in range(steps):
        part = sums[j * tables : (j + 1) * tables]
        slot = jnp.sum(hits[j] * (part[:, :LANES] + carry), axis=0, keepdims=True)
        slot = slot.astype(jnp.int32)
        carry = carry + part[:, LANES:]
        upper = jnp.where(slot >= pairs, 1, 0)
        pos_ref[j : j + 1, :] = (
            upper * (tables * pairs - pairs) + owners[j] * pairs + slot
        )
        local = local_ref[j // bag, j % bag : j % bag + 1, :]
        code = (((local >> 11) & 1) << 14) | ((local >> 12) << 11) | (local & 2047)
        high, low = (code >> 8).astype(F32), (code & 255).astype(F32)
        left.append(
            jnp.concatenate([hits[j] * high, hits[j] * low, hits[j]], axis=0).astype(BF16)
        )
        right.append(jnp.where(slot + upper * (LANES - pairs) == slot_row, 1.0, 0.0).astype(BF16))
    placed = dot(jnp.concatenate(left, axis=1), jnp.concatenate(right, axis=1), NT)
    ids = (placed[:tables] * 256.0 + placed[tables : 2 * tables]).astype(jnp.int32)
    ids = jnp.where(placed[2 * tables :] > 0.5, ids, iota(ids.shape, 0) * 256 + iota(ids.shape, 1))
    lane = iota(ids.shape, 1)
    rows = ids & 16383
    twice = jnp.zeros(ids.shape, F32)
    for d in range(1, 4):
        met = (rows == pltpu.roll(rows, d, 1)) & (lane % 4 >= d) & (lane % LANES < pairs)
        twice = jnp.where(met, 1.0, twice)
    twice = jnp.max(twice, axis=1, keepdims=True).astype(jnp.int32)
    ids = jnp.where(lane == pairs, twice, ids)
    for k in range(tables):
        ids_ref[k] = ids[k : k + 1]


def lane_is_low(shape):
    return iota(shape, len(shape) - 1) < 64


def gather_kernel(ids_ref, vec_ref, table_ref, out_ref, packed, got_a, got_b):
    tables, pairs, _ = out_ref.shape
    size = 2048
    for c in range(packed.shape[0] // size):
        first = table_ref[:, 2 * c * size : (2 * c + 1) * size]
        second = table_ref[:, (2 * c + 1) * size : (2 * c + 2) * size]
        both = jnp.concatenate([first, second], axis=0)
        packed[c * size : (c + 1) * size, :] = both.astype(F32).T
    step = pairs // 2

    def one(part, source):
        first = source * (2 * LANES) + part * step
        base = pl.multiple_of(source * pairs + part * step, 8)
        read_a = [packed[pl.ds(ids_ref[first + u], 1), :] for u in range(step)]
        read_b = [packed[pl.ds(ids_ref[first + LANES + u], 1), :] for u in range(step)]
        for u in range(step):
            got_a[pl.ds(base + u, 1), :] = read_a[u]
            got_b[pl.ds(base + u, 1), :] = read_b[u]
        return source

    def per_source(source, carry):
        lax.fori_loop(0, 2, one, source)
        return carry

    lax.fori_loop(0, tables, per_source, 0)
    upper = (vec_ref[...] >> 14).astype(F32).T
    low = lane_is_low((pairs, LANES))
    for k in range(tables):
        a = got_a[k * pairs : (k + 1) * pairs, :]
        b = got_b[k * pairs : (k + 1) * pairs, :]
        up_a = upper[:pairs, k : k + 1] > 0.5
        up_b = upper[LANES : LANES + pairs, k : k + 1] > 0.5
        a = jnp.where(up_a, pltpu.roll(a, 64, 1), a)
        b = jnp.where(up_b, b, pltpu.roll(b, 64, 1))
        out_ref[k] = jnp.where(low, a, b).astype(BF16)


def front_kernel(
    dense_ref,
    weight_ref,
    hot_ref,
    unique_ref,
    line_ref,
    map_ref,
    grad_ref,
    pre_ref,
    bottom_ref,
    emb_ref,
    extra_ref,
    high_ref,
    low_ref,
):
    batch = dense_ref.shape[0]
    hot_feats, bag = map_ref.shape[0], map_ref.shape[1]
    unique = unique_ref.shape[0]
    feats = high_ref.shape[0]
    pre = dot(dense_ref[...], weight_ref[...])
    pre_ref[...] = pre
    bottom_ref[...] = jax.nn.silu(pre).astype(BF16)
    picks = jnp.where(unique_ref[...] == iota((unique, hot_ref.shape[0]), 1), 1.0, 0.0)
    rows = dot(picks.astype(BF16), hot_ref[...]).astype(BF16)
    place = iota((unique, batch), 0)
    for h in range(hot_feats):
        count = jnp.zeros((unique, batch), F32)
        for l in range(bag):
            count += jnp.where(map_ref[h, l : l + 1, :] == place, 1.0, 0.0)
        at = slice(h % 4 * batch, (h % 4 + 1) * batch)
        extra_ref[h // 4 * 2, :, at] = count[:batch].astype(BF16)
        extra_ref[h // 4 * 2 + 1, :, at] = count[batch:].astype(BF16)
        emb_ref[h] = dot(count.T.astype(BF16), rows).astype(BF16)
    line = line_ref[...]
    line = jnp.concatenate([line >> 5, line & 31], axis=1).astype(F32)
    extra_ref[4] = jnp.broadcast_to(line, extra_ref.shape[1:]).astype(BF16)
    grad = grad_ref[...]
    grad_high, grad_low = split_two(grad)
    square = feats * feats
    at = iota((square, square), 0)
    other = iota((square, square), 1) // feats
    same = iota((batch, square), 0) % feats == iota((batch, square), 1) % feats
    for f in range(feats):
        pick = jnp.where(at == f * feats + other, 1.0, 0.0) + jnp.where(
            at == other * feats + f, 1.0, 0.0
        )
        pick = pick.astype(BF16)
        spread = jnp.where(same, dot(grad_high, pick) + dot(grad_low, pick), 0.0)
        high_ref[f], low_ref[f] = split_two(spread)


def silu_slope(pre):
    sigma = jax.nn.sigmoid(pre)
    return sigma * (1.0 + pre * (1.0 - sigma))


def main_kernel(
    place_ref,
    pos_ref,
    rows_ref,
    band_ref,
    proj_ref,
    pre_ref,
    dense_ref,
    extra_ref,
    bottom_ref,
    hot_ref,
    high_ref,
    low_ref,
    slots_ref,
    cold_ref,
    keep_ref,
    give_ref,
    wide,
    lookups,
    stack,
    high,
    low_part,
    d_stack,
    bags,
    pre,
    d_pre,
    dense,
    extra,
    sems,
):
    tables, pairs, _ = rows_ref.shape
    feats, batch, hidden = stack.shape
    cold_feats = cold_ref.shape[0]
    bag = band_ref.shape[0] // cold_feats
    half = tables * pairs
    fixed = pl.ds(1 + cold_feats, feats - 1 - cold_feats)
    incoming = [
        pltpu.make_async_copy(bottom_ref, stack.at[0], sems.at[0]),
        pltpu.make_async_copy(hot_ref, stack.at[fixed], sems.at[1]),
        pltpu.make_async_copy(high_ref, high, sems.at[2]),
        pltpu.make_async_copy(low_ref, low_part, sems.at[3]),
        pltpu.make_async_copy(pre_ref, pre, sems.at[11]),
        pltpu.make_async_copy(dense_ref, dense, sems.at[12]),
        pltpu.make_async_copy(extra_ref, extra, sems.at[13]),
    ]
    for copy in incoming:
        copy.start()
    low = lane_is_low((pairs, LANES))
    for k in range(tables):
        x = rows_ref[k].astype(F32)
        r = pltpu.roll(x, 64, 1)
        wide[k * pairs : (k + 1) * pairs, :] = jnp.where(low, x, r)
        wide[half + k * pairs : half + (k + 1) * pairs, :] = jnp.where(low, r, x)

    def fetch(i, carry):
        base = pl.multiple_of(i * 128, 8)
        got = [wide[pl.ds(pos_ref[base + u], 1), :] for u in range(128)]
        for u in range(128):
            lookups[pl.ds(base + u, 1), :] = got[u]
        return carry

    lax.fori_loop(0, lookups.shape[0] // 128, fetch, 0)
    band = band_ref[...].astype(F32).T
    side = jnp.where(lane_is_low((batch, LANES)), 0.0, 1.0)
    bands = proj_ref.shape[0]
    bags[3, :, bands:] = jnp.zeros((batch, hidden - bands), BF16)
    for f in range(cold_feats):
        first = jnp.zeros((batch, LANES), F32)
        second = jnp.zeros((batch, LANES), F32)
        for l in range(bag):
            j = f * bag + l
            x = lookups[j * batch : (j + 1) * batch, :]
            b = band[:, j : j + 1] - side
            first += jnp.where(b == 0.0, x, 0.0)
            second += jnp.where(b == 2.0, x, 0.0)
        pooled = jnp.concatenate([first, second], axis=1).astype(BF16)
        bags[f // 2, :, f % 2 * bands : (f % 2 + 1) * bands] = pooled
        stack[1 + f] = dot(pooled, proj_ref[...]).astype(BF16)
    outgoing = pltpu.make_async_copy(stack.at[pl.ds(1, cold_feats)], cold_ref, sems.at[4])
    outgoing.start()
    for copy in incoming:
        copy.wait()
    for g in range(batch // 16):
        at = slice(g * 16, (g + 1) * 16)
        x = stack[:, at, :].reshape(feats * 16, hidden)
        first = high[:, at, :].reshape(feats * 16, feats * 16)
        rest = low_part[:, at, :].reshape(feats * 16, feats * 16)
        d = (dot(first, x) + dot(rest, x)).astype(BF16)
        d_stack[:, at, :] = d.reshape(feats, 16, hidden)
    d_pre[...] = (d_stack[0].astype(F32) * silu_slope(pre[...])).astype(BF16)

    def factors(hot_to, rest_to):
        pieces = [
            (d_stack.at[fixed], hot_to.at[pl.ds(0, 8)]),
            (extra, hot_to.at[pl.ds(8, 5)]),
            (d_stack.at[pl.ds(1, cold_feats)], rest_to.at[pl.ds(0, 7)]),
            (bags, rest_to.at[pl.ds(7, 4)]),
            (dense, rest_to.at[11]),
            (d_pre, rest_to.at[12]),
        ]
        return [pltpu.make_async_copy(*p, sems.at[5 + i]) for i, p in enumerate(pieces)]

    first_core = place_ref[1] == 0

    @pl.when(first_core)
    def _():
        for copy in factors(keep_ref, give_ref):
            copy.start()

    @pl.when(jnp.logical_not(first_core))
    def _():
        for copy in factors(give_ref, keep_ref):
            copy.start()

    low = lane_is_low((batch, LANES))
    for f in range(cold_feats):
        d_pool = dot(d_stack[1 + f], proj_ref[...], NT).astype(BF16).astype(F32)
        first, second = d_pool[:, :LANES], d_pool[:, LANES:]
        first_r, second_r = pltpu.roll(first, 64, 1), pltpu.roll(second, 64, 1)
        each = [
            jnp.where(low, first, first_r),
            jnp.where(low, first_r, first),
            jnp.where(low, second, second_r),
            jnp.where(low, second_r, second),
        ]
        for l in range(bag):
            j = f * bag + l
            b = jnp.broadcast_to(band[:, j : j + 1], (batch, LANES))
            x = jnp.where(b < 0.5, each[0], each[1])
            y = jnp.where(b < 2.5, each[2], each[3])
            lookups[j * batch : (j + 1) * batch, :] = jnp.where(b < 1.5, x, y)
            share = wide.shape[0] // (cold_feats * bag)
            wide[j * share : (j + 1) * share, :] = jnp.zeros((share, LANES), F32)

    def place(i, carry):
        base = pl.multiple_of(i * 128, 8)
        got = [lookups[pl.ds(base + u, 1), :] for u in range(128)]
        for u in range(128):
            wide[pl.ds(pos_ref[base + u], 1), :] = got[u]
        return carry

    lax.fori_loop(0, lookups.shape[0] // 128, place, 0)
    low = lane_is_low((pairs, LANES))
    for k in range(tables):
        a = wide[k * pairs : (k + 1) * pairs, :]
        b = wide[half + k * pairs : half + (k + 1) * pairs, :]
        slots_ref[k] = jnp.where(low, a, b).astype(BF16)
    outgoing.wait()

    @pl.when(first_core)
    def _():
        for copy in factors(keep_ref, give_ref):
            copy.wait()

    @pl.when(jnp.logical_not(first_core))
    def _():
        for copy in factors(give_ref, keep_ref):
            copy.wait()


def dense_part_kernel(place_ref, keep_ref, took_ref, own_ref, up_ref, far_ref, down_ref, sums):
    cuts, rows, _ = sums.shape
    batch, hidden = keep_ref.shape[1:]

    def put(make):
        for c in range(cuts):
            sums[(c - place_ref[0] + cuts) % cuts] = make(slice(c * LANES, (c + 1) * LANES))

    @pl.when(place_ref[1] == 0)
    def _():
        picks, parts = [], []
        for ref in (keep_ref, took_ref):
            d_hot = ref[:8].reshape(8 * batch, hidden)
            counts = [jnp.concatenate([ref[8 + u], ref[10 + u]], axis=1) for u in range(2)]
            parts.append(dot(jnp.concatenate(counts, axis=0), d_hot))
            line = ref[12][:16].astype(F32)[:1]
            line = line[:, : hidden // 2] * 32.0 + line[:, hidden // 2 :]
            at = iota((rows, hidden // 2), 0).astype(F32)
            picks.append(jnp.where(at == line, 1.0, 0.0).astype(BF16))
        picks = jnp.concatenate(picks, axis=1)
        high, rest = split_two(jnp.concatenate(parts, axis=0))
        hot = dot(picks, high) + dot(picks, rest)
        put(lambda at: hot[:, at])

    @pl.when(place_ref[1] != 0)
    def _():
        both = (keep_ref, took_ref)
        dense = jnp.concatenate([ref[11] for ref in both], axis=0)
        d_pre = jnp.concatenate([ref[12] for ref in both], axis=0)
        bottom = dot(dense, d_pre, TN)
        half = hidden // 2
        proj = jnp.zeros((half, hidden), F32)
        for ref in both:
            bags = [ref[7 + f // 2][:, f % 2 * half : (f % 2 + 1) * half] for f in range(7)]
            d_cold = ref[:7].reshape(7 * batch, hidden)
            proj += dot(jnp.concatenate(bags, axis=0), d_cold, TN)
        tables = rows // 32
        put(
            lambda at: jnp.concatenate(
                [
                    bottom[:, at].reshape(tables, 16, LANES),
                    proj[:, at].reshape(tables, 8, LANES),
                    jnp.zeros((tables, 8, LANES), F32),
                ],
                axis=1,
            ).reshape(rows, LANES)
        )

    own_ref[...] = sums[0]
    for k, out_ref in enumerate((up_ref, far_ref, down_ref)):
        out_ref[...] = sums[k + 1].astype(BF16)


def inter_kernel(bottom_ref, cold_ref, hot_ref, inter_ref, stack, grams):
    feats, batch, hidden = stack.shape
    cold_feats = cold_ref.shape[0]
    stack[0] = bottom_ref[...]
    for f in range(cold_feats):
        stack[1 + f] = cold_ref[f]
    for h in range(hot_ref.shape[0]):
        stack[1 + cold_feats + h] = hot_ref[h]
    square = feats * feats
    same = iota((square, square), 0) % feats == iota((square, square), 1) % feats
    for g in range(batch // 16):
        at = slice(g * 16, (g + 1) * 16)
        x = stack[:, at, :].reshape(feats * 16, hidden)
        grams[:, at, :] = jnp.where(same, dot(x, x, NT), 0.0).reshape(feats, 16, square)
    total = jnp.zeros((batch, square), F32)
    other = iota((square, square), 0) // feats
    to = iota((square, square), 1)
    for f in range(feats):
        pick = jnp.where(to == f * feats + other, 1.0, 0.0).astype(BF16)
        high, rest = split_two(grams[f])
        total += dot(high, pick) + dot(rest, pick)
    inter_ref[...] = total


def add_kernel(
    place_ref,
    ids_ref,
    vec_ref,
    rows_ref,
    given_far_ref,
    given_near_ref,
    given_own_ref,
    kept_far_ref,
    kept_near_ref,
    kept_own_ref,
    val_a,
    val_b,
    given,
    kept,
    kept_own,
    sems,
    *sums,
):
    tables, pairs, _ = rows_ref.shape
    upper = (vec_ref[...] >> 14).astype(F32).T
    low = lane_is_low((pairs, LANES))
    side = jnp.where(low, 0.0, 1.0)
    for k in range(tables):
        x = rows_ref[k].astype(F32)
        r = pltpu.roll(x, 64, 1)
        share = sums[0].shape[0] // tables
        for part in sums:
            part[k * share : (k + 1) * share, :] = jnp.zeros((share, LANES), F32)
        at = slice(k * pairs, (k + 1) * pairs)
        up_a, up_b = upper[:pairs, k : k + 1], upper[LANES : LANES + pairs, k : k + 1]
        val_a[at, :] = jnp.where(up_a == side, jnp.where(low, x, r), 0.0)
        val_b[at, :] = jnp.where(up_b == side, jnp.where(low, r, x), 0.0)
    sides = ((0, val_a, sums[0]), (LANES, val_b, sums[1]))
    step = pairs // 2

    def spread(part, source):
        first = source * (2 * LANES) + part * step
        base = pl.multiple_of(source * pairs + part * step, 8)
        for q in range(0, step, 4):
            work = [
                (to, ids_ref[first + lane + q + t], val[pl.ds(base + q + t, 1), :])
                for lane, val, to in sides
                for t in range(4)
            ]
            new = [to[pl.ds(row, 1), :] + value for to, row, value in work]
            for (to, row, _), value in zip(work, new):
                to[pl.ds(row, 1), :] = value
        return source

    def one_by_one(group, source):
        first = source * (2 * LANES) + group * 8
        base = pl.multiple_of(source * pairs + group * 8, 8)
        for u in range(8):
            for lane, val, to in sides:
                row = ids_ref[first + lane + u]
                to[pl.ds(row, 1), :] = to[pl.ds(row, 1), :] + val[pl.ds(base + u, 1), :]
        return source

    def per_source(source, carry):
        twice = ids_ref[source * (2 * LANES) + pairs]

        @pl.when(twice == 0)
        def _():
            lax.fori_loop(0, 2, spread, source)

        @pl.when(twice != 0)
        def _():
            lax.fori_loop(0, pairs // 8, one_by_one, source)

        return carry

    lax.fori_loop(0, tables, per_source, 0)
    core = place_ref[1]
    half = kept_own.shape[1]
    size = 2 * half

    def total(k, h, of):
        chunk = 2 * ((place_ref[0] + k) % 4) + of
        at = pl.ds(pl.multiple_of(chunk * size + h * half, half), half)
        return functools.reduce(jnp.add, [part[at, :] for part in sums])

    copies = []

    def send(source, target):
        copies.append(pltpu.make_async_copy(source, target, sems.at[len(copies)]))
        copies[-1].start()

    for k, target in enumerate((given_far_ref, given_near_ref, given_near_ref, given_own_ref)):
        for h in range(2):
            given[k, h] = total((2, 1, 3, 0)[k], h, 1 - core).astype(BF16)
        send(given.at[k], target.at[k - 1] if k in (1, 2) else target)
    for k, target in enumerate((kept_far_ref, kept_near_ref, kept_near_ref)):
        for h in range(2):
            kept[k, h] = total((2, 1, 3)[k], h, core).astype(BF16)
        send(kept.at[k], target.at[k - 1] if k else target)
    for h in range(2):
        kept_own[h] = total(0, h, core)
    send(kept_own, kept_own_ref)
    for copy in copies:
        copy.wait()


def sum_rows(rows_ref):
    total = rows_ref[0].astype(F32)
    for k in range(1, rows_ref.shape[0]):
        total += rows_ref[k].astype(F32)
    return total


def dense_kernel(rows_ref, out_ref):
    rows = rows_ref.shape[1]
    out_ref[:rows], out_ref[rows:] = split_two(sum_rows(rows_ref))


def add_pair(kept, taken):
    return (kept.astype(F32) + taken.astype(F32)).astype(BF16)


def far_kernel(place_ref, kept_ref, taken_ref, mine_ref, theirs_ref, up_ref, down_ref):
    half = kept_ref.shape[1]
    rows = mine_ref.shape[0]
    first = place_ref[1] == 0
    mine, theirs = mine_ref[...].astype(F32), theirs_ref[...].astype(F32)
    low = jnp.where(first, mine, theirs).astype(BF16)
    high = jnp.where(first, theirs, mine).astype(BF16)
    for h, out_ref in enumerate((up_ref, down_ref)):
        out_ref[:half] = add_pair(kept_ref[h], taken_ref[h])
        out_ref[half : half + rows] = low
        out_ref[half + rows :] = high


def second_kernel(kept_ref, taken_ref, below_ref, above_ref, up_ref, down_ref):
    half = kept_ref.shape[2]

    def total(k, h, far):
        return (
            kept_ref[k, h].astype(F32) + taken_ref[k, h].astype(F32) + far.astype(F32)
        ).astype(BF16)

    up_ref[:half] = total(0, 0, below_ref[:half])
    up_ref[half : 2 * half] = add_pair(kept_ref[0, 1], taken_ref[0, 1])
    up_ref[2 * half :] = below_ref[half:]
    down_ref[:half] = add_pair(kept_ref[1, 0], taken_ref[1, 0])
    down_ref[half:] = total(1, 1, above_ref[:half])


def own_kernel(kept_ref, taken_ref, out_ref):
    out_ref[...] = kept_ref[...] + taken_ref[...].astype(F32)


def last_kernel(
    place_ref,
    pair_ref,
    below_ref,
    above_ref,
    own_ref,
    next_ref,
    before_ref,
    out_ref,
    hot_ref,
    proj_ref,
    bottom_ref,
):
    half = pair_ref.shape[1]

    def total(h):
        at = slice(h * half, (h + 1) * half)
        return pair_ref[h] + below_ref[at].astype(F32) + above_ref[at].astype(F32)

    wide = jnp.concatenate([total(0), total(1)], axis=0).T
    out_ref[...] = jnp.concatenate([wide[:64], wide[64:]], axis=1)
    tails = (own_ref[half:], next_ref[half:], below_ref[2 * half :], before_ref[half:])
    for k, tail in enumerate(tails):
        chunk = (place_ref[0] + k) % len(tails)
        at = pl.ds(pl.multiple_of(chunk * LANES, LANES), LANES)
        rows = tail.astype(F32)
        hot_ref[:, at] = rows[:32] + rows[32:64]
        rest = rows[64:96] + rows[96:]
        bottom_ref[:, at] = rest[:16]
        proj_ref[:, at] = rest[16:24]


def to_other_core(x):
    return lax.ppermute(x, "dp", [(i, i ^ 1) for i in range(8)])


def along_x(x, steps):
    return lax.ppermute(x, "dp", [(i, (i + 2 * steps) % 8) for i in range(8)])


def exchange(x, axis):
    return lax.all_to_all(x, axis, split_axis=0, concat_axis=0, tiled=True)


def shards(
    dense_input,
    bottom_weight,
    cold_table,
    projection,
    hot_table,
    cold_owner,
    cold_local,
    cold_band,
    hot_unique,
    hot_map,
    grad_inter,
):
    batch, hidden = dense_input.shape
    cold_feats, bag = cold_local.shape[1], cold_local.shape[2]
    hot_feats = hot_map.shape[1]
    feats = 1 + cold_feats + hot_feats
    tables = lax.axis_size("table")
    rows_dev, width = cold_table.shape
    unique = hot_unique.shape[0]
    lookups = batch * cold_feats * bag
    slots = 2 * lookups // tables
    pairs = slots // 2
    bands = projection.shape[0]
    at_dp = lax.axis_index("dp").astype(jnp.int32)
    place = jnp.stack([at_dp // 2, at_dp % 2])

    def by_sample(v):
        return jnp.transpose(v.reshape(batch, cold_feats, bag), (1, 2, 0))

    shape = jax.ShapeDtypeStruct
    ids, pos = call(
        functools.partial(prep_kernel, tables, pairs),
        (shape((tables, 1, 2 * LANES), jnp.int32), shape((cold_feats * bag, batch), jnp.int32)),
    )(by_sample(cold_owner), by_sample(cold_local))
    pos = pos.reshape(lookups)
    asked = exchange(ids, "table").reshape(tables, 2 * LANES)
    row_ids = (asked & (rows_dev // 2 - 1)).reshape(tables * 2 * LANES)
    fetched = call(
        gather_kernel,
        shape((tables, pairs, LANES), BF16),
        scratch=[pltpu.VMEM((rows_dev // 2, LANES), F32)]
        + [pltpu.VMEM((tables * pairs, LANES), F32)] * 2,
        specs=[SMEM, VMEM, VMEM],
        us=12,
        vmem=24,
    )(row_ids, asked, cold_table.T)
    received = exchange(fetched, "table")
    pre, bottom, hot_emb, extra, high, low = call(
        front_kernel,
        (
            shape((batch, hidden), F32),
            shape((batch, hidden), BF16),
            shape((hot_feats, batch, hidden), BF16),
            shape((5, batch, hidden), BF16),
            shape((feats, batch, feats * feats), BF16),
            shape((feats, batch, feats * feats), BF16),
        ),
        us=3,
    )(
        dense_input,
        bottom_weight,
        hot_table,
        hot_unique.reshape(unique, 1),
        hot_unique.reshape(1, unique),
        jnp.transpose(hot_map, (1, 2, 0)),
        grad_inter,
    )
    cuts = hidden // LANES
    slot_grads, cold_emb, keep, give = call(
        main_kernel,
        (
            shape((tables, pairs, LANES), BF16),
            shape((cold_feats, batch, hidden), BF16),
            shape((13, batch, hidden), BF16),
            shape((13, batch, hidden), BF16),
        ),
        scratch=[
            pltpu.VMEM((2 * tables * pairs, LANES), F32),
            pltpu.VMEM((lookups, LANES), F32),
            pltpu.VMEM((feats, batch, hidden), BF16),
            pltpu.VMEM((feats, batch, feats * feats), BF16),
            pltpu.VMEM((feats, batch, feats * feats), BF16),
            pltpu.VMEM((feats, batch, hidden), BF16),
            pltpu.VMEM((4, batch, hidden), BF16),
            pltpu.VMEM((batch, hidden), F32),
            pltpu.VMEM((batch, hidden), BF16),
            pltpu.VMEM((batch, hidden), BF16),
            pltpu.VMEM((5, batch, hidden), BF16),
            pltpu.SemaphoreType.DMA((14,)),
        ],
        specs=[SMEM] * 2 + [VMEM] * 3 + [HBM] * 7,
        out_specs=[VMEM, HBM, HBM, HBM],
        us=14,
        vmem=62,
    )(
        place,
        pos,
        received,
        by_sample(cold_band).reshape(cold_feats * bag, batch),
        projection,
        pre,
        dense_input,
        extra,
        bottom,
        hot_emb,
        high,
        low,
    )
    returned = exchange(slot_grads, "table")
    took = to_other_core(give)
    dense_row, dense_up, dense_far, dense_down = call(
        dense_part_kernel,
        (shape((tables * 32, LANES), F32),) + (shape((tables * 32, LANES), BF16),) * 3,
        scratch=[pltpu.VMEM((cuts, tables * 32, LANES), F32)],
        specs=[SMEM, VMEM, VMEM],
        us=4,
        vmem=32,
    )(place, keep, took)
    for part, steps in ((dense_up, 1), (dense_far, 2), (dense_down, -1)):
        dense_row += along_x(part, steps).astype(F32)
    dense_row = dense_row.astype(BF16).reshape(tables, 32, LANES)
    returned, dense_row = lax.optimization_barrier((returned, dense_row))
    dense_all = exchange(dense_row, "table")

    half = rows_dev // 32
    given_far, given_near, given_own, kept_far, kept_near, kept_own = call(
        add_kernel,
        (
            shape((2, half, LANES), BF16),
            shape((2, 2, half, LANES), BF16),
            shape((2, half, LANES), BF16),
            shape((2, half, LANES), BF16),
            shape((2, 2, half, LANES), BF16),
            shape((2, half, LANES), F32),
        ),
        scratch=[pltpu.VMEM((tables * pairs, LANES), F32)] * 2
        + [
            pltpu.VMEM((4, 2, half, LANES), BF16),
            pltpu.VMEM((3, 2, half, LANES), BF16),
            pltpu.VMEM((2, half, LANES), F32),
            pltpu.SemaphoreType.DMA((8,)),
        ]
        + [pltpu.VMEM((rows_dev // 2, LANES), F32)] * 2,
        specs=[SMEM, SMEM, VMEM, VMEM],
        out_specs=[HBM] * 6,
        us=20,
        vmem=62,
    )(place, row_ids, asked, returned)
    given_far, dense_all = lax.optimization_barrier((given_far, dense_all))
    mine = call(dense_kernel, shape((64, LANES), BF16))(dense_all)
    taken_far = to_other_core(given_far)
    theirs = to_other_core(mine)
    up, down = call(far_kernel, (shape((half + 128, LANES), BF16),) * 2, specs=[SMEM] + [VMEM] * 4)(
        place, kept_far, taken_far, mine, theirs
    )
    from_below = along_x(up, 1)
    from_above = along_x(down, -1)
    up, down, cold_emb, given_near, given_own = lax.optimization_barrier(
        (up, down, cold_emb, given_near, given_own)
    )
    taken_near = to_other_core(given_near)
    taken_own = to_other_core(given_own)
    inter = call(
        inter_kernel,
        shape((batch, feats * feats), F32),
        scratch=[
            pltpu.VMEM((feats, batch, hidden), BF16),
            pltpu.VMEM((feats, batch, feats * feats), F32),
        ],
        us=4,
    )(bottom, cold_emb, hot_emb)
    from_below, from_above, taken_near, taken_own, inter = lax.optimization_barrier(
        (from_below, from_above, taken_near, taken_own, inter)
    )
    next_up, next_down = call(
        second_kernel,
        (shape((2 * half + 128, LANES), BF16), shape((2 * half, LANES), BF16)),
    )(kept_near, taken_near, from_below, from_above)
    next_up, next_down, kept_own, taken_own = lax.optimization_barrier(
        (next_up, next_down, kept_own, taken_own)
    )
    pair_own = call(own_kernel, shape((2, half, LANES), F32), us=2)(kept_own, taken_own)
    next_below = along_x(next_up, 1)
    next_above = along_x(next_down, -1)
    cold_grad, hot_grad, projection_grad, bottom_grad = call(
        last_kernel,
        (
            shape((width, rows_dev // 8), F32),
            shape((32, hidden), F32),
            shape((8, hidden), F32),
            shape((16, hidden), F32),
        ),
        specs=[SMEM] + [VMEM] * 6,
        us=2,
    )(place, pair_own, next_below, next_above, up, from_above, from_below)
    return inter, cold_grad.T, hot_grad, projection_grad, bottom_grad


def solution(mesh):
    placed = (
        P(("table", "dp"), None),
        P(),
        P("table", None),
        P(),
        P(),
        P(("table", "dp"), None, None, None),
        P(("table", "dp"), None, None),
        P(("table", "dp"), None, None),
        P(("table", "dp")),
        P(("table", "dp"), None, None),
        P(("table", "dp"), None),
    )
    return jax.shard_map(
        shards,
        mesh=mesh,
        in_specs=placed,
        out_specs=(
            P(("table", "dp"), None),
            P(("table", "dp"), None),
            P("table", None),
            P("table", None),
            P("table", None),
        ),
        check_vma=False,
    )
```

```python
import functools

import jax
import jax.numpy as jnp
from jax import lax
from jax.experimental import pallas as pl
from jax.experimental.pallas import tpu as pltpu
from jax.sharding import PartitionSpec as P

F32 = jnp.float32
BF16 = jnp.bfloat16
LANES = 128
NT = (((1,), (1,)), ((), ()))
TN = (((0,), (0,)), ((), ()))
MIB = 1 << 20


def dot(a, b, dims=(((1,), (0,)), ((), ()))):
    return lax.dot_general(a, b, dims, preferred_element_type=F32)


def split_two(v):
    high = v.astype(BF16)
    return high, (v - high.astype(F32)).astype(BF16)


def iota(shape, dim):
    return lax.broadcasted_iota(jnp.int32, shape, dim)


def call(kernel, outs, scratch=(), specs=None, vmem=16, us=1, grid=None, out_specs=None):
    args = {} if specs is None else {"in_specs": specs}
    if grid is not None:
        args["grid"] = grid
    if out_specs is not None:
        args["out_specs"] = out_specs
    return pl.pallas_call(
        kernel,
        out_shape=outs,
        scratch_shapes=list(scratch),
        compiler_params=pltpu.CompilerParams(vmem_limit_bytes=vmem * MIB),
        cost_estimate=pl.CostEstimate(
            flops=us * 1_100_000_000, bytes_accessed=MIB, transcendentals=0
        ),
        **args,
    )


SMEM = pl.BlockSpec(memory_space=pltpu.SMEM)
VMEM = pl.BlockSpec(memory_space=pltpu.VMEM)
HBM = pl.BlockSpec(memory_space=pltpu.HBM)


def prep_kernel(tables, pairs, owner_ref, local_ref, ids_ref, pos_ref):
    bag = owner_ref.shape[1]
    steps = owner_ref.shape[0] * bag
    owners = [owner_ref[j // bag, j % bag : j % bag + 1, :] for j in range(steps)]
    row, col = iota((LANES, 2 * LANES), 0), iota((LANES, 2 * LANES), 1)
    tri = jnp.where((row < col) | (col >= LANES), 1.0, 0.0).astype(BF16)
    table_row = iota((tables, LANES), 0)
    slot_row = iota((2 * LANES, LANES), 0)
    hits = [
        jnp.where(owner == table_row, 1.0, 0.0) for owner in owners
    ]
    sums = dot(jnp.concatenate(hits, axis=0).astype(BF16), tri)
    carry = jnp.zeros((tables, LANES), F32)
    left, right = [], []
    for j in range(steps):
        part = sums[j * tables : (j + 1) * tables]
        slot = jnp.sum(hits[j] * (part[:, :LANES] + carry), axis=0, keepdims=True)
        slot = slot.astype(jnp.int32)
        carry = carry + part[:, LANES:]
        upper = jnp.where(slot >= pairs, 1, 0)
        pos_ref[j : j + 1, :] = (
            upper * (tables * pairs - pairs) + owners[j] * pairs + slot
        )
        local = local_ref[j // bag, j % bag : j % bag + 1, :]
        code = (((local >> 11) & 1) << 14) | ((local >> 12) << 11) | (local & 2047)
        high, low = (code >> 8).astype(F32), (code & 255).astype(F32)
        left.append(
            jnp.concatenate([hits[j] * high, hits[j] * low, hits[j]], axis=0).astype(BF16)
        )
        right.append(jnp.where(slot + upper * (LANES - pairs) == slot_row, 1.0, 0.0).astype(BF16))
    placed = dot(jnp.concatenate(left, axis=1), jnp.concatenate(right, axis=1), NT)
    ids = (placed[:tables] * 256.0 + placed[tables : 2 * tables]).astype(jnp.int32)
    ids = jnp.where(placed[2 * tables :] > 0.5, ids, iota(ids.shape, 0) * 256 + iota(ids.shape, 1))
    lane = iota(ids.shape, 1)
    rows = ids & 16383
    twice = jnp.zeros(ids.shape, F32)
    for d in range(1, 4):
        met = (rows == pltpu.roll(rows, d, 1)) & (lane % 4 >= d) & (lane % LANES < pairs)
        twice = jnp.where(met, 1.0, twice)
    twice = jnp.max(twice, axis=1, keepdims=True).astype(jnp.int32)
    ids = jnp.where(lane == pairs, twice, ids)
    for k in range(tables):
        ids_ref[k] = ids[k : k + 1]


def lane_is_low(shape):
    return iota(shape, len(shape) - 1) < 64


def gather_kernel(ids_ref, vec_ref, table_ref, out_ref, packed, got_a, got_b):
    tables, pairs, _ = out_ref.shape
    size = 2048
    for c in range(packed.shape[0] // size):
        first = table_ref[:, 2 * c * size : (2 * c + 1) * size]
        second = table_ref[:, (2 * c + 1) * size : (2 * c + 2) * size]
        both = jnp.concatenate([first, second], axis=0)
        packed[c * size : (c + 1) * size, :] = both.astype(F32).T
    step = pairs // 2

    def one(part, source):
        first = source * (2 * LANES) + part * step
        base = pl.multiple_of(source * pairs + part * step, 8)
        read_a = [packed[pl.ds(ids_ref[first + u], 1), :] for u in range(step)]
        read_b = [packed[pl.ds(ids_ref[first + LANES + u], 1), :] for u in range(step)]
        for u in range(step):
            got_a[pl.ds(base + u, 1), :] = read_a[u]
            got_b[pl.ds(base + u, 1), :] = read_b[u]
        return source

    def per_source(source, carry):
        lax.fori_loop(0, 2, one, source)
        return carry

    lax.fori_loop(0, tables, per_source, 0)
    upper = (vec_ref[...] >> 14).astype(F32).T
    low = lane_is_low((pairs, LANES))
    for k in range(tables):
        a = got_a[k * pairs : (k + 1) * pairs, :]
        b = got_b[k * pairs : (k + 1) * pairs, :]
        up_a = upper[:pairs, k : k + 1] > 0.5
        up_b = upper[LANES : LANES + pairs, k : k + 1] > 0.5
        a = jnp.where(up_a, pltpu.roll(a, 64, 1), a)
        b = jnp.where(up_b, b, pltpu.roll(b, 64, 1))
        out_ref[k] = jnp.where(low, a, b).astype(BF16)


def front_kernel(
    dense_ref,
    weight_ref,
    hot_ref,
    unique_ref,
    line_ref,
    map_ref,
    grad_ref,
    pre_ref,
    bottom_ref,
    emb_ref,
    extra_ref,
    high_ref,
    low_ref,
):
    batch = dense_ref.shape[0]
    hot_feats, bag = map_ref.shape[0], map_ref.shape[1]
    unique = unique_ref.shape[0]
    feats = high_ref.shape[0]
    pre = dot(dense_ref[...], weight_ref[...])
    pre_ref[...] = pre
    bottom_ref[...] = jax.nn.silu(pre).astype(BF16)
    picks = jnp.where(unique_ref[...] == iota((unique, hot_ref.shape[0]), 1), 1.0, 0.0)
    rows = dot(picks.astype(BF16), hot_ref[...]).astype(BF16)
    place = iota((unique, batch), 0)
    for h in range(hot_feats):
        count = jnp.zeros((unique, batch), F32)
        for l in range(bag):
            count += jnp.where(map_ref[h, l : l + 1, :] == place, 1.0, 0.0)
        at = slice(h % 4 * batch, (h % 4 + 1) * batch)
        extra_ref[h // 4 * 2, :, at] = count[:batch].astype(BF16)
        extra_ref[h // 4 * 2 + 1, :, at] = count[batch:].astype(BF16)
        emb_ref[h] = dot(count.T.astype(BF16), rows).astype(BF16)
    line = line_ref[...]
    line = jnp.concatenate([line >> 5, line & 31], axis=1).astype(F32)
    extra_ref[4] = jnp.broadcast_to(line, extra_ref.shape[1:]).astype(BF16)
    grad = grad_ref[...]
    grad_high, grad_low = split_two(grad)
    square = feats * feats
    at = iota((square, square), 0)
    other = iota((square, square), 1) // feats
    same = iota((batch, square), 0) % feats == iota((batch, square), 1) % feats
    for f in range(feats):
        pick = jnp.where(at == f * feats + other, 1.0, 0.0) + jnp.where(
            at == other * feats + f, 1.0, 0.0
        )
        pick = pick.astype(BF16)
        spread = jnp.where(same, dot(grad_high, pick) + dot(grad_low, pick), 0.0)
        high_ref[f], low_ref[f] = split_two(spread)


def silu_slope(pre):
    sigma = jax.nn.sigmoid(pre)
    return sigma * (1.0 + pre * (1.0 - sigma))


def main_kernel(
    place_ref,
    pos_ref,
    rows_ref,
    band_ref,
    proj_ref,
    pre_ref,
    dense_ref,
    extra_ref,
    bottom_ref,
    hot_ref,
    high_ref,
    low_ref,
    slots_ref,
    cold_ref,
    keep_ref,
    give_ref,
    wide,
    lookups,
    stack,
    high,
    low_part,
    d_stack,
    bags,
    pre,
    d_pre,
    dense,
    extra,
    sems,
):
    tables, pairs, _ = rows_ref.shape
    feats, batch, hidden = stack.shape
    cold_feats = cold_ref.shape[0]
    bag = band_ref.shape[0] // cold_feats
    half = tables * pairs
    fixed = pl.ds(1 + cold_feats, feats - 1 - cold_feats)
    incoming = [
        pltpu.make_async_copy(bottom_ref, stack.at[0], sems.at[0]),
        pltpu.make_async_copy(hot_ref, stack.at[fixed], sems.at[1]),
        pltpu.make_async_copy(high_ref, high, sems.at[2]),
        pltpu.make_async_copy(low_ref, low_part, sems.at[3]),
        pltpu.make_async_copy(pre_ref, pre, sems.at[11]),
        pltpu.make_async_copy(dense_ref, dense, sems.at[12]),
        pltpu.make_async_copy(extra_ref, extra, sems.at[13]),
    ]
    for copy in incoming:
        copy.start()
    low = lane_is_low((pairs, LANES))
    for k in range(tables):
        x = rows_ref[k].astype(F32)
        r = pltpu.roll(x, 64, 1)
        wide[k * pairs : (k + 1) * pairs, :] = jnp.where(low, x, r)
        wide[half + k * pairs : half + (k + 1) * pairs, :] = jnp.where(low, r, x)

    def fetch(i, carry):
        base = pl.multiple_of(i * 128, 8)
        got = [wide[pl.ds(pos_ref[base + u], 1), :] for u in range(128)]
        for u in range(128):
            lookups[pl.ds(base + u, 1), :] = got[u]
        return carry

    lax.fori_loop(0, lookups.shape[0] // 128, fetch, 0)
    band = band_ref[...].astype(F32).T
    side = jnp.where(lane_is_low((batch, LANES)), 0.0, 1.0)
    bands = proj_ref.shape[0]
    bags[3, :, bands:] = jnp.zeros((batch, hidden - bands), BF16)
    for f in range(cold_feats):
        first = jnp.zeros((batch, LANES), F32)
        second = jnp.zeros((batch, LANES), F32)
        for l in range(bag):
            j = f * bag + l
            x = lookups[j * batch : (j + 1) * batch, :]
            b = band[:, j : j + 1] - side
            first += jnp.where(b == 0.0, x, 0.0)
            second += jnp.where(b == 2.0, x, 0.0)
        pooled = jnp.concatenate([first, second], axis=1).astype(BF16)
        bags[f // 2, :, f % 2 * bands : (f % 2 + 1) * bands] = pooled
        stack[1 + f] = dot(pooled, proj_ref[...]).astype(BF16)
    outgoing = pltpu.make_async_copy(stack.at[pl.ds(1, cold_feats)], cold_ref, sems.at[4])
    outgoing.start()
    for copy in incoming:
        copy.wait()
    for g in range(batch // 16):
        at = slice(g * 16, (g + 1) * 16)
        x = stack[:, at, :].reshape(feats * 16, hidden)
        first = high[:, at, :].reshape(feats * 16, feats * 16)
        rest = low_part[:, at, :].reshape(feats * 16, feats * 16)
        d = (dot(first, x) + dot(rest, x)).astype(BF16)
        d_stack[:, at, :] = d.reshape(feats, 16, hidden)
    d_pre[...] = (d_stack[0].astype(F32) * silu_slope(pre[...])).astype(BF16)

    def factors(hot_to, rest_to):
        pieces = [
            (d_stack.at[fixed], hot_to.at[pl.ds(0, 8)]),
            (extra, hot_to.at[pl.ds(8, 5)]),
            (d_stack.at[pl.ds(1, cold_feats)], rest_to.at[pl.ds(0, 7)]),
            (bags, rest_to.at[pl.ds(7, 4)]),
            (dense, rest_to.at[11]),
            (d_pre, rest_to.at[12]),
        ]
        return [pltpu.make_async_copy(*p, sems.at[5 + i]) for i, p in enumerate(pieces)]

    first_core = place_ref[1] == 0

    @pl.when(first_core)
    def _():
        for copy in factors(keep_ref, give_ref):
            copy.start()

    @pl.when(jnp.logical_not(first_core))
    def _():
        for copy in factors(give_ref, keep_ref):
            copy.start()

    low = lane_is_low((batch, LANES))
    for f in range(cold_feats):
        d_pool = dot(d_stack[1 + f], proj_ref[...], NT).astype(BF16).astype(F32)
        first, second = d_pool[:, :LANES], d_pool[:, LANES:]
        first_r, second_r = pltpu.roll(first, 64, 1), pltpu.roll(second, 64, 1)
        each = [
            jnp.where(low, first, first_r),
            jnp.where(low, first_r, first),
            jnp.where(low, second, second_r),
            jnp.where(low, second_r, second),
        ]
        for l in range(bag):
            j = f * bag + l
            b = jnp.broadcast_to(band[:, j : j + 1], (batch, LANES))
            x = jnp.where(b < 0.5, each[0], each[1])
            y = jnp.where(b < 2.5, each[2], each[3])
            lookups[j * batch : (j + 1) * batch, :] = jnp.where(b < 1.5, x, y)
            share = wide.shape[0] // (cold_feats * bag)
            wide[j * share : (j + 1) * share, :] = jnp.zeros((share, LANES), F32)

    def place(i, carry):
        base = pl.multiple_of(i * 128, 8)
        got = [lookups[pl.ds(base + u, 1), :] for u in range(128)]
        for u in range(128):
            wide[pl.ds(pos_ref[base + u], 1), :] = got[u]
        return carry

    lax.fori_loop(0, lookups.shape[0] // 128, place, 0)
    low = lane_is_low((pairs, LANES))
    for k in range(tables):
        a = wide[k * pairs : (k + 1) * pairs, :]
        b = wide[half + k * pairs : half + (k + 1) * pairs, :]
        slots_ref[k] = jnp.where(low, a, b).astype(BF16)
    outgoing.wait()

    @pl.when(first_core)
    def _():
        for copy in factors(keep_ref, give_ref):
            copy.wait()

    @pl.when(jnp.logical_not(first_core))
    def _():
        for copy in factors(give_ref, keep_ref):
            copy.wait()


def dense_part_kernel(place_ref, keep_ref, took_ref, own_ref, up_ref, far_ref, down_ref, sums):
    cuts, rows, _ = sums.shape
    batch, hidden = keep_ref.shape[1:]

    def put(make):
        for c in range(cuts):
            sums[(c - place_ref[0] + cuts) % cuts] = make(slice(c * LANES, (c + 1) * LANES))

    @pl.when(place_ref[1] == 0)
    def _():
        picks, parts = [], []
        for ref in (keep_ref, took_ref):
            d_hot = ref[:8].reshape(8 * batch, hidden)
            counts = [jnp.concatenate([ref[8 + u], ref[10 + u]], axis=1) for u in range(2)]
            parts.append(dot(jnp.concatenate(counts, axis=0), d_hot))
            line = ref[12][:16].astype(F32)[:1]
            line = line[:, : hidden // 2] * 32.0 + line[:, hidden // 2 :]
            at = iota((rows, hidden // 2), 0).astype(F32)
            picks.append(jnp.where(at == line, 1.0, 0.0).astype(BF16))
        picks = jnp.concatenate(picks, axis=1)
        high, rest = split_two(jnp.concatenate(parts, axis=0))
        hot = dot(picks, high) + dot(picks, rest)
        put(lambda at: hot[:, at])

    @pl.when(place_ref[1] != 0)
    def _():
        both = (keep_ref, took_ref)
        dense = jnp.concatenate([ref[11] for ref in both], axis=0)
        d_pre = jnp.concatenate([ref[12] for ref in both], axis=0)
        bottom = dot(dense, d_pre, TN)
        half = hidden // 2
        proj = jnp.zeros((half, hidden), F32)
        for ref in both:
            bags = [ref[7 + f // 2][:, f % 2 * half : (f % 2 + 1) * half] for f in range(7)]
            d_cold = ref[:7].reshape(7 * batch, hidden)
            proj += dot(jnp.concatenate(bags, axis=0), d_cold, TN)
        tables = rows // 32
        put(
            lambda at: jnp.concatenate(
                [
                    bottom[:, at].reshape(tables, 16, LANES),
                    proj[:, at].reshape(tables, 8, LANES),
                    jnp.zeros((tables, 8, LANES), F32),
                ],
                axis=1,
            ).reshape(rows, LANES)
        )

    own_ref[...] = sums[0]
    for k, out_ref in enumerate((up_ref, far_ref, down_ref)):
        out_ref[...] = sums[k + 1].astype(BF16)


def inter_kernel(bottom_ref, cold_ref, hot_ref, inter_ref, stack, grams):
    feats, batch, hidden = stack.shape
    cold_feats = cold_ref.shape[0]
    stack[0] = bottom_ref[...]
    for f in range(cold_feats):
        stack[1 + f] = cold_ref[f]
    for h in range(hot_ref.shape[0]):
        stack[1 + cold_feats + h] = hot_ref[h]
    square = feats * feats
    same = iota((square, square), 0) % feats == iota((square, square), 1) % feats
    for g in range(batch // 16):
        at = slice(g * 16, (g + 1) * 16)
        x = stack[:, at, :].reshape(feats * 16, hidden)
        grams[:, at, :] = jnp.where(same, dot(x, x, NT), 0.0).reshape(feats, 16, square)
    total = jnp.zeros((batch, square), F32)
    other = iota((square, square), 0) // feats
    to = iota((square, square), 1)
    for f in range(feats):
        pick = jnp.where(to == f * feats + other, 1.0, 0.0).astype(BF16)
        high, rest = split_two(grams[f])
        total += dot(high, pick) + dot(rest, pick)
    inter_ref[...] = total


def add_kernel(
    place_ref,
    ids_ref,
    vec_ref,
    rows_ref,
    given_far_ref,
    given_near_ref,
    given_own_ref,
    kept_far_ref,
    kept_near_ref,
    kept_own_ref,
    val_a,
    val_b,
    given,
    kept,
    kept_own,
    sems,
    *sums,
):
    tables, pairs, _ = rows_ref.shape
    upper = (vec_ref[...] >> 14).astype(F32).T
    low = lane_is_low((pairs, LANES))
    side = jnp.where(low, 0.0, 1.0)
    for k in range(tables):
        x = rows_ref[k].astype(F32)
        r = pltpu.roll(x, 64, 1)
        share = sums[0].shape[0] // tables
        for part in sums:
            part[k * share : (k + 1) * share, :] = jnp.zeros((share, LANES), F32)
        at = slice(k * pairs, (k + 1) * pairs)
        up_a, up_b = upper[:pairs, k : k + 1], upper[LANES : LANES + pairs, k : k + 1]
        val_a[at, :] = jnp.where(up_a == side, jnp.where(low, x, r), 0.0)
        val_b[at, :] = jnp.where(up_b == side, jnp.where(low, r, x), 0.0)
    sides = ((0, val_a, sums[0]), (LANES, val_b, sums[1]))
    step = pairs // 2

    def spread(part, source):
        first = source * (2 * LANES) + part * step
        base = pl.multiple_of(source * pairs + part * step, 8)
        for q in range(0, step, 4):
            work = [
                (to, ids_ref[first + lane + q + t], val[pl.ds(base + q + t, 1), :])
                for lane, val, to in sides
                for t in range(4)
            ]
            new = [to[pl.ds(row, 1), :] + value for to, row, value in work]
            for (to, row, _), value in zip(work, new):
                to[pl.ds(row, 1), :] = value
        return source

    def one_by_one(group, source):
        first = source * (2 * LANES) + group * 8
        base = pl.multiple_of(source * pairs + group * 8, 8)
        for u in range(8):
            for lane, val, to in sides:
                row = ids_ref[first + lane + u]
                to[pl.ds(row, 1), :] = to[pl.ds(row, 1), :] + val[pl.ds(base + u, 1), :]
        return source

    def per_source(source, carry):
        twice = ids_ref[source * (2 * LANES) + pairs]

        @pl.when(twice == 0)
        def _():
            lax.fori_loop(0, 2, spread, source)

        @pl.when(twice != 0)
        def _():
            lax.fori_loop(0, pairs // 8, one_by_one, source)

        return carry

    lax.fori_loop(0, tables, per_source, 0)
    core = place_ref[1]
    half = kept_own.shape[1]
    size = 2 * half

    def total(k, h, of):
        chunk = 2 * ((place_ref[0] + k) % 4) + of
        at = pl.ds(pl.multiple_of(chunk * size + h * half, half), half)
        return functools.reduce(jnp.add, [part[at, :] for part in sums])

    copies = []

    def send(source, target):
        copies.append(pltpu.make_async_copy(source, target, sems.at[len(copies)]))
        copies[-1].start()

    for k, target in enumerate((given_far_ref, given_near_ref, given_near_ref, given_own_ref)):
        for h in range(2):
            given[k, h] = total((2, 1, 3, 0)[k], h, 1 - core).astype(BF16)
        send(given.at[k], target.at[k - 1] if k in (1, 2) else target)
    for k, target in enumerate((kept_far_ref, kept_near_ref, kept_near_ref)):
        for h in range(2):
            kept[k, h] = total((2, 1, 3)[k], h, core).astype(BF16)
        send(kept.at[k], target.at[k - 1] if k else target)
    for h in range(2):
        kept_own[h] = total(0, h, core)
    send(kept_own, kept_own_ref)
    for copy in copies:
        copy.wait()


def sum_rows(rows_ref):
    total = rows_ref[0].astype(F32)
    for k in range(1, rows_ref.shape[0]):
        total += rows_ref[k].astype(F32)
    return total


def dense_kernel(rows_ref, out_ref):
    rows = rows_ref.shape[1]
    out_ref[:rows], out_ref[rows:] = split_two(sum_rows(rows_ref))


def add_pair(kept, taken):
    return (kept.astype(F32) + taken.astype(F32)).astype(BF16)


def far_kernel(place_ref, kept_ref, taken_ref, mine_ref, theirs_ref, up_ref, down_ref):
    half = kept_ref.shape[1]
    rows = mine_ref.shape[0]
    first = place_ref[1] == 0
    mine, theirs = mine_ref[...].astype(F32), theirs_ref[...].astype(F32)
    low = jnp.where(first, mine, theirs).astype(BF16)
    high = jnp.where(first, theirs, mine).astype(BF16)
    for h, out_ref in enumerate((up_ref, down_ref)):
        out_ref[:half] = add_pair(kept_ref[h], taken_ref[h])
        out_ref[half : half + rows] = low
        out_ref[half + rows :] = high


def second_kernel(kept_ref, taken_ref, below_ref, above_ref, up_ref, down_ref):
    half = kept_ref.shape[2]

    def total(k, h, far):
        return (
            kept_ref[k, h].astype(F32) + taken_ref[k, h].astype(F32) + far.astype(F32)
        ).astype(BF16)

    up_ref[:half] = total(0, 0, below_ref[:half])
    up_ref[half : 2 * half] = add_pair(kept_ref[0, 1], taken_ref[0, 1])
    up_ref[2 * half :] = below_ref[half:]
    down_ref[:half] = add_pair(kept_ref[1, 0], taken_ref[1, 0])
    down_ref[half:] = total(1, 1, above_ref[:half])


def own_kernel(kept_ref, taken_ref, out_ref):
    out_ref[...] = kept_ref[...] + taken_ref[...].astype(F32)


def last_kernel(
    place_ref,
    pair_ref,
    below_ref,
    above_ref,
    own_ref,
    next_ref,
    before_ref,
    out_ref,
    hot_ref,
    proj_ref,
    bottom_ref,
):
    half = pair_ref.shape[1]

    def total(h):
        at = slice(h * half, (h + 1) * half)
        return pair_ref[h] + below_ref[at].astype(F32) + above_ref[at].astype(F32)

    wide = jnp.concatenate([total(0), total(1)], axis=0).T
    out_ref[...] = jnp.concatenate([wide[:64], wide[64:]], axis=1)
    tails = (own_ref[half:], next_ref[half:], below_ref[2 * half :], before_ref[half:])
    for k, tail in enumerate(tails):
        chunk = (place_ref[0] + k) % len(tails)
        at = pl.ds(pl.multiple_of(chunk * LANES, LANES), LANES)
        rows = tail.astype(F32)
        hot_ref[:, at] = rows[:32] + rows[32:64]
        rest = rows[64:96] + rows[96:]
        bottom_ref[:, at] = rest[:16]
        proj_ref[:, at] = rest[16:24]


def to_other_core(x):
    return lax.ppermute(x, "dp", [(i, i ^ 1) for i in range(8)])


def along_x(x, steps):
    return lax.ppermute(x, "dp", [(i, (i + 2 * steps) % 8) for i in range(8)])


def exchange(x, axis):
    return lax.all_to_all(x, axis, split_axis=0, concat_axis=0, tiled=True)


def shards(
    dense_input,
    bottom_weight,
    cold_table,
    projection,
    hot_table,
    cold_owner,
    cold_local,
    cold_band,
    hot_unique,
    hot_map,
    grad_inter,
):
    batch, hidden = dense_input.shape
    cold_feats, bag = cold_local.shape[1], cold_local.shape[2]
    hot_feats = hot_map.shape[1]
    feats = 1 + cold_feats + hot_feats
    tables = lax.axis_size("table")
    rows_dev, width = cold_table.shape
    unique = hot_unique.shape[0]
    lookups = batch * cold_feats * bag
    slots = 2 * lookups // tables
    pairs = slots // 2
    bands = projection.shape[0]
    at_dp = lax.axis_index("dp").astype(jnp.int32)
    place = jnp.stack([at_dp // 2, at_dp % 2])

    def by_sample(v):
        return jnp.transpose(v.reshape(batch, cold_feats, bag), (1, 2, 0))

    shape = jax.ShapeDtypeStruct
    ids, pos = call(
        functools.partial(prep_kernel, tables, pairs),
        (shape((tables, 1, 2 * LANES), jnp.int32), shape((cold_feats * bag, batch), jnp.int32)),
    )(by_sample(cold_owner), by_sample(cold_local))
    pos = pos.reshape(lookups)
    asked = exchange(ids, "table").reshape(tables, 2 * LANES)
    row_ids = (asked & (rows_dev // 2 - 1)).reshape(tables * 2 * LANES)
    fetched = call(
        gather_kernel,
        shape((tables, pairs, LANES), BF16),
        scratch=[pltpu.VMEM((rows_dev // 2, LANES), F32)]
        + [pltpu.VMEM((tables * pairs, LANES), F32)] * 2,
        specs=[SMEM, VMEM, VMEM],
        us=12,
        vmem=24,
    )(row_ids, asked, cold_table.T)
    received = exchange(fetched, "table")
    pre, bottom, hot_emb, extra, high, low = call(
        front_kernel,
        (
            shape((batch, hidden), F32),
            shape((batch, hidden), BF16),
            shape((hot_feats, batch, hidden), BF16),
            shape((5, batch, hidden), BF16),
            shape((feats, batch, feats * feats), BF16),
            shape((feats, batch, feats * feats), BF16),
        ),
        us=3,
    )(
        dense_input,
        bottom_weight,
        hot_table,
        hot_unique.reshape(unique, 1),
        hot_unique.reshape(1, unique),
        jnp.transpose(hot_map, (1, 2, 0)),
        grad_inter,
    )
    received, high, low = lax.optimization_barrier((received, high, low))
    cuts = hidden // LANES
    slot_grads, cold_emb, keep, give = call(
        main_kernel,
        (
            shape((tables, pairs, LANES), BF16),
            shape((cold_feats, batch, hidden), BF16),
            shape((13, batch, hidden), BF16),
            shape((13, batch, hidden), BF16),
        ),
        scratch=[
            pltpu.VMEM((2 * tables * pairs, LANES), F32),
            pltpu.VMEM((lookups, LANES), F32),
            pltpu.VMEM((feats, batch, hidden), BF16),
            pltpu.VMEM((feats, batch, feats * feats), BF16),
            pltpu.VMEM((feats, batch, feats * feats), BF16),
            pltpu.VMEM((feats, batch, hidden), BF16),
            pltpu.VMEM((4, batch, hidden), BF16),
            pltpu.VMEM((batch, hidden), F32),
            pltpu.VMEM((batch, hidden), BF16),
            pltpu.VMEM((batch, hidden), BF16),
            pltpu.VMEM((5, batch, hidden), BF16),
            pltpu.SemaphoreType.DMA((14,)),
        ],
        specs=[SMEM] * 2 + [VMEM] * 3 + [HBM] * 7,
        out_specs=[VMEM, HBM, HBM, HBM],
        us=14,
        vmem=63,
    )(
        place,
        pos,
        received,
        by_sample(cold_band).reshape(cold_feats * bag, batch),
        projection,
        pre,
        dense_input,
        extra,
        bottom,
        hot_emb,
        high,
        low,
    )
    returned = exchange(slot_grads, "table")
    took = to_other_core(give)
    dense_row, dense_up, dense_far, dense_down = call(
        dense_part_kernel,
        (shape((tables * 32, LANES), F32),) + (shape((tables * 32, LANES), BF16),) * 3,
        scratch=[pltpu.VMEM((cuts, tables * 32, LANES), F32)],
        specs=[SMEM, VMEM, VMEM],
        us=4,
        vmem=32,
    )(place, keep, took)
    for part, steps in ((dense_up, 1), (dense_far, 2), (dense_down, -1)):
        dense_row += along_x(part, steps).astype(F32)
    dense_row = dense_row.astype(BF16).reshape(tables, 32, LANES)
    returned, dense_row = lax.optimization_barrier((returned, dense_row))
    dense_all = exchange(dense_row, "table")

    half = rows_dev // 32
    given_far, given_near, given_own, kept_far, kept_near, kept_own = call(
        add_kernel,
        (
            shape((2, half, LANES), BF16),
            shape((2, 2, half, LANES), BF16),
            shape((2, half, LANES), BF16),
            shape((2, half, LANES), BF16),
            shape((2, 2, half, LANES), BF16),
            shape((2, half, LANES), F32),
        ),
        scratch=[pltpu.VMEM((tables * pairs, LANES), F32)] * 2
        + [
            pltpu.VMEM((4, 2, half, LANES), BF16),
            pltpu.VMEM((3, 2, half, LANES), BF16),
            pltpu.VMEM((2, half, LANES), F32),
            pltpu.SemaphoreType.DMA((8,)),
        ]
        + [pltpu.VMEM((rows_dev // 2, LANES), F32)] * 2,
        specs=[SMEM, SMEM, VMEM, VMEM],
        out_specs=[HBM] * 6,
        us=20,
        vmem=62,
    )(place, row_ids, asked, returned)
    given_far, dense_all = lax.optimization_barrier((given_far, dense_all))
    mine = call(dense_kernel, shape((64, LANES), BF16))(dense_all)
    taken_far = to_other_core(given_far)
    theirs = to_other_core(mine)
    up, down = call(far_kernel, (shape((half + 128, LANES), BF16),) * 2, specs=[SMEM] + [VMEM] * 4)(
        place, kept_far, taken_far, mine, theirs
    )
    from_below = along_x(up, 1)
    from_above = along_x(down, -1)
    up, down, cold_emb, given_near, given_own = lax.optimization_barrier(
        (up, down, cold_emb, given_near, given_own)
    )
    taken_near = to_other_core(given_near)
    taken_own = to_other_core(given_own)
    inter = call(
        inter_kernel,
        shape((batch, feats * feats), F32),
        scratch=[
            pltpu.VMEM((feats, batch, hidden), BF16),
            pltpu.VMEM((feats, batch, feats * feats), F32),
        ],
        us=4,
    )(bottom, cold_emb, hot_emb)
    from_below, from_above, taken_near, taken_own, inter = lax.optimization_barrier(
        (from_below, from_above, taken_near, taken_own, inter)
    )
    next_up, next_down = call(
        second_kernel,
        (shape((2 * half + 128, LANES), BF16), shape((2 * half, LANES), BF16)),
    )(kept_near, taken_near, from_below, from_above)
    next_up, next_down, kept_own, taken_own = lax.optimization_barrier(
        (next_up, next_down, kept_own, taken_own)
    )
    pair_own = call(own_kernel, shape((2, half, LANES), F32), us=2)(kept_own, taken_own)
    next_below = along_x(next_up, 1)
    next_above = along_x(next_down, -1)
    cold_grad, hot_grad, projection_grad, bottom_grad = call(
        last_kernel,
        (
            shape((width, rows_dev // 8), F32),
            shape((32, hidden), F32),
            shape((8, hidden), F32),
            shape((16, hidden), F32),
        ),
        specs=[SMEM] + [VMEM] * 6,
        us=2,
    )(place, pair_own, next_below, next_above, up, from_above, from_below)
    return inter, cold_grad.T, hot_grad, projection_grad, bottom_grad


def solution(mesh):
    placed = (
        P(("table", "dp"), None),
        P(),
        P("table", None),
        P(),
        P(),
        P(("table", "dp"), None, None, None),
        P(("table", "dp"), None, None),
        P(("table", "dp"), None, None),
        P(("table", "dp")),
        P(("table", "dp"), None, None),
        P(("table", "dp"), None),
    )
    return jax.shard_map(
        shards,
        mesh=mesh,
        in_specs=placed,
        out_specs=(
            P(("table", "dp"), None),
            P(("table", "dp"), None),
            P("table", None),
            P("table", None),
            P("table", None),
        ),
        check_vma=False,
    )
```

```python
import functools

import jax
import jax.numpy as jnp
from jax import lax
from jax.experimental import pallas as pl
from jax.experimental.pallas import tpu as pltpu
from jax.sharding import PartitionSpec as P

F32 = jnp.float32
BF16 = jnp.bfloat16
LANES = 128
NT = (((1,), (1,)), ((), ()))
TN = (((0,), (0,)), ((), ()))
MIB = 1 << 20


def dot(a, b, dims=(((1,), (0,)), ((), ()))):
    return lax.dot_general(a, b, dims, preferred_element_type=F32)


def split_two(v):
    high = v.astype(BF16)
    return high, (v - high.astype(F32)).astype(BF16)


def iota(shape, dim):
    return lax.broadcasted_iota(jnp.int32, shape, dim)


def call(kernel, outs, scratch=(), specs=None, vmem=16, us=1, grid=None, out_specs=None):
    args = {} if specs is None else {"in_specs": specs}
    if grid is not None:
        args["grid"] = grid
    if out_specs is not None:
        args["out_specs"] = out_specs
    return pl.pallas_call(
        kernel,
        out_shape=outs,
        scratch_shapes=list(scratch),
        compiler_params=pltpu.CompilerParams(vmem_limit_bytes=vmem * MIB),
        cost_estimate=pl.CostEstimate(
            flops=us * 1_100_000_000, bytes_accessed=MIB, transcendentals=0
        ),
        **args,
    )


SMEM = pl.BlockSpec(memory_space=pltpu.SMEM)
VMEM = pl.BlockSpec(memory_space=pltpu.VMEM)
HBM = pl.BlockSpec(memory_space=pltpu.HBM)


def prep_kernel(tables, pairs, owner_ref, local_ref, ids_ref, pos_ref):
    bag = owner_ref.shape[1]
    steps = owner_ref.shape[0] * bag
    owners = [owner_ref[j // bag, j % bag : j % bag + 1, :] for j in range(steps)]
    row, col = iota((LANES, 2 * LANES), 0), iota((LANES, 2 * LANES), 1)
    tri = jnp.where((row < col) | (col >= LANES), 1.0, 0.0).astype(BF16)
    table_row = iota((tables, LANES), 0)
    slot_row = iota((2 * LANES, LANES), 0)
    hits = [
        jnp.where(owner == table_row, 1.0, 0.0) for owner in owners
    ]
    sums = dot(jnp.concatenate(hits, axis=0).astype(BF16), tri)
    carry = jnp.zeros((tables, LANES), F32)
    left, right = [], []
    for j in range(steps):
        part = sums[j * tables : (j + 1) * tables]
        slot = jnp.sum(hits[j] * (part[:, :LANES] + carry), axis=0, keepdims=True)
        slot = slot.astype(jnp.int32)
        carry = carry + part[:, LANES:]
        upper = jnp.where(slot >= pairs, 1, 0)
        pos_ref[j : j + 1, :] = (
            upper * (tables * pairs - pairs) + owners[j] * pairs + slot
        )
        local = local_ref[j // bag, j % bag : j % bag + 1, :]
        code = (((local >> 11) & 1) << 14) | ((local >> 12) << 11) | (local & 2047)
        high, low = (code >> 8).astype(F32), (code & 255).astype(F32)
        left.append(
            jnp.concatenate([hits[j] * high, hits[j] * low, hits[j]], axis=0).astype(BF16)
        )
        right.append(jnp.where(slot + upper * (LANES - pairs) == slot_row, 1.0, 0.0).astype(BF16))
    placed = dot(jnp.concatenate(left, axis=1), jnp.concatenate(right, axis=1), NT)
    ids = (placed[:tables] * 256.0 + placed[tables : 2 * tables]).astype(jnp.int32)
    ids = jnp.where(placed[2 * tables :] > 0.5, ids, iota(ids.shape, 0) * 256 + iota(ids.shape, 1))
    lane = iota(ids.shape, 1)
    rows = ids & 16383
    twice = jnp.zeros(ids.shape, F32)
    for d in range(1, 4):
        met = (rows == pltpu.roll(rows, d, 1)) & (lane % 4 >= d) & (lane % LANES < pairs)
        twice = jnp.where(met, 1.0, twice)
    twice = jnp.max(twice, axis=1, keepdims=True).astype(jnp.int32)
    ids = jnp.where(lane == pairs, twice, ids)
    for k in range(tables):
        ids_ref[k] = ids[k : k + 1]


def lane_is_low(shape):
    return iota(shape, len(shape) - 1) < 64


def gather_kernel(ids_ref, vec_ref, table_ref, out_ref, packed, got_a, got_b):
    tables, pairs, _ = out_ref.shape
    size = 2048
    for c in range(packed.shape[0] // size):
        first = table_ref[:, 2 * c * size : (2 * c + 1) * size]
        second = table_ref[:, (2 * c + 1) * size : (2 * c + 2) * size]
        both = jnp.concatenate([first, second], axis=0)
        packed[c * size : (c + 1) * size, :] = both.astype(F32).T
    step = pairs // 2

    def one(part, source):
        first = source * (2 * LANES) + part * step
        base = pl.multiple_of(source * pairs + part * step, 8)
        read_a = [packed[pl.ds(ids_ref[first + u], 1), :] for u in range(step)]
        read_b = [packed[pl.ds(ids_ref[first + LANES + u], 1), :] for u in range(step)]
        for u in range(step):
            got_a[pl.ds(base + u, 1), :] = read_a[u]
            got_b[pl.ds(base + u, 1), :] = read_b[u]
        return source

    def per_source(source, carry):
        lax.fori_loop(0, 2, one, source)
        return carry

    lax.fori_loop(0, tables, per_source, 0)
    upper = (vec_ref[...] >> 14).astype(F32).T
    low = lane_is_low((pairs, LANES))
    for k in range(tables):
        a = got_a[k * pairs : (k + 1) * pairs, :]
        b = got_b[k * pairs : (k + 1) * pairs, :]
        up_a = upper[:pairs, k : k + 1] > 0.5
        up_b = upper[LANES : LANES + pairs, k : k + 1] > 0.5
        a = jnp.where(up_a, pltpu.roll(a, 64, 1), a)
        b = jnp.where(up_b, b, pltpu.roll(b, 64, 1))
        out_ref[k] = jnp.where(low, a, b).astype(BF16)


def front_kernel(
    dense_ref,
    weight_ref,
    hot_ref,
    unique_ref,
    line_ref,
    map_ref,
    grad_ref,
    pre_ref,
    bottom_ref,
    emb_ref,
    extra_ref,
    high_ref,
    low_ref,
):
    batch = dense_ref.shape[0]
    hot_feats, bag = map_ref.shape[0], map_ref.shape[1]
    unique = unique_ref.shape[0]
    feats = high_ref.shape[0]
    pre = dot(dense_ref[...], weight_ref[...])
    pre_ref[...] = pre
    bottom_ref[...] = jax.nn.silu(pre).astype(BF16)
    picks = jnp.where(unique_ref[...] == iota((unique, hot_ref.shape[0]), 1), 1.0, 0.0)
    rows = dot(picks.astype(BF16), hot_ref[...]).astype(BF16)
    place = iota((unique, batch), 0)
    for h in range(hot_feats):
        count = jnp.zeros((unique, batch), F32)
        for l in range(bag):
            count += jnp.where(map_ref[h, l : l + 1, :] == place, 1.0, 0.0)
        at = slice(h % 4 * batch, (h % 4 + 1) * batch)
        extra_ref[h // 4 * 2, :, at] = count[:batch].astype(BF16)
        extra_ref[h // 4 * 2 + 1, :, at] = count[batch:].astype(BF16)
        emb_ref[h] = dot(count.T.astype(BF16), rows).astype(BF16)
    line = line_ref[...]
    line = jnp.concatenate([line >> 5, line & 31], axis=1).astype(F32)
    extra_ref[4] = jnp.broadcast_to(line, extra_ref.shape[1:]).astype(BF16)
    grad = grad_ref[...]
    grad_high, grad_low = split_two(grad)
    square = feats * feats
    at = iota((square, square), 0)
    other = iota((square, square), 1) // feats
    same = iota((batch, square), 0) % feats == iota((batch, square), 1) % feats
    for f in range(feats):
        pick = jnp.where(at == f * feats + other, 1.0, 0.0) + jnp.where(
            at == other * feats + f, 1.0, 0.0
        )
        pick = pick.astype(BF16)
        spread = jnp.where(same, dot(grad_high, pick) + dot(grad_low, pick), 0.0)
        high_ref[f], low_ref[f] = split_two(spread)


def silu_slope(pre):
    sigma = jax.nn.sigmoid(pre)
    return sigma * (1.0 + pre * (1.0 - sigma))


def main_kernel(
    place_ref,
    pos_ref,
    rows_ref,
    band_ref,
    proj_ref,
    pre_ref,
    dense_ref,
    extra_ref,
    bottom_ref,
    hot_ref,
    high_ref,
    low_ref,
    slots_ref,
    cold_ref,
    keep_ref,
    give_ref,
    wide,
    lookups,
    stack,
    high,
    low_part,
    d_stack,
    bags,
    pre,
    d_pre,
    dense,
    extra,
    sems,
):
    tables, pairs, _ = rows_ref.shape
    feats, batch, hidden = stack.shape
    cold_feats = cold_ref.shape[0]
    bag = band_ref.shape[0] // cold_feats
    half = tables * pairs
    fixed = pl.ds(1 + cold_feats, feats - 1 - cold_feats)
    incoming = [
        pltpu.make_async_copy(bottom_ref, stack.at[0], sems.at[0]),
        pltpu.make_async_copy(hot_ref, stack.at[fixed], sems.at[1]),
        pltpu.make_async_copy(high_ref, high, sems.at[2]),
        pltpu.make_async_copy(low_ref, low_part, sems.at[3]),
        pltpu.make_async_copy(pre_ref, pre, sems.at[11]),
        pltpu.make_async_copy(dense_ref, dense, sems.at[12]),
        pltpu.make_async_copy(extra_ref, extra, sems.at[13]),
    ]
    for copy in incoming:
        copy.start()
    low = lane_is_low((pairs, LANES))
    for k in range(tables):
        x = rows_ref[k].astype(F32)
        r = pltpu.roll(x, 64, 1)
        wide[k * pairs : (k + 1) * pairs, :] = jnp.where(low, x, r)
        wide[half + k * pairs : half + (k + 1) * pairs, :] = jnp.where(low, r, x)

    def fetch(i, carry):
        base = pl.multiple_of(i * 128, 8)
        got = [wide[pl.ds(pos_ref[base + u], 1), :] for u in range(128)]
        for u in range(128):
            lookups[pl.ds(base + u, 1), :] = got[u]
        return carry

    lax.fori_loop(0, lookups.shape[0] // 128, fetch, 0)
    band = band_ref[...].astype(F32).T
    side = jnp.where(lane_is_low((batch, LANES)), 0.0, 1.0)
    bands = proj_ref.shape[0]
    bags[3, :, bands:] = jnp.zeros((batch, hidden - bands), BF16)
    for f in range(cold_feats):
        first = jnp.zeros((batch, LANES), F32)
        second = jnp.zeros((batch, LANES), F32)
        for l in range(bag):
            j = f * bag + l
            x = lookups[j * batch : (j + 1) * batch, :]
            b = band[:, j : j + 1] - side
            first += jnp.where(b == 0.0, x, 0.0)
            second += jnp.where(b == 2.0, x, 0.0)
        pooled = jnp.concatenate([first, second], axis=1).astype(BF16)
        bags[f // 2, :, f % 2 * bands : (f % 2 + 1) * bands] = pooled
        stack[1 + f] = dot(pooled, proj_ref[...]).astype(BF16)
    outgoing = pltpu.make_async_copy(stack.at[pl.ds(1, cold_feats)], cold_ref, sems.at[4])
    outgoing.start()
    for copy in incoming:
        copy.wait()
    for g in range(batch // 16):
        at = slice(g * 16, (g + 1) * 16)
        x = stack[:, at, :].reshape(feats * 16, hidden)
        first = high[:, at, :].reshape(feats * 16, feats * 16)
        rest = low_part[:, at, :].reshape(feats * 16, feats * 16)
        d = (dot(first, x) + dot(rest, x)).astype(BF16)
        d_stack[:, at, :] = d.reshape(feats, 16, hidden)
    d_pre[...] = (d_stack[0].astype(F32) * silu_slope(pre[...])).astype(BF16)

    def factors(hot_to, rest_to):
        pieces = [
            (d_stack.at[fixed], hot_to.at[pl.ds(0, 8)]),
            (extra, hot_to.at[pl.ds(8, 5)]),
            (d_stack.at[pl.ds(1, cold_feats)], rest_to.at[pl.ds(0, 7)]),
            (bags, rest_to.at[pl.ds(7, 4)]),
            (dense, rest_to.at[11]),
            (d_pre, rest_to.at[12]),
        ]
        return [pltpu.make_async_copy(*p, sems.at[5 + i]) for i, p in enumerate(pieces)]

    first_core = place_ref[1] == 0

    @pl.when(first_core)
    def _():
        for copy in factors(keep_ref, give_ref):
            copy.start()

    @pl.when(jnp.logical_not(first_core))
    def _():
        for copy in factors(give_ref, keep_ref):
            copy.start()

    low = lane_is_low((batch, LANES))
    for f in range(cold_feats):
        d_pool = dot(d_stack[1 + f], proj_ref[...], NT).astype(BF16).astype(F32)
        first, second = d_pool[:, :LANES], d_pool[:, LANES:]
        first_r, second_r = pltpu.roll(first, 64, 1), pltpu.roll(second, 64, 1)
        each = [
            jnp.where(low, first, first_r),
            jnp.where(low, first_r, first),
            jnp.where(low, second, second_r),
            jnp.where(low, second_r, second),
        ]
        for l in range(bag):
            j = f * bag + l
            b = jnp.broadcast_to(band[:, j : j + 1], (batch, LANES))
            x = jnp.where(b < 0.5, each[0], each[1])
            y = jnp.where(b < 2.5, each[2], each[3])
            lookups[j * batch : (j + 1) * batch, :] = jnp.where(b < 1.5, x, y)
            share = wide.shape[0] // (cold_feats * bag)
            wide[j * share : (j + 1) * share, :] = jnp.zeros((share, LANES), F32)

    def place(i, carry):
        base = pl.multiple_of(i * 128, 8)
        got = [lookups[pl.ds(base + u, 1), :] for u in range(128)]
        for u in range(128):
            wide[pl.ds(pos_ref[base + u], 1), :] = got[u]
        return carry

    lax.fori_loop(0, lookups.shape[0] // 128, place, 0)
    low = lane_is_low((pairs, LANES))
    for k in range(tables):
        a = wide[k * pairs : (k + 1) * pairs, :]
        b = wide[half + k * pairs : half + (k + 1) * pairs, :]
        slots_ref[k] = jnp.where(low, a, b).astype(BF16)
    outgoing.wait()

    @pl.when(first_core)
    def _():
        for copy in factors(keep_ref, give_ref):
            copy.wait()

    @pl.when(jnp.logical_not(first_core))
    def _():
        for copy in factors(give_ref, keep_ref):
            copy.wait()


def dense_part_kernel(place_ref, keep_ref, took_ref, own_ref, up_ref, far_ref, down_ref, sums):
    cuts, rows, _ = sums.shape
    batch, hidden = keep_ref.shape[1:]

    def put(make):
        for c in range(cuts):
            sums[(c - place_ref[0] + cuts) % cuts] = make(slice(c * LANES, (c + 1) * LANES))

    @pl.when(place_ref[1] == 0)
    def _():
        picks, parts = [], []
        for ref in (keep_ref, took_ref):
            d_hot = ref[:8].reshape(8 * batch, hidden)
            counts = [jnp.concatenate([ref[8 + u], ref[10 + u]], axis=1) for u in range(2)]
            parts.append(dot(jnp.concatenate(counts, axis=0), d_hot))
            line = ref[12][:16].astype(F32)[:1]
            line = line[:, : hidden // 2] * 32.0 + line[:, hidden // 2 :]
            at = iota((rows, hidden // 2), 0).astype(F32)
            picks.append(jnp.where(at == line, 1.0, 0.0).astype(BF16))
        picks = jnp.concatenate(picks, axis=1)
        high, rest = split_two(jnp.concatenate(parts, axis=0))
        hot = dot(picks, high) + dot(picks, rest)
        put(lambda at: hot[:, at])

    @pl.when(place_ref[1] != 0)
    def _():
        both = (keep_ref, took_ref)
        dense = jnp.concatenate([ref[11] for ref in both], axis=0)
        d_pre = jnp.concatenate([ref[12] for ref in both], axis=0)
        bottom = dot(dense, d_pre, TN)
        half = hidden // 2
        proj = jnp.zeros((half, hidden), F32)
        for ref in both:
            bags = [ref[7 + f // 2][:, f % 2 * half : (f % 2 + 1) * half] for f in range(7)]
            d_cold = ref[:7].reshape(7 * batch, hidden)
            proj += dot(jnp.concatenate(bags, axis=0), d_cold, TN)
        tables = rows // 32
        put(
            lambda at: jnp.concatenate(
                [
                    bottom[:, at].reshape(tables, 16, LANES),
                    proj[:, at].reshape(tables, 8, LANES),
                    jnp.zeros((tables, 8, LANES), F32),
                ],
                axis=1,
            ).reshape(rows, LANES)
        )

    own_ref[...] = sums[0]
    for k, out_ref in enumerate((up_ref, far_ref, down_ref)):
        out_ref[...] = sums[k + 1].astype(BF16)


def inter_kernel(bottom_ref, cold_ref, hot_ref, inter_ref, stack, grams):
    feats, batch, hidden = stack.shape
    cold_feats = cold_ref.shape[0]
    stack[0] = bottom_ref[...]
    for f in range(cold_feats):
        stack[1 + f] = cold_ref[f]
    for h in range(hot_ref.shape[0]):
        stack[1 + cold_feats + h] = hot_ref[h]
    square = feats * feats
    same = iota((square, square), 0) % feats == iota((square, square), 1) % feats
    for g in range(batch // 16):
        at = slice(g * 16, (g + 1) * 16)
        x = stack[:, at, :].reshape(feats * 16, hidden)
        grams[:, at, :] = jnp.where(same, dot(x, x, NT), 0.0).reshape(feats, 16, square)
    total = jnp.zeros((batch, square), F32)
    other = iota((square, square), 0) // feats
    to = iota((square, square), 1)
    for f in range(feats):
        pick = jnp.where(to == f * feats + other, 1.0, 0.0).astype(BF16)
        high, rest = split_two(grams[f])
        total += dot(high, pick) + dot(rest, pick)
    inter_ref[...] = total


def add_kernel(
    place_ref,
    ids_ref,
    vec_ref,
    rows_ref,
    given_far_ref,
    given_near_ref,
    given_own_ref,
    kept_far_ref,
    kept_near_ref,
    kept_own_ref,
    val_a,
    val_b,
    given,
    kept,
    kept_own,
    sems,
    *sums,
):
    tables, pairs, _ = rows_ref.shape
    upper = (vec_ref[...] >> 14).astype(F32).T
    low = lane_is_low((pairs, LANES))
    side = jnp.where(low, 0.0, 1.0)
    for k in range(tables):
        x = rows_ref[k].astype(F32)
        r = pltpu.roll(x, 64, 1)
        share = sums[0].shape[0] // tables
        for part in sums:
            part[k * share : (k + 1) * share, :] = jnp.zeros((share, LANES), F32)
        at = slice(k * pairs, (k + 1) * pairs)
        up_a, up_b = upper[:pairs, k : k + 1], upper[LANES : LANES + pairs, k : k + 1]
        val_a[at, :] = jnp.where(up_a == side, jnp.where(low, x, r), 0.0)
        val_b[at, :] = jnp.where(up_b == side, jnp.where(low, r, x), 0.0)
    sides = ((0, val_a, sums[0]), (LANES, val_b, sums[1]))
    step = pairs // 2

    def spread(part, source):
        first = source * (2 * LANES) + part * step
        base = pl.multiple_of(source * pairs + part * step, 8)
        for q in range(0, step, 4):
            work = [
                (to, ids_ref[first + lane + q + t], val[pl.ds(base + q + t, 1), :])
                for lane, val, to in sides
                for t in range(4)
            ]
            new = [to[pl.ds(row, 1), :] + value for to, row, value in work]
            for (to, row, _), value in zip(work, new):
                to[pl.ds(row, 1), :] = value
        return source

    def one_by_one(group, source):
        first = source * (2 * LANES) + group * 8
        base = pl.multiple_of(source * pairs + group * 8, 8)
        for u in range(8):
            for lane, val, to in sides:
                row = ids_ref[first + lane + u]
                to[pl.ds(row, 1), :] = to[pl.ds(row, 1), :] + val[pl.ds(base + u, 1), :]
        return source

    def per_source(source, carry):
        twice = ids_ref[source * (2 * LANES) + pairs]

        @pl.when(twice == 0)
        def _():
            lax.fori_loop(0, 2, spread, source)

        @pl.when(twice != 0)
        def _():
            lax.fori_loop(0, pairs // 8, one_by_one, source)

        return carry

    lax.fori_loop(0, tables, per_source, 0)
    core = place_ref[1]
    half = kept_own.shape[1]
    size = 2 * half

    def total(k, h, of):
        chunk = 2 * ((place_ref[0] + k) % 4) + of
        at = pl.ds(pl.multiple_of(chunk * size + h * half, half), half)
        return functools.reduce(jnp.add, [part[at, :] for part in sums])

    copies = []

    def send(source, target):
        copies.append(pltpu.make_async_copy(source, target, sems.at[len(copies)]))
        copies[-1].start()

    for k, target in enumerate((given_far_ref, given_near_ref, given_near_ref, given_own_ref)):
        for h in range(2):
            given[k, h] = total((2, 1, 3, 0)[k], h, 1 - core).astype(BF16)
        send(given.at[k], target.at[k - 1] if k in (1, 2) else target)
    for k, target in enumerate((kept_far_ref, kept_near_ref, kept_near_ref)):
        for h in range(2):
            kept[k, h] = total((2, 1, 3)[k], h, core).astype(BF16)
        send(kept.at[k], target.at[k - 1] if k else target)
    for h in range(2):
        kept_own[h] = total(0, h, core)
    send(kept_own, kept_own_ref)
    for copy in copies:
        copy.wait()


def sum_rows(rows_ref):
    total = rows_ref[0].astype(F32)
    for k in range(1, rows_ref.shape[0]):
        total += rows_ref[k].astype(F32)
    return total


def dense_kernel(rows_ref, out_ref):
    out_ref[...] = sum_rows(rows_ref).astype(BF16)


def add_pair(kept, taken):
    return (kept.astype(F32) + taken.astype(F32)).astype(BF16)


def far_kernel(place_ref, kept_ref, taken_ref, mine_ref, theirs_ref, up_ref, down_ref):
    half = kept_ref.shape[1]
    rows = mine_ref.shape[0]
    first = place_ref[1] == 0
    mine, theirs = mine_ref[...].astype(F32), theirs_ref[...].astype(F32)
    low = jnp.where(first, mine, theirs).astype(BF16)
    high = jnp.where(first, theirs, mine).astype(BF16)
    for h, out_ref in enumerate((up_ref, down_ref)):
        out_ref[:half] = add_pair(kept_ref[h], taken_ref[h])
        out_ref[half : half + rows] = low
        out_ref[half + rows :] = high


def second_kernel(kept_ref, taken_ref, below_ref, above_ref, up_ref, down_ref):
    half = kept_ref.shape[2]

    def total(k, h, far):
        return (
            kept_ref[k, h].astype(F32) + taken_ref[k, h].astype(F32) + far.astype(F32)
        ).astype(BF16)

    up_ref[:half] = total(0, 0, below_ref[:half])
    up_ref[half : 2 * half] = add_pair(kept_ref[0, 1], taken_ref[0, 1])
    up_ref[2 * half :] = below_ref[half:]
    down_ref[:half] = add_pair(kept_ref[1, 0], taken_ref[1, 0])
    down_ref[half:] = total(1, 1, above_ref[:half])


def own_kernel(kept_ref, taken_ref, out_ref):
    out_ref[...] = kept_ref[...] + taken_ref[...].astype(F32)


def last_kernel(
    place_ref,
    pair_ref,
    below_ref,
    above_ref,
    own_ref,
    next_ref,
    before_ref,
    out_ref,
    hot_ref,
    proj_ref,
    bottom_ref,
):
    half = pair_ref.shape[1]

    def total(h):
        at = slice(h * half, (h + 1) * half)
        return pair_ref[h] + below_ref[at].astype(F32) + above_ref[at].astype(F32)

    wide = jnp.concatenate([total(0), total(1)], axis=0).T
    out_ref[...] = jnp.concatenate([wide[:64], wide[64:]], axis=1)
    tails = (own_ref[half:], next_ref[half:], below_ref[2 * half :], before_ref[half:])
    for k, tail in enumerate(tails):
        chunk = (place_ref[0] + k) % len(tails)
        at = pl.ds(pl.multiple_of(chunk * LANES, LANES), LANES)
        rows = tail.astype(F32)
        hot_ref[:, at] = rows[:32]
        rest = rows[32:]
        bottom_ref[:, at] = rest[:16]
        proj_ref[:, at] = rest[16:24]


def to_other_core(x):
    return lax.ppermute(x, "dp", [(i, i ^ 1) for i in range(8)])


def along_x(x, steps):
    return lax.ppermute(x, "dp", [(i, (i + 2 * steps) % 8) for i in range(8)])


def exchange(x, axis):
    return lax.all_to_all(x, axis, split_axis=0, concat_axis=0, tiled=True)


def shards(
    dense_input,
    bottom_weight,
    cold_table,
    projection,
    hot_table,
    cold_owner,
    cold_local,
    cold_band,
    hot_unique,
    hot_map,
    grad_inter,
):
    batch, hidden = dense_input.shape
    cold_feats, bag = cold_local.shape[1], cold_local.shape[2]
    hot_feats = hot_map.shape[1]
    feats = 1 + cold_feats + hot_feats
    tables = lax.axis_size("table")
    rows_dev, width = cold_table.shape
    unique = hot_unique.shape[0]
    lookups = batch * cold_feats * bag
    slots = 2 * lookups // tables
    pairs = slots // 2
    bands = projection.shape[0]
    at_dp = lax.axis_index("dp").astype(jnp.int32)
    place = jnp.stack([at_dp // 2, at_dp % 2])

    def by_sample(v):
        return jnp.transpose(v.reshape(batch, cold_feats, bag), (1, 2, 0))

    shape = jax.ShapeDtypeStruct
    ids, pos = call(
        functools.partial(prep_kernel, tables, pairs),
        (shape((tables, 1, 2 * LANES), jnp.int32), shape((cold_feats * bag, batch), jnp.int32)),
    )(by_sample(cold_owner), by_sample(cold_local))
    pos = pos.reshape(lookups)
    asked = exchange(ids, "table").reshape(tables, 2 * LANES)
    row_ids = (asked & (rows_dev // 2 - 1)).reshape(tables * 2 * LANES)
    fetched = call(
        gather_kernel,
        shape((tables, pairs, LANES), BF16),
        scratch=[pltpu.VMEM((rows_dev // 2, LANES), F32)]
        + [pltpu.VMEM((tables * pairs, LANES), F32)] * 2,
        specs=[SMEM, VMEM, VMEM],
        us=12,
        vmem=24,
    )(row_ids, asked, cold_table.T)
    received = exchange(fetched, "table")
    pre, bottom, hot_emb, extra, high, low = call(
        front_kernel,
        (
            shape((batch, hidden), F32),
            shape((batch, hidden), BF16),
            shape((hot_feats, batch, hidden), BF16),
            shape((5, batch, hidden), BF16),
            shape((feats, batch, feats * feats), BF16),
            shape((feats, batch, feats * feats), BF16),
        ),
        us=3,
    )(
        dense_input,
        bottom_weight,
        hot_table,
        hot_unique.reshape(unique, 1),
        hot_unique.reshape(1, unique),
        jnp.transpose(hot_map, (1, 2, 0)),
        grad_inter,
    )
    received, high, low = lax.optimization_barrier((received, high, low))
    cuts = hidden // LANES
    slot_grads, cold_emb, keep, give = call(
        main_kernel,
        (
            shape((tables, pairs, LANES), BF16),
            shape((cold_feats, batch, hidden), BF16),
            shape((13, batch, hidden), BF16),
            shape((13, batch, hidden), BF16),
        ),
        scratch=[
            pltpu.VMEM((2 * tables * pairs, LANES), F32),
            pltpu.VMEM((lookups, LANES), F32),
            pltpu.VMEM((feats, batch, hidden), BF16),
            pltpu.VMEM((feats, batch, feats * feats), BF16),
            pltpu.VMEM((feats, batch, feats * feats), BF16),
            pltpu.VMEM((feats, batch, hidden), BF16),
            pltpu.VMEM((4, batch, hidden), BF16),
            pltpu.VMEM((batch, hidden), F32),
            pltpu.VMEM((batch, hidden), BF16),
            pltpu.VMEM((batch, hidden), BF16),
            pltpu.VMEM((5, batch, hidden), BF16),
            pltpu.SemaphoreType.DMA((14,)),
        ],
        specs=[SMEM] * 2 + [VMEM] * 3 + [HBM] * 7,
        out_specs=[VMEM, HBM, HBM, HBM],
        us=14,
        vmem=63,
    )(
        place,
        pos,
        received,
        by_sample(cold_band).reshape(cold_feats * bag, batch),
        projection,
        pre,
        dense_input,
        extra,
        bottom,
        hot_emb,
        high,
        low,
    )
    returned = exchange(slot_grads, "table")
    took = to_other_core(give)
    dense_row, dense_up, dense_far, dense_down = call(
        dense_part_kernel,
        (shape((tables * 32, LANES), F32),) + (shape((tables * 32, LANES), BF16),) * 3,
        scratch=[pltpu.VMEM((cuts, tables * 32, LANES), F32)],
        specs=[SMEM, VMEM, VMEM],
        us=4,
        vmem=32,
    )(place, keep, took)
    for part, steps in ((dense_up, 1), (dense_far, 2), (dense_down, -1)):
        dense_row += along_x(part, steps).astype(F32)
    dense_row = dense_row.astype(BF16).reshape(tables, 32, LANES)
    returned, dense_row = lax.optimization_barrier((returned, dense_row))
    dense_all = exchange(dense_row, "table")

    half = rows_dev // 32
    given_far, given_near, given_own, kept_far, kept_near, kept_own = call(
        add_kernel,
        (
            shape((2, half, LANES), BF16),
            shape((2, 2, half, LANES), BF16),
            shape((2, half, LANES), BF16),
            shape((2, half, LANES), BF16),
            shape((2, 2, half, LANES), BF16),
            shape((2, half, LANES), F32),
        ),
        scratch=[pltpu.VMEM((tables * pairs, LANES), F32)] * 2
        + [
            pltpu.VMEM((4, 2, half, LANES), BF16),
            pltpu.VMEM((3, 2, half, LANES), BF16),
            pltpu.VMEM((2, half, LANES), F32),
            pltpu.SemaphoreType.DMA((8,)),
        ]
        + [pltpu.VMEM((rows_dev // 2, LANES), F32)] * 2,
        specs=[SMEM, SMEM, VMEM, VMEM],
        out_specs=[HBM] * 6,
        us=20,
        vmem=62,
    )(place, row_ids, asked, returned)
    given_far, dense_all = lax.optimization_barrier((given_far, dense_all))
    mine = call(dense_kernel, shape((32, LANES), BF16))(dense_all)
    taken_far = to_other_core(given_far)
    theirs = to_other_core(mine)
    up, down = call(far_kernel, (shape((half + 64, LANES), BF16),) * 2, specs=[SMEM] + [VMEM] * 4)(
        place, kept_far, taken_far, mine, theirs
    )
    from_below = along_x(up, 1)
    from_above = along_x(down, -1)
    up, down, cold_emb, given_near, given_own = lax.optimization_barrier(
        (up, down, cold_emb, given_near, given_own)
    )
    taken_near = to_other_core(given_near)
    taken_own = to_other_core(given_own)
    inter = call(
        inter_kernel,
        shape((batch, feats * feats), F32),
        scratch=[
            pltpu.VMEM((feats, batch, hidden), BF16),
            pltpu.VMEM((feats, batch, feats * feats), F32),
        ],
        us=4,
    )(bottom, cold_emb, hot_emb)
    from_below, from_above, taken_near, taken_own, inter = lax.optimization_barrier(
        (from_below, from_above, taken_near, taken_own, inter)
    )
    next_up, next_down = call(
        second_kernel,
        (shape((2 * half + 64, LANES), BF16), shape((2 * half, LANES), BF16)),
    )(kept_near, taken_near, from_below, from_above)
    next_up, next_down, kept_own, taken_own = lax.optimization_barrier(
        (next_up, next_down, kept_own, taken_own)
    )
    pair_own = call(own_kernel, shape((2, half, LANES), F32), us=2)(kept_own, taken_own)
    next_below = along_x(next_up, 1)
    next_above = along_x(next_down, -1)
    cold_grad, hot_grad, projection_grad, bottom_grad = call(
        last_kernel,
        (
            shape((width, rows_dev // 8), F32),
            shape((32, hidden), F32),
            shape((8, hidden), F32),
            shape((16, hidden), F32),
        ),
        specs=[SMEM] + [VMEM] * 6,
        us=2,
    )(place, pair_own, next_below, next_above, up, from_above, from_below)
    return inter, cold_grad.T, hot_grad, projection_grad, bottom_grad


def solution(mesh):
    placed = (
        P(("table", "dp"), None),
        P(),
        P("table", None),
        P(),
        P(),
        P(("table", "dp"), None, None, None),
        P(("table", "dp"), None, None),
        P(("table", "dp"), None, None),
        P(("table", "dp")),
        P(("table", "dp"), None, None),
        P(("table", "dp"), None),
    )
    return jax.shard_map(
        shards,
        mesh=mesh,
        in_specs=placed,
        out_specs=(
            P(("table", "dp"), None),
            P(("table", "dp"), None),
            P("table", None),
            P("table", None),
            P("table", None),
        ),
        check_vma=False,
    )
```
